32 devices in a mesh: cfg: 2 (over y), rows: 8 (over z, x), tp: 2 (over core).
Axes of the slice: x: 2, y: 2, z: 4, core: 2. Of those that a mesh axis runs over, the one named last changes fastest.
Arguments:
- latent: bfloat16 [2, 32, 1280, 128], P('cfg', 'rows', 'tp'), may hold values from -60 to 60
- stale_kv: bfloat16 [2, 2, 32, 128, 1024], P('cfg', None, 'rows', None, 'tp'), may hold values from -60 to 60
- timestep: int32 [1], replicated, may hold values from 0 to 999
- w_time: bfloat16 [320, 1280], P(None, 'tp'), may hold values from -0.3125 to 0.3125
- gn_gain: bfloat16 [1280], P('tp'), may hold values from 0.5 to 1.5
- gn_bias: bfloat16 [1280], P('tp'), may hold values from -3 to 3
- conv_w: bfloat16 [3, 3, 1280, 1280], P(None, None, 'tp', 'cfg'), may hold values from -0.0546875 to 0.0546875
- conv_b: bfloat16 [1280], P('tp'), may hold values from -3 to 3
- ln_gain: bfloat16 [1280], P('tp'), may hold values from 0.5 to 1.5
- ln_bias: bfloat16 [1280], P('tp'), may hold values from -3 to 3
- w_qkv: bfloat16 [1280, 3, 1024], P(None, None, 'tp'), may hold values from -0.15625 to 0.15625
- w_out: bfloat16 [1024, 1280], P('tp'), may hold values from -0.25 to 0.25
Outputs:
- guided: bfloat16 [32, 640, 2, 128], P('rows', 'tp', 'cfg')
- fresh_kv: bfloat16 [2, 2, 32, 128, 1024], P('cfg', None, 'rows', None, 'tp')
The draws below stay inside these ranges and needn't reach their ends.
All inputs are finite; a program needn't handle non-finite values.
Results may differ from the reference program's by a relative error of at most 0.029.
Values may be sent and summed in bfloat16 or wider, within the bound.
No kernel may reach another device: no remote copies, remote signals or barrier semaphores. Data moves between devices by JAX's collectives and lax.ppermute only.
A program may use at most 128 MiB of HBM per device.

```python
import math
import jax
import jax.numpy as jnp
from jax import lax

D = 1280
H = 16
HD = 64
GROUPS = 32
TEMB = 320
W = 128
ROW_DEV = 4
NR = 32


def draw_latent(key, part):
    key = jax.random.fold_in(key, 11)
    key_base, key_rows, key_chan = jax.random.split(key, 3)
    shape = (2, NR, D, W)
    rise = 1.0 + 2.0 * jnp.arange(NR, dtype=jnp.float32) / max(NR - 1, 1)
    row_scale = jnp.exp(jax.random.uniform(key_rows, (2, NR, 1, 1), minval=-1.15, maxval=1.15)) * rise[None, :, None, None]
    chan_scale = jnp.exp(jax.random.uniform(key_chan, (1, 1, D, 1), minval=-1.15, maxval=1.15))
    base = jax.random.normal(key_base, shape)
    return jnp.clip(0.5 * base * row_scale * chan_scale, -60.0, 60.0).astype(jnp.bfloat16)


def draw_stale_kv(key, part):
    key = jax.random.fold_in(key, 23)
    key_base = jax.random.fold_in(key, 0)
    shape = (2, 2, NR, W, H * HD)
    pair_scale = jnp.array([1.5, 8.0], jnp.float32).reshape(1, 2, 1, 1, 1)
    base = jax.random.normal(key_base, shape)
    return jnp.clip(base * pair_scale, -60.0, 60.0).astype(jnp.bfloat16)


def raised(entries, stream_key, source, target, blocks, factor):
    def block_of(axis_at):
        return (jnp.arange(entries.shape[axis_at]) // (entries.shape[axis_at] // blocks)).reshape((-1,) + (1,) * (entries.ndim - 1 - axis_at))

    near = jax.random.permutation(stream_key, blocks)[block_of(target)]
    far = (block_of(target) + blocks // 2) % blocks
    return jnp.where((block_of(source) == near) | (block_of(source) == far), factor * entries, entries)


def level_of(stream_key, shape, shards, smallest, largest):
    def one(dim, parts):
        steps = jax.random.uniform(jax.random.fold_in(jax.random.fold_in(stream_key, 6), dim), (parts,), jnp.float32, smallest / len(shards), largest / len(shards))
        return jnp.repeat(jnp.exp(steps), shape[dim] // parts).reshape((-1,) + (1,) * (len(shape) - dim - 1))

    level = one(*shards[0])
    for cut in shards[1:]:
        level = level * one(*cut)
    return level


def scatter_about(rng, extent, spread, reach, pieces=(), kind=jnp.bfloat16):
    gain = level_of(rng, extent, pieces, -0.22, 0.18) if pieces else 1.0
    result = jax.random.normal(rng, extent, jnp.float32) * spread * gain
    return jnp.minimum(jnp.maximum(result, -reach), reach).astype(kind)


def bell_draw_with(key, dims, spread, most, cuts, heavy, held_as=jnp.bfloat16):
    values = spread * jax.random.normal(key, dims, jnp.float32)
    if cuts:
        values = values * level_of(key, dims, cuts, -0.22, 0.18)
    return jnp.clip(raised(values, jax.random.fold_in(key, 3), *heavy), -most, most).astype(held_as)


def setup_inputs(seed: int = 0) -> dict:
    splits = jax.random.split(jax.random.key(seed), 13)
    return {
        "latent": draw_latent(jax.random.fold_in(splits[12], 71), 0),
        "stale_kv": draw_stale_kv(jax.random.fold_in(splits[12], 71), 0),
        "timestep": jax.random.randint(splits[2], (1,), 0, 1000).astype(jnp.int32),
        "w_time": scatter_about(splits[3], (TEMB, D), TEMB ** -0.5, 0.3125, ((1, 2),)),
        "gn_gain": jnp.clip(1.0 + 0.1 * jax.random.normal(splits[4], (D,), jnp.float32), 0.5, 1.5).astype(jnp.bfloat16),
        "gn_bias": scatter_about(splits[5], (D,), 0.5, 3.0, ((0, 2),)),
        "conv_w": scatter_about(splits[6], (3, 3, D, D), (9 * D) ** -0.5, 0.0546875, ((2, 2), (3, 2))),
        "conv_b": scatter_about(splits[7], (D,), 0.5, 3.0, ((0, 2),)),
        "ln_gain": jnp.clip(1.0 + 0.1 * jax.random.normal(splits[8], (D,), jnp.float32), 0.5, 1.5).astype(jnp.bfloat16),
        "ln_bias": scatter_about(splits[9], (D,), 0.5, 3.0, ((0, 2),)),
        "w_qkv": scatter_about(splits[10], (D, 3, H * HD), D ** -0.5, 0.15625, ((2, 2),)),
        "w_out": bell_draw_with(splits[11], (H * HD, D), (H * HD) ** -0.5, 0.25, ((0, 2),), (0, 1, 2, 2.0)),
    }


epsilon = 1e-05
guidance = 5.0

def time_features(timestep):
    half_width = TEMB // 2
    frequencies = jnp.exp(-math.log(10000.0) * jnp.arange(half_width, dtype=jnp.float32) / half_width)
    angles = timestep.astype(jnp.float32)[0] * frequencies
    return jnp.concatenate([jnp.cos(angles), jnp.sin(angles)])

def attend_all(queries, keys_new, values_new, stale_keys, stale_values):
    positions = NR * W
    block_tokens = ROW_DEV * W
    blocks = NR // ROW_DEV
    score_scale = 1.0 / math.sqrt(HD)
    key_block = jnp.arange(positions, dtype=jnp.int32) // block_tokens

    def attend_block(job_index):
        block_index = job_index // H
        head_start = job_index % H * HD
        zero_index = jnp.int32(0)
        row_start = block_index * block_tokens
        query_rows = lax.dynamic_slice(queries, (row_start, head_start), (block_tokens, HD))
        far_keys = lax.dynamic_slice(stale_keys, (zero_index, head_start), (positions, HD))
        far_values = lax.dynamic_slice(stale_values, (zero_index, head_start), (positions, HD))
        near_keys = lax.dynamic_slice(keys_new, (row_start, head_start), (block_tokens, HD))
        near_values = lax.dynamic_slice(values_new, (row_start, head_start), (block_tokens, HD))
        far_scores = jnp.dot(query_rows, far_keys.T, preferred_element_type=jnp.float32) * score_scale
        far_scores = jnp.where((key_block == block_index)[None, :], -jnp.inf, far_scores)
        near_scores = jnp.dot(query_rows, near_keys.T, preferred_element_type=jnp.float32) * score_scale
        peak = jnp.maximum(lax.optimization_barrier(jnp.max(far_scores, axis=1)), lax.optimization_barrier(jnp.max(near_scores, axis=1)))
        far_weights = jnp.exp(far_scores - peak[:, None])
        near_weights = jnp.exp(near_scores - peak[:, None])
        totals = lax.optimization_barrier(jnp.sum(far_weights, axis=1)) + lax.optimization_barrier(jnp.sum(near_weights, axis=1))
        summed = jnp.dot(far_weights.astype(jnp.bfloat16), far_values, preferred_element_type=jnp.float32)
        summed = summed + jnp.dot(near_weights.astype(jnp.bfloat16), near_values, preferred_element_type=jnp.float32)
        return (summed / totals[:, None]).astype(jnp.bfloat16)
    results = lax.map(attend_block, jnp.arange(blocks * H, dtype=jnp.int32))
    return results.reshape(blocks, H, block_tokens, HD).transpose(0, 2, 1, 3).reshape(positions, H * HD)

def branch(latent_one, stale_one, time_bias, gn_gain, gn_bias, conv_w, conv_b, ln_gain, ln_bias, w_qkv, w_out):
    positions = NR * W
    group_width = D // GROUPS
    latent_tokens = latent_one.transpose(0, 2, 1)
    values32 = latent_tokens.astype(jnp.float32).reshape(positions, GROUPS, group_width)
    amount = positions * group_width
    group_mean = lax.optimization_barrier(jnp.sum(values32, axis=(0, 2))) / amount
    variance = lax.optimization_barrier(jnp.sum(values32 * values32, axis=(0, 2))) / amount - group_mean * group_mean
    scaled = ((values32 - group_mean[None, :, None]) * lax.rsqrt(variance + epsilon)[None, :, None]).reshape(positions, D)
    scaled = scaled * gn_gain.astype(jnp.float32) + gn_bias.astype(jnp.float32)
    activated = jax.nn.silu(scaled).astype(jnp.bfloat16).reshape(NR, W, D)
    framed = jnp.pad(activated, ((1, 1), (1, 1), (0, 0)))
    convolved = jnp.zeros((positions, D), jnp.float32)
    for row_tap in range(3):
        for col_tap in range(3):
            window = framed[row_tap:row_tap + NR, col_tap:col_tap + W].reshape(positions, D)
            convolved = convolved + jnp.dot(window, conv_w[row_tap, col_tap].T, preferred_element_type=jnp.float32)
    hidden = convolved + conv_b.astype(jnp.float32) + time_bias
    resid = (latent_tokens.astype(jnp.float32).reshape(positions, D) + hidden).astype(jnp.bfloat16)
    resid32 = resid.astype(jnp.float32)
    token_mean = lax.optimization_barrier(jnp.mean(resid32, axis=1))
    token_var = lax.optimization_barrier(jnp.mean(resid32 * resid32, axis=1)) - token_mean * token_mean
    normed = (resid32 - token_mean[:, None]) * lax.rsqrt(token_var + epsilon)[:, None]
    normed = (normed * ln_gain.astype(jnp.float32) + ln_bias.astype(jnp.float32)).astype(jnp.bfloat16)
    features = H * HD
    projected = jnp.dot(normed, w_qkv.reshape(D, 3 * features), preferred_element_type=jnp.float32).reshape(positions, 3, features)
    queries = projected[:, 0].astype(jnp.bfloat16)
    keys_new = projected[:, 1].astype(jnp.bfloat16)
    values_new = projected[:, 2].astype(jnp.bfloat16)
    stale_keys = stale_one[0].reshape(positions, features)
    stale_values = stale_one[1].reshape(positions, features)
    attended = attend_all(queries, keys_new, values_new, stale_keys, stale_values)
    branch_out = (resid32 + jnp.dot(attended, w_out, preferred_element_type=jnp.float32)).astype(jnp.bfloat16)
    fresh_pair = jnp.stack([keys_new, values_new]).reshape(2, NR, W, features)
    return (branch_out, fresh_pair)

def reference(latent, stale_kv, timestep, w_time, gn_gain, gn_bias, conv_w, conv_b, ln_gain, ln_bias, w_qkv, w_out):
    embedding = time_features(timestep)
    time_bias = jnp.dot(jax.nn.silu(embedding)[None, :], w_time.astype(jnp.float32), precision=lax.Precision.HIGHEST)[0]
    outputs = []
    pairs = []
    for index_branch in range(2):
        branch_out, fresh_pair = branch(latent[index_branch], stale_kv[index_branch], time_bias, gn_gain, gn_bias, conv_w, conv_b, ln_gain, ln_bias, w_qkv, w_out)
        outputs.append(branch_out.astype(jnp.float32))
        pairs.append(fresh_pair)
    guided = (outputs[1] + guidance * (outputs[0] - outputs[1])).astype(jnp.bfloat16).reshape(NR, W, D)
    guided = guided.transpose(0, 2, 1).reshape(NR, D // 2, 2, W)
    return (guided, jnp.stack(pairs))
```

```python
import functools
import math

import jax
import jax.numpy as jnp
from jax import lax
from jax.experimental import pallas as pl
from jax.experimental.pallas import tpu as pltpu
from jax.sharding import PartitionSpec as P

D = 1280
HD = 64
GROUPS = 32
TEMB = 320
LANES = 128

epsilon = 1e-05
guidance = 5.0
EXP2_SCALE = math.log2(math.e) / math.sqrt(HD)
VMEM_LIMIT = 50 * 1024 * 1024


def swapped(array, axis):
    return lax.ppermute(array, axis, [(i, i ^ 1) for i in range(lax.axis_size(axis))])


def ring_pairs(count):
    order = list(range(0, count, 2)) + list(range(count - 1, 0, -2))
    forward = [(order[i], order[(i + 1) % count]) for i in range(count)]
    backward = [(j, i) for i, j in forward]
    return forward, backward


def gather_tp(array, axis):
    if lax.axis_size("tp") != 2:
        return lax.all_gather(array, "tp", axis=axis, tiled=True)
    other = swapped(array, "tp")
    first = lax.axis_index("tp") == 0
    return jnp.concatenate(
        [jnp.where(first, array, other), jnp.where(first, other, array)], axis=axis
    )


def halves_of_inputs(own):
    cfg = lax.axis_index("cfg")
    if lax.axis_size("tp") != 2:
        full = lax.all_gather(own, "tp", axis=1, tiled=True)
        half = full.shape[1] // 2
        mine = lax.dynamic_slice_in_dim(full, cfg * half, half, 1)
        sent = lax.dynamic_slice_in_dim(full, (1 - cfg) * half, half, 1)
        return mine, swapped(sent, "cfg")
    at = lax.axis_index("tp") == cfg
    across = lax.ppermute(own, ("cfg", "tp"), [(1, 3), (2, 0)])
    pairs = [(0, 1), (3, 2)]
    own_side = lax.ppermute(own, ("cfg", "tp"), pairs)
    across_side = lax.ppermute(across, ("cfg", "tp"), pairs)
    return jnp.where(at, own, own_side), jnp.where(at, across, across_side)


def conv_kernel(flags_ref, x_ref, coef_ref, w_ref, out_ref, act_ref, acc_ref):
    rows = out_ref.shape[0]
    step = pl.program_id(0)

    @pl.when(step == 0)
    def _():
        mean = coef_ref[:, 0:1]
        scale = coef_ref[:, 1:2]
        shift = coef_ref[:, 2:3]
        for r in range(rows + 2):
            x = x_ref[r].astype(jnp.float32)
            z = (x - mean) * scale + shift
            z = z * jax.nn.sigmoid(z)
            if r == 0:
                z = jnp.where(flags_ref[0] == 1, z, 0.0)
            if r == rows + 1:
                z = jnp.where(flags_ref[1] == 1, z, 0.0)
            act_ref[:, r * LANES : (r + 1) * LANES] = z.astype(jnp.bfloat16)

    def product(row_tap):
        return jnp.dot(
            w_ref[row_tap, 0],
            act_ref[:, row_tap * LANES : (row_tap + rows) * LANES],
            preferred_element_type=jnp.float32,
        )

    y = product(0) + product(1) + product(2)
    lane = lax.broadcasted_iota(jnp.int32, (y.shape[0], LANES), 1)

    @pl.when(step == 0)
    def _():
        for r in range(rows):
            part = pltpu.roll(y[:, r * LANES : (r + 1) * LANES], 1, axis=1)
            acc_ref[r] = jnp.where(lane == 0, 0.0, part)

    @pl.when(step == 1)
    def _():
        for r in range(rows):
            acc_ref[r] += y[:, r * LANES : (r + 1) * LANES]

    @pl.when(step == 2)
    def _():
        for r in range(rows):
            part = pltpu.roll(y[:, r * LANES : (r + 1) * LANES], LANES - 1, axis=1)
            total = acc_ref[r] + jnp.where(lane == LANES - 1, 0.0, part)
            out_ref[r] = total.astype(out_ref.dtype)


def conv_call(flags, x, coef, conv_w, out_dtype):
    rows = x.shape[0] - 2
    outs, ins = conv_w.shape[2:]
    return pl.pallas_call(
        conv_kernel,
        grid=(3,),
        in_specs=[
            pl.BlockSpec(memory_space=pltpu.SMEM),
            pl.BlockSpec(x.shape, lambda i: (0, 0, 0)),
            pl.BlockSpec(coef.shape, lambda i: (0, 0)),
            pl.BlockSpec((3, 1, outs, ins), lambda i: (0, i, 0, 0)),
        ],
        out_specs=pl.BlockSpec((rows, outs, LANES), lambda i: (0, 0, 0)),
        out_shape=jax.ShapeDtypeStruct((rows, outs, LANES), out_dtype),
        scratch_shapes=[
            pltpu.VMEM((ins, (rows + 2) * LANES), jnp.bfloat16),
            pltpu.VMEM((rows, outs, LANES), jnp.float32),
        ],
        compiler_params=pltpu.CompilerParams(vmem_limit_bytes=VMEM_LIMIT),
        cost_estimate=pl.CostEstimate(
            flops=2 * 9 * outs * ins * rows * LANES,
            bytes_accessed=2 * 9 * outs * ins,
            transcendentals=ins * rows * LANES,
        ),
        name="norm_conv",
    )(flags, x, coef, conv_w)


def attention_kernel(blocks, carried, final, *refs):
    q_ref = refs[0]
    kv_refs = refs[1 : 1 + 2 * blocks]
    at = 1 + 2 * blocks
    if carried:
        m_in, acc_in = refs[at : at + 2]
        at += 2
    outs = refs[at:]
    positions = q_ref.shape[0]
    tile = min(256, positions)
    for start in range(0, positions, tile):
        rows = pl.ds(start, tile)
        q = q_ref[rows, :]
        low_q = lax.broadcasted_iota(jnp.int32, q.shape, 1) < HD
        results = []
        for head in range(2):
            sel_q = low_q if head == 0 else jnp.logical_not(low_q)
            qh = jnp.where(sel_q, q, jnp.zeros_like(q))
            peak = m_in[0, head, rows, :] if carried else None
            acc = acc_in[0, head, rows, :] if carried else None
            for block in range(blocks):
                keys = kv_refs[2 * block]
                values = kv_refs[2 * block + 1]
                k = keys[...]
                v = values[...]
                low_v = lax.broadcasted_iota(jnp.int32, v.shape, 1) < HD
                sel_v = low_v if head == 0 else jnp.logical_not(low_v)
                v = jnp.where(sel_v, v, jnp.ones_like(v))
                s = lax.dot_general(
                    qh, k, (((1,), (1,)), ((), ())), preferred_element_type=jnp.float32
                )
                top = jnp.broadcast_to(jnp.max(s, axis=1, keepdims=True), (tile, LANES))
                new_peak = top if peak is None else jnp.maximum(peak, top)
                wide = jnp.concatenate([new_peak] * (s.shape[1] // LANES), axis=1)
                p = jnp.exp2((s - wide) * EXP2_SCALE).astype(jnp.bfloat16)
                term = jnp.dot(p, v, preferred_element_type=jnp.float32)
                if acc is None:
                    acc = term
                else:
                    acc = acc * jnp.exp2((peak - new_peak) * EXP2_SCALE) + term
                peak = new_peak
            if final:
                results.append(acc / pltpu.roll(acc, HD, axis=1))
            else:
                outs[0][0, head, rows, :] = peak
                outs[1][0, head, rows, :] = acc
        if final:
            outs[0][rows, :] = jnp.where(low_q, results[0], results[1]).astype(jnp.bfloat16)


def attention_call(q, pairs, state, final):
    positions, features = q.shape
    tiles = features // LANES
    column = pl.BlockSpec((positions, LANES), lambda i: (0, i))
    carry = pl.BlockSpec((1, 2, positions, LANES), lambda i: (i, 0, 0, 0))
    carry_shape = jax.ShapeDtypeStruct((tiles, 2, positions, LANES), jnp.float32)
    operands = [q]
    specs = [column]
    for k, v in pairs:
        operands += [k, v]
        specs += [column, column]
    if state is not None:
        operands += list(state)
        specs += [carry, carry]
    if final:
        out_shape = jax.ShapeDtypeStruct((positions, features), jnp.bfloat16)
        out_specs = column
    else:
        out_shape = (carry_shape, carry_shape)
        out_specs = (carry, carry)
    keys = positions * len(pairs)
    return pl.pallas_call(
        functools.partial(attention_kernel, len(pairs), state is not None, final),
        grid=(tiles,),
        in_specs=specs,
        out_specs=out_specs,
        out_shape=out_shape,
        compiler_params=pltpu.CompilerParams(vmem_limit_bytes=VMEM_LIMIT),
        cost_estimate=pl.CostEstimate(
            flops=16 * positions * keys * features,
            bytes_accessed=4 * keys * features,
            transcendentals=positions * keys * features // HD,
        ),
        name="attend",
    )(*operands)


def per_device(
    latent,
    stale_kv,
    timestep,
    w_time,
    gn_gain,
    gn_bias,
    conv_w,
    conv_b,
    ln_gain,
    ln_bias,
    w_qkv,
    w_out,
):
    latent_rows = latent[0]
    rows_count = lax.axis_size("rows")
    tp_count = lax.axis_size("tp")
    span_rows, local_channels, grid_width = latent_rows.shape
    positions = span_rows * grid_width
    group_width = D // GROUPS
    local_groups = local_channels // group_width
    my_block = lax.axis_index("rows")
    cfg = lax.axis_index("cfg")
    tp = lax.axis_index("tp")

    up_pairs = [(i, i + 1) for i in range(rows_count - 1)]
    down_pairs = [(i + 1, i) for i in range(rows_count - 1)]
    before = lax.ppermute(latent_rows[span_rows - 1 :], "rows", up_pairs)
    after = lax.ppermute(latent_rows[:1], "rows", down_pairs)
    rimmed = jnp.concatenate([before, latent_rows, after], axis=0)
    x_mine, x_other = halves_of_inputs(rimmed)

    forward, backward = ring_pairs(rows_count)
    stale_k = stale_kv[0, 0].reshape(positions, -1)
    stale_v = stale_kv[0, 1].reshape(positions, -1)
    kf = vf = None
    kb = vb = None
    kf, vf, kb, vb = stale_k, stale_v, stale_k, stale_v
    arrived = []
    for hop in range(1, rows_count // 2 + 1):
        last = hop == rows_count // 2
        kf = lax.ppermute(kf, "rows", forward)
        vb = lax.ppermute(vb, "rows", backward)
        if last:
            arrived.append([(kf, vb)])
        else:
            vf = lax.ppermute(vf, "rows", forward)
            kb = lax.ppermute(kb, "rows", backward)
            arrived.append([(kf, vf), (kb, vb)])

    latent32 = latent_rows.astype(jnp.float32)
    values32 = latent32.reshape(span_rows, local_groups, group_width, grid_width)
    sums = jnp.stack(
        [jnp.sum(values32, axis=(0, 2, 3)), jnp.sum(values32 * values32, axis=(0, 2, 3))]
    )
    table = jnp.zeros((2, 2, GROUPS), jnp.float32)
    table = lax.dynamic_update_slice(table, sums[None], (cfg, 0, tp * local_groups))
    table = lax.psum(table, ("cfg", "rows", "tp"))
    vectors = gather_tp(jnp.stack([gn_gain, gn_bias, ln_gain, ln_bias]), 1).astype(jnp.float32)

    amount = span_rows * rows_count * grid_width * group_width
    table = lax.dynamic_slice_in_dim(table, cfg * (GROUPS // 2), GROUPS // 2, 2)
    group_mean = table[:, 0] / amount
    variance = table[:, 1] / amount - group_mean * group_mean
    inverse = lax.rsqrt(variance + epsilon)
    half = D // 2
    gain_half = lax.dynamic_slice_in_dim(vectors[0], cfg * half, half)
    bias_half = lax.dynamic_slice_in_dim(vectors[1], cfg * half, half)
    mean_c = jnp.repeat(group_mean, group_width, axis=1)
    scale_c = jnp.repeat(inverse, group_width, axis=1) * gain_half[None]
    coef = jnp.stack(
        [mean_c, scale_c, jnp.broadcast_to(bias_half[None], mean_c.shape)], axis=2
    )
    coef_mine = lax.dynamic_index_in_dim(coef, cfg, 0, keepdims=False)
    coef_other = lax.dynamic_index_in_dim(coef, 1 - cfg, 0, keepdims=False)
    flags = jnp.stack([my_block > 0, my_block < rows_count - 1]).astype(jnp.int32)

    conv_sent = conv_call(flags, x_other, coef_other, conv_w, jnp.bfloat16)
    conv_received = swapped(conv_sent, "cfg")
    conv_own = conv_call(flags, x_mine, coef_mine, conv_w, jnp.float32)

    half_width = TEMB // 2
    frequencies = jnp.exp(
        -math.log(10000.0) * jnp.arange(half_width, dtype=jnp.float32) / half_width
    )
    angles = timestep.astype(jnp.float32)[0] * frequencies
    embedding = jnp.concatenate([jnp.cos(angles), jnp.sin(angles)])
    time_bias = jnp.dot(
        jax.nn.silu(embedding)[None, :], w_time.astype(jnp.float32), precision=lax.Precision.HIGHEST
    )[0]
    bias = conv_b.astype(jnp.float32) + time_bias
    resid = (
        latent32 + (conv_own + conv_received.astype(jnp.float32) + bias[None, :, None])
    ).astype(jnp.bfloat16)

    full = gather_tp(resid, 1).astype(jnp.float32)
    token_mean = jnp.mean(full, axis=1)
    token_var = jnp.mean(full * full, axis=1) - token_mean * token_mean
    normed = (full - token_mean[:, None, :]) * lax.rsqrt(token_var + epsilon)[:, None, :]
    normed = (normed * vectors[2][None, :, None] + vectors[3][None, :, None]).astype(jnp.bfloat16)
    local_features = w_qkv.shape[2]
    projected = (
        jnp.einsum(
            "rdw,df->rwf",
            normed,
            w_qkv.reshape(D, 3 * local_features),
            preferred_element_type=jnp.float32,
        )
        .reshape(positions, 3 * local_features)
        .astype(jnp.bfloat16)
    )
    queries = projected[:, :local_features]
    keys_new = projected[:, local_features : 2 * local_features]
    values_new = projected[:, 2 * local_features :]
    fresh_kv = jnp.stack([keys_new, values_new]).reshape(
        1, 2, span_rows, grid_width, local_features
    )

    state = attention_call(queries, [(keys_new, values_new)] + arrived[0], None, False)
    for group in arrived[1:-1]:
        state = attention_call(queries, group, state, False)
    attended = attention_call(queries, arrived[-1], state, True)

    attended_full = gather_tp(attended, 1)
    if tp_count == 2:
        w_split = w_out.reshape(-1, tp_count, local_channels)
        first = tp == 0
        w_mine = lax.dynamic_index_in_dim(w_split, tp, 1, keepdims=False)
        w_side = swapped(lax.dynamic_index_in_dim(w_split, 1 - tp, 1, keepdims=False), "tp")
        w_cols = jnp.concatenate(
            [jnp.where(first, w_mine, w_side), jnp.where(first, w_side, w_mine)], axis=0
        )
    else:
        w_cols = lax.all_to_all(w_out, "tp", 1, 0, tiled=True)
    w_pairs = w_cols.reshape(w_cols.shape[0], local_channels // 2, 2)
    att_rows = attended_full.reshape(span_rows, grid_width, -1)
    resid_pairs = resid.reshape(span_rows, local_channels // 2, 2, grid_width)

    def branch_out(parity):
        terms = jnp.einsum(
            "rwf,fd->rdw",
            att_rows,
            lax.dynamic_index_in_dim(w_pairs, parity, 2, keepdims=False),
            preferred_element_type=jnp.float32,
        )
        base = lax.dynamic_index_in_dim(resid_pairs, parity, 2, keepdims=False)
        return (base.astype(jnp.float32) + terms).astype(jnp.bfloat16)

    other_branch = swapped(branch_out(1 - cfg), "cfg")
    kept = branch_out(cfg)
    is_cond = cfg == 0
    cond_out = jnp.where(is_cond, kept, other_branch).astype(jnp.float32)
    uncond_out = jnp.where(is_cond, other_branch, kept).astype(jnp.float32)
    guided = (uncond_out + guidance * (cond_out - uncond_out)).astype(jnp.bfloat16)
    return (guided[:, :, None, :], fresh_kv)


def solution(mesh):
    in_specs = (
        P("cfg", "rows", "tp", None),
        P("cfg", None, "rows", None, "tp"),
        P(),
        P(None, "tp"),
        P("tp"),
        P("tp"),
        P(None, None, "tp", "cfg"),
        P("tp"),
        P("tp"),
        P("tp"),
        P(None, None, "tp"),
        P("tp", None),
    )
    out_specs = (P("rows", "tp", "cfg", None), P("cfg", None, "rows", None, "tp"))
    return jax.shard_map(
        per_device, mesh=mesh, in_specs=in_specs, out_specs=out_specs, check_vma=False
    )
```

```python
import functools
import math

import jax
import jax.numpy as jnp
from jax import lax
from jax.experimental import pallas as pl
from jax.experimental.pallas import tpu as pltpu
from jax.sharding import PartitionSpec as P

D = 1280
HD = 64
GROUPS = 32
TEMB = 320
LANES = 128

epsilon = 1e-05
guidance = 5.0
SCORE_SCALE = 1.0 / math.sqrt(HD)
VMEM_LIMIT = 50 * 1024 * 1024


def swapped(array, axis):
    return lax.ppermute(array, axis, [(i, i ^ 1) for i in range(lax.axis_size(axis))])


def ring_pairs(count):
    order = list(range(0, count, 2)) + list(range(count - 1, 0, -2))
    forward = [(order[i], order[(i + 1) % count]) for i in range(count)]
    backward = [(j, i) for i, j in forward]
    return forward, backward


def gather_tp(array, axis):
    if lax.axis_size("tp") != 2:
        return lax.all_gather(array, "tp", axis=axis, tiled=True)
    other = swapped(array, "tp")
    first = lax.axis_index("tp") == 0
    return jnp.concatenate(
        [jnp.where(first, array, other), jnp.where(first, other, array)], axis=axis
    )


def summed(array, axes):
    for axis in axes:
        count = lax.axis_size(axis)
        if count & (count - 1):
            array = lax.psum(array, axis)
            continue
        distance = 1
        while distance < count:
            pairs = [(i, i ^ distance) for i in range(count)]
            array = array + lax.ppermute(array, axis, pairs)
            distance *= 2
    return array


def halves_of_inputs(own):
    cfg = lax.axis_index("cfg")
    if lax.axis_size("tp") != 2:
        full = lax.all_gather(own, "tp", axis=1, tiled=True)
        half = full.shape[1] // 2
        mine = lax.dynamic_slice_in_dim(full, cfg * half, half, 1)
        sent = lax.dynamic_slice_in_dim(full, (1 - cfg) * half, half, 1)
        return [mine], [swapped(sent, "cfg")]
    across = lax.ppermute(own, ("cfg", "tp"), [(1, 3), (2, 0)])
    pairs = [(0, 1), (3, 2)]
    own_side = lax.ppermute(own, ("cfg", "tp"), pairs)
    across_side = lax.ppermute(across, ("cfg", "tp"), pairs)
    return [own, own_side], [across, across_side]


def conv_kernel(choices, flags_ref, *refs):
    x_refs = refs[:choices]
    coef_ref, w_ref, out_ref, act_ref, acc_ref = refs[choices:]
    rows = out_ref.shape[0]
    step = pl.program_id(0)

    @pl.when(step == 0)
    def _():
        mean = coef_ref[:, 0:1]
        scale = coef_ref[:, 1:2]
        shift = coef_ref[:, 2:3]
        for r in range(rows + 2):
            x = x_refs[0][r]
            if choices == 2:
                x = jnp.where(flags_ref[2] == 1, x, x_refs[1][r])
            x = x.astype(jnp.float32)
            z = (x - mean) * scale + shift
            z = z * jax.nn.sigmoid(z)
            if r == 0:
                z = jnp.where(flags_ref[0] == 1, z, 0.0)
            if r == rows + 1:
                z = jnp.where(flags_ref[1] == 1, z, 0.0)
            act_ref[:, r * LANES : (r + 1) * LANES] = z.astype(jnp.bfloat16)

    def product(row_tap):
        return jnp.dot(
            w_ref[row_tap, 0],
            act_ref[:, row_tap * LANES : (row_tap + rows) * LANES],
            preferred_element_type=jnp.float32,
        )

    y = product(0) + product(1) + product(2)
    lane = lax.broadcasted_iota(jnp.int32, (y.shape[0], LANES), 1)

    @pl.when(step == 0)
    def _():
        for r in range(rows):
            part = pltpu.roll(y[:, r * LANES : (r + 1) * LANES], 1, axis=1)
            acc_ref[r] = jnp.where(lane == 0, 0.0, part)

    @pl.when(step == 1)
    def _():
        for r in range(rows):
            acc_ref[r] += y[:, r * LANES : (r + 1) * LANES]

    @pl.when(step == 2)
    def _():
        for r in range(rows):
            part = pltpu.roll(y[:, r * LANES : (r + 1) * LANES], LANES - 1, axis=1)
            total = acc_ref[r] + jnp.where(lane == LANES - 1, 0.0, part)
            out_ref[r] = total.astype(out_ref.dtype)


def conv_call(flags, xs, coef, conv_w, out_dtype):
    x = xs[0]
    rows = x.shape[0] - 2
    outs, ins = conv_w.shape[2:]
    return pl.pallas_call(
        functools.partial(conv_kernel, len(xs)),
        grid=(3,),
        in_specs=[
            pl.BlockSpec(memory_space=pltpu.SMEM),
            *[pl.BlockSpec(x.shape, lambda i: (0, 0, 0))] * len(xs),
            pl.BlockSpec(coef.shape, lambda i: (0, 0)),
            pl.BlockSpec((3, 1, outs, ins), lambda i: (0, i, 0, 0)),
        ],
        out_specs=pl.BlockSpec((rows, outs, LANES), lambda i: (0, 0, 0)),
        out_shape=jax.ShapeDtypeStruct((rows, outs, LANES), out_dtype),
        scratch_shapes=[
            pltpu.VMEM((ins, (rows + 2) * LANES), jnp.bfloat16),
            pltpu.VMEM((rows, outs, LANES), jnp.float32),
        ],
        compiler_params=pltpu.CompilerParams(vmem_limit_bytes=VMEM_LIMIT),
        cost_estimate=pl.CostEstimate(
            flops=2 * 9 * outs * ins * rows * LANES,
            bytes_accessed=2 * 9 * outs * ins,
            transcendentals=ins * rows * LANES,
        ),
        name="norm_conv",
    )(flags, *xs, coef, conv_w)


def project_kernel(parts, order_ref, *refs):
    part_refs = refs[:parts]
    own_ref, gain_ref, bias_ref, w_ref, q_ref, kv_ref, split_ref, normed_ref = refs[parts:]
    rows, channels, _ = part_refs[0].shape
    total = parts * channels
    step = pl.program_id(0)

    @pl.when(step == 0)
    def _():
        for r in range(rows):
            x = [ref[r].astype(jnp.float32) for ref in part_refs]
            mean = sum(jnp.sum(a, axis=0, keepdims=True) for a in x) / total
            var = sum(jnp.sum(a * a, axis=0, keepdims=True) for a in x) / total - mean * mean
            inverse = lax.rsqrt(var + epsilon)
            for j in range(parts):
                at = pl.ds(pl.multiple_of(order_ref[j] * channels, LANES), channels)
                z = (x[j] - mean) * inverse * gain_ref[at, :] + bias_ref[at, :]
                normed_ref[r * LANES : (r + 1) * LANES, at] = z.astype(jnp.bfloat16).T
        own_channels = own_ref.shape[1]
        half = own_channels // 2
        shape = (own_channels, own_channels)
        to = lax.broadcasted_iota(jnp.int32, shape, 0)
        source = lax.broadcasted_iota(jnp.int32, shape, 1)
        wanted = jnp.where(to < half, 2 * to, 2 * (to - half) + 1)
        chosen = (source == wanted).astype(jnp.bfloat16)
        for r in range(rows):
            y = jnp.dot(chosen, own_ref[r], preferred_element_type=jnp.float32)
            y = y.astype(jnp.bfloat16)
            split_ref[0, r] = y[:half]
            split_ref[1, r] = y[half:]

    y = jnp.dot(normed_ref[...], w_ref[0], preferred_element_type=jnp.float32)
    y = y.astype(jnp.bfloat16)

    @pl.when(step == 0)
    def _():
        q_ref[...] = y * SCORE_SCALE

    @pl.when(step > 0)
    def _():
        kv_ref[0] = y


def project_call(order, parts, own, gain, bias, w):
    rows, channels, _ = parts[0].shape
    positions = rows * LANES
    _, depth, features = w.shape
    half = own.shape[1] // 2
    whole = lambda shape: pl.BlockSpec(shape, lambda i: (0,) * len(shape))
    return pl.pallas_call(
        functools.partial(project_kernel, len(parts)),
        grid=(3,),
        in_specs=[
            pl.BlockSpec(memory_space=pltpu.SMEM),
            *[whole(part.shape) for part in parts],
            whole(own.shape),
            whole(gain.shape),
            whole(bias.shape),
            pl.BlockSpec((1, depth, features), lambda i: (i, 0, 0)),
        ],
        out_specs=(
            whole((positions, features)),
            pl.BlockSpec((1, positions, features), lambda i: (jnp.maximum(i - 1, 0), 0, 0)),
            whole((2, rows, half, LANES)),
        ),
        out_shape=(
            jax.ShapeDtypeStruct((positions, features), jnp.bfloat16),
            jax.ShapeDtypeStruct((2, positions, features), jnp.bfloat16),
            jax.ShapeDtypeStruct((2, rows, half, LANES), jnp.bfloat16),
        ),
        scratch_shapes=[pltpu.VMEM((positions, depth), jnp.bfloat16)],
        compiler_params=pltpu.CompilerParams(vmem_limit_bytes=VMEM_LIMIT),
        cost_estimate=pl.CostEstimate(
            flops=6 * positions * depth * features,
            bytes_accessed=6 * depth * features,
            transcendentals=0,
        ),
        name="norm_project",
    )(order, *parts, own, gain, bias, w)


def attention_kernel(blocks, carried, final, *refs):
    q_ref = refs[0]
    kv_refs = refs[1 : 1 + 2 * blocks]
    at = 1 + 2 * blocks
    if carried:
        m_in, acc_in = refs[at : at + 2]
        at += 2
    if final:
        w_ref = refs[at]
        at += 1
        out_refs = refs[at:-1]
        joined_ref = refs[-1]
    else:
        m_out, acc_out = refs[at:]
    positions = q_ref.shape[0]
    tile = min(256, positions)
    starts = range(0, positions, tile)
    lanes = lambda array, low: (lax.broadcasted_iota(jnp.int32, array.shape, 1) < HD) == low

    def scores(item):
        start, head, block = item
        q = q_ref[start : start + tile, :]
        q = jnp.where(lanes(q, head == 0), q, jnp.zeros_like(q))
        return lax.dot_general(
            q,
            kv_refs[2 * block][0],
            (((1,), (1,)), ((), ())),
            preferred_element_type=jnp.float32,
        )

    items = [(start, head, block) for start in starts for block in range(blocks) for head in (0, 1)]
    state = {}
    upcoming = scores(items[0])
    for number, item in enumerate(items):
        s = upcoming
        if number + 1 < len(items):
            upcoming = scores(items[number + 1])
        start, head, block = item
        rows = slice(start, start + tile)
        if block == 0 and carried:
            peak, acc = m_in[0, head, rows, :], acc_in[0, head, rows, :]
        elif block == 0:
            peak = acc = None
        else:
            peak, acc = state[start, head]
        v = kv_refs[2 * block + 1][0]
        v = jnp.where(lanes(v, head == 0), v, jnp.ones_like(v))
        top = jnp.broadcast_to(jnp.max(s, axis=1, keepdims=True), (tile, LANES))
        new_peak = top if peak is None else jnp.maximum(peak, top)
        wide = jnp.concatenate([new_peak] * (s.shape[1] // LANES), axis=1)
        p = jnp.exp(s - wide).astype(jnp.bfloat16)
        term = jnp.dot(p, v, preferred_element_type=jnp.float32)
        acc = term if acc is None else acc * jnp.exp(peak - new_peak) + term
        state[start, head] = new_peak, acc
        if block < blocks - 1:
            continue
        if not final:
            m_out[0, head, rows, :] = new_peak
            acc_out[0, head, rows, :] = acc
        elif head == 1:
            parts = [state[start, h][1] for h in (0, 1)]
            parts = [a / pltpu.roll(a, HD, axis=1) for a in parts]
            pair = jnp.where(lanes(acc, True), parts[0], parts[1]).astype(jnp.bfloat16)
            joined_ref[pl.program_id(0), rows, :] = pair

    if final:
        tiles, _, _ = joined_ref.shape

        @pl.when(pl.program_id(0) == tiles - 1)
        def _():
            joined = jnp.concatenate([joined_ref[i] for i in range(tiles)], axis=1)
            for j in range(w_ref.shape[0]):
                y = lax.dot_general(
                    w_ref[j],
                    joined,
                    (((1,), (1,)), ((), ())),
                    preferred_element_type=jnp.float32,
                )
                out = out_refs[j] if len(out_refs) > 1 else out_refs[0].at[j]
                half = w_ref.shape[1] // 2
                for parity in range(2):
                    for r in range(positions // LANES):
                        out[parity, r] = y[
                            parity * half : (parity + 1) * half, r * LANES : (r + 1) * LANES
                        ].astype(out.dtype)


def attention_call(q, pairs, state, w=None, own_apart=False):
    positions, features = q.shape
    tiles = features // LANES
    final = w is not None
    carry = pl.BlockSpec((1, 2, positions, LANES), lambda i: (i, 0, 0, 0))
    carry_shape = jax.ShapeDtypeStruct((tiles, 2, positions, LANES), jnp.float32)
    operands = [q]
    specs = [pl.BlockSpec((positions, LANES), lambda i: (0, i))]
    for pair in pairs:
        for array, place in pair:
            operands.append(array)
            specs.append(
                pl.BlockSpec((1, positions, LANES), functools.partial(lambda p, i: (p, 0, i), place))
            )
    if state is not None:
        operands += list(state)
        specs += [carry, carry]
    scratch = []
    if final:
        operands.append(w)
        specs.append(pl.BlockSpec(w.shape, lambda i: (0, 0, 0)))
        shape = (2, positions // LANES, w.shape[1] // 2, LANES)
        if own_apart:
            out_shape = (
                jax.ShapeDtypeStruct(shape, jnp.bfloat16),
                jax.ShapeDtypeStruct(shape, jnp.float32),
            )
        else:
            out_shape = (jax.ShapeDtypeStruct((w.shape[0],) + shape, jnp.bfloat16),)
        out_specs = tuple(
            pl.BlockSpec(o.shape, functools.partial(lambda n, i: (0,) * n, len(o.shape)))
            for o in out_shape
        )
        scratch = [pltpu.VMEM((tiles, positions, LANES), jnp.bfloat16)]
    else:
        out_shape = (carry_shape, carry_shape)
        out_specs = (carry, carry)
    keys = positions * len(pairs)
    return pl.pallas_call(
        functools.partial(attention_kernel, len(pairs), state is not None, final),
        grid=(tiles,),
        in_specs=specs,
        out_specs=out_specs,
        out_shape=out_shape,
        scratch_shapes=scratch,
        compiler_params=pltpu.CompilerParams(vmem_limit_bytes=VMEM_LIMIT),
        cost_estimate=pl.CostEstimate(
            flops=16 * positions * keys * features,
            bytes_accessed=4 * keys * features,
            transcendentals=positions * keys * features // HD,
        ),
        name="attend",
    )(*operands)


def per_device(
    latent,
    stale_kv,
    timestep,
    w_time,
    gn_gain,
    gn_bias,
    conv_w,
    conv_b,
    ln_gain,
    ln_bias,
    w_qkv,
    w_out,
):
    latent_rows = latent[0]
    rows_count = lax.axis_size("rows")
    tp_count = lax.axis_size("tp")
    span_rows, local_channels, grid_width = latent_rows.shape
    positions = span_rows * grid_width
    group_width = D // GROUPS
    local_groups = local_channels // group_width
    my_block = lax.axis_index("rows")
    cfg = lax.axis_index("cfg")
    tp = lax.axis_index("tp")

    up_pairs = [(i, i + 1) for i in range(rows_count - 1)]
    down_pairs = [(i + 1, i) for i in range(rows_count - 1)]
    before = lax.ppermute(latent_rows[span_rows - 1 :], "rows", up_pairs)
    after = lax.ppermute(latent_rows[:1], "rows", down_pairs)
    rimmed = jnp.concatenate([before, latent_rows, after], axis=0)
    x_mine, x_other = halves_of_inputs(rimmed)

    forward, backward = ring_pairs(rows_count)
    pair = stale_kv[0].reshape(2, positions, -1)
    ahead = behind = pair
    hops = []
    for hop in range(1, rows_count // 2):
        ahead = lax.ppermute(ahead, "rows", forward)
        behind = lax.ppermute(behind, "rows", backward)
        hops.append([((ahead, 0), (ahead, 1)), ((behind, 0), (behind, 1))])
    far_k = lax.ppermute(ahead[:1], "rows", forward)
    far_v = lax.ppermute(behind[1:], "rows", backward)
    hops.append([((far_k, 0), (far_v, 0))])

    latent32 = latent_rows.astype(jnp.float32)
    values32 = latent32.reshape(span_rows, local_groups, group_width, grid_width)
    sums = jnp.stack(
        [jnp.sum(values32, axis=(0, 2, 3)), jnp.sum(values32 * values32, axis=(0, 2, 3))]
    )
    table = jnp.zeros((2, 2, GROUPS), jnp.float32)
    table = lax.dynamic_update_slice(table, sums[None], (cfg, 0, tp * local_groups))
    table = summed(table.reshape(1, -1), ("tp", "cfg", "rows")).reshape(2, 2, GROUPS)
    vectors = gather_tp(jnp.stack([gn_gain, gn_bias, ln_gain, ln_bias]), 1).astype(jnp.float32)

    amount = span_rows * rows_count * grid_width * group_width
    table = lax.dynamic_slice_in_dim(table, cfg * (GROUPS // 2), GROUPS // 2, 2)
    group_mean = table[:, 0] / amount
    variance = table[:, 1] / amount - group_mean * group_mean
    inverse = lax.rsqrt(variance + epsilon)
    half = D // 2
    gain_half = lax.dynamic_slice_in_dim(vectors[0], cfg * half, half)
    bias_half = lax.dynamic_slice_in_dim(vectors[1], cfg * half, half)
    mean_c = jnp.repeat(group_mean, group_width, axis=1)
    scale_c = jnp.repeat(inverse, group_width, axis=1) * gain_half[None]
    coef = jnp.stack(
        [mean_c, scale_c, jnp.broadcast_to(bias_half[None], mean_c.shape)], axis=2
    )
    coef_mine = lax.dynamic_index_in_dim(coef, cfg, 0, keepdims=False)
    coef_other = lax.dynamic_index_in_dim(coef, 1 - cfg, 0, keepdims=False)
    flags = jnp.stack([my_block > 0, my_block < rows_count - 1, tp == cfg]).astype(jnp.int32)

    local_features = w_qkv.shape[2]
    w_project = w_qkv.transpose(1, 0, 2)
    w_back = w_out.T.reshape(tp_count, local_channels // 2, 2, local_features)
    w_back = w_back.transpose(0, 2, 1, 3).reshape(tp_count, local_channels, local_features)
    if tp_count == 2:
        w_back = jnp.where(tp == 0, w_back[::-1], w_back)
    conv_w, coef_other, w_project, w_back = lax.optimization_barrier(
        (conv_w, coef_other, w_project, w_back)
    )

    conv_sent = conv_call(flags, x_other, coef_other, conv_w, jnp.bfloat16)
    conv_received = swapped(conv_sent, "cfg")
    conv_own = conv_call(flags, x_mine, coef_mine, conv_w, jnp.float32)

    half_width = TEMB // 2
    frequencies = jnp.exp(
        -math.log(10000.0) * jnp.arange(half_width, dtype=jnp.float32) / half_width
    )
    angles = timestep.astype(jnp.float32)[0] * frequencies
    embedding = jnp.concatenate([jnp.cos(angles), jnp.sin(angles)])
    time_bias = jnp.dot(
        jax.nn.silu(embedding)[None, :], w_time.astype(jnp.float32), precision=lax.Precision.HIGHEST
    )[0]
    bias = conv_b.astype(jnp.float32) + time_bias
    resid = (
        latent32 + (conv_own + conv_received.astype(jnp.float32) + bias[None, :, None])
    ).astype(jnp.bfloat16)

    if tp_count == 2:
        parts = [resid, swapped(resid, "tp")]
        order = jnp.stack([tp, 1 - tp]).astype(jnp.int32)
    else:
        parts = [lax.all_gather(resid, "tp", axis=1, tiled=True)]
        order = jnp.zeros((1,), jnp.int32)
    queries, fresh, resid_split = project_call(
        order, parts, resid, vectors[2][:, None], vectors[3][:, None], w_project
    )
    fresh_kv = fresh.reshape(1, 2, span_rows, grid_width, local_features)

    state = attention_call(queries, [((fresh, 0), (fresh, 1))] + hops[0] + hops[1], None)
    for group in hops[2:-1]:
        state = attention_call(queries, group, state)
    if tp_count == 2:
        sent, kept_terms = attention_call(queries, hops[-1], state, w_back, True)
        terms = kept_terms + swapped(sent, "tp").astype(jnp.float32)
    else:
        (sent,) = attention_call(queries, hops[-1], state, w_back)
        terms = lax.psum_scatter(sent, "tp", scatter_dimension=0).astype(jnp.float32)

    def branch_out(parity):
        term = lax.dynamic_index_in_dim(terms, parity, 0, keepdims=False)
        base = lax.dynamic_index_in_dim(resid_split, parity, 0, keepdims=False)
        return (base.astype(jnp.float32) + term).astype(jnp.bfloat16)

    other_branch = swapped(branch_out(1 - cfg), "cfg")
    kept = branch_out(cfg)
    is_cond = cfg == 0
    cond_out = jnp.where(is_cond, kept, other_branch).astype(jnp.float32)
    uncond_out = jnp.where(is_cond, other_branch, kept).astype(jnp.float32)
    guided = (uncond_out + guidance * (cond_out - uncond_out)).astype(jnp.bfloat16)
    return (guided[:, :, None, :], fresh_kv)


def solution(mesh):
    in_specs = (
        P("cfg", "rows", "tp", None),
        P("cfg", None, "rows", None, "tp"),
        P(),
        P(None, "tp"),
        P("tp"),
        P("tp"),
        P(None, None, "tp", "cfg"),
        P("tp"),
        P("tp"),
        P("tp"),
        P(None, None, "tp"),
        P("tp", None),
    )
    out_specs = (P("rows", "tp", "cfg", None), P("cfg", None, "rows", None, "tp"))
    return jax.shard_map(
        per_device, mesh=mesh, in_specs=in_specs, out_specs=out_specs, check_vma=False
    )
```

```python
import functools
import math

import jax
import jax.numpy as jnp
from jax import lax
from jax.experimental import pallas as pl
from jax.experimental.pallas import tpu as pltpu
from jax.sharding import PartitionSpec as P

D = 1280
HD = 64
GROUPS = 32
TEMB = 320
LANES = 128

epsilon = 1e-05
guidance = 5.0
SCORE_SCALE = 1.0 / math.sqrt(HD)
VMEM_LIMIT = 32 * 1024 * 1024
COST_DIVISOR = 2


def swapped(array, axis):
    return lax.ppermute(array, axis, [(i, i ^ 1) for i in range(lax.axis_size(axis))])


def ring_pairs(count):
    order = list(range(0, count, 2)) + list(range(count - 1, 0, -2))
    forward = [(order[i], order[(i + 1) % count]) for i in range(count)]
    backward = [(j, i) for i, j in forward]
    return forward, backward


def gather_tp(array, axis):
    if lax.axis_size("tp") != 2:
        return lax.all_gather(array, "tp", axis=axis, tiled=True)
    other = swapped(array, "tp")
    first = lax.axis_index("tp") == 0
    return jnp.concatenate(
        [jnp.where(first, array, other), jnp.where(first, other, array)], axis=axis
    )


def summed(array, axes):
    count = lax.axis_size(axes)
    spread = jnp.broadcast_to(array[None], (count,) + array.shape)
    return jnp.sum(lax.all_to_all(spread, axes, 0, 0, tiled=True), axis=0)


def halves_of_inputs(own):
    cfg = lax.axis_index("cfg")
    if lax.axis_size("tp") != 2:
        full = lax.all_gather(own, "tp", axis=1, tiled=True)
        half = full.shape[1] // 2
        mine = lax.dynamic_slice_in_dim(full, cfg * half, half, 1)
        sent = lax.dynamic_slice_in_dim(full, (1 - cfg) * half, half, 1)
        return [mine], [swapped(sent, "cfg")]
    across = lax.ppermute(own, ("cfg", "tp"), [(1, 3), (2, 0)])
    pairs = [(0, 1), (3, 2)]
    own_side = lax.ppermute(own, ("cfg", "tp"), pairs)
    across_side = lax.ppermute(across, ("cfg", "tp"), pairs)
    return [own, own_side], [across, across_side]


def conv_kernel(choices, amount, flags_ref, sums_ref, *refs):
    x_refs = refs[:choices]
    affine_ref, w_hbm, out_ref, w_ref, act_ref, sems = refs[choices:]
    rows = out_ref.shape[0]
    ins = affine_ref.shape[0]
    copies = {}
    for b in (1, 0, 2):
        for a in range(3):
            copies[a, b] = pltpu.make_async_copy(
                w_hbm.at[a, b], w_ref.at[b, :, a * ins : (a + 1) * ins], sems.at[a, b]
            )
            copies[a, b].start()

    groups = ins // (D // GROUPS)
    base = flags_ref[3]

    def column(offset):
        return jnp.concatenate(
            [jnp.full((D // GROUPS, 1), sums_ref[base + offset + g], jnp.float32) for g in range(groups)],
            axis=0,
        )

    mean = column(0) / amount
    variance = column(GROUPS) / amount - mean * mean
    scale = lax.rsqrt(variance + epsilon) * affine_ref[:, 0:1]
    shift = affine_ref[:, 1:2]
    for r in range(rows + 2):
        x = x_refs[0][r]
        if choices == 2:
            x = jnp.where(flags_ref[2] == 1, x, x_refs[1][r])
        z = (x.astype(jnp.float32) - mean) * scale + shift
        z = z * jax.nn.sigmoid(z)
        if r == 0:
            z = jnp.where(flags_ref[0] == 1, z, 0.0)
        if r == rows + 1:
            z = jnp.where(flags_ref[1] == 1, z, 0.0)
        z = z.astype(jnp.bfloat16)
        for a in range(3):
            if 0 <= r - a < rows:
                act_ref[a * ins : (a + 1) * ins, (r - a) * LANES : (r - a + 1) * LANES] = z

    width = min(2, rows)
    lane = lax.broadcasted_iota(jnp.int32, (out_ref.shape[1], LANES), 1)
    for start in range(0, rows, width):
        cols = slice(start * LANES, (start + width) * LANES)
        total = [0.0] * width
        for b in (1, 0, 2):
            if start == 0:
                for a in range(3):
                    copies[a, b].wait()
            y = jnp.dot(w_ref[b], act_ref[:, cols], preferred_element_type=jnp.float32)
            for r in range(width):
                part = y[:, r * LANES : (r + 1) * LANES]
                if b == 0:
                    part = jnp.where(lane == 0, 0.0, pltpu.roll(part, 1, axis=1))
                if b == 2:
                    part = jnp.where(lane == LANES - 1, 0.0, pltpu.roll(part, LANES - 1, axis=1))
                total[r] = total[r] + part
        for r in range(width):
            out_ref[start + r] = total[r].astype(out_ref.dtype)


def conv_call(flags, sums, amount, xs, affine, conv_w, out_dtype):
    x = xs[0]
    rows = x.shape[0] - 2
    outs, ins = conv_w.shape[2:]
    return pl.pallas_call(
        functools.partial(conv_kernel, len(xs), amount),
        in_specs=[
            pl.BlockSpec(memory_space=pltpu.SMEM),
            pl.BlockSpec(memory_space=pltpu.SMEM),
            *[pl.BlockSpec(memory_space=pltpu.VMEM)] * (len(xs) + 1),
            pl.BlockSpec(memory_space=pl.ANY),
        ],
        out_specs=pl.BlockSpec(memory_space=pltpu.VMEM),
        out_shape=jax.ShapeDtypeStruct((rows, outs, LANES), out_dtype),
        scratch_shapes=[
            pltpu.VMEM((3, outs, 3 * ins), jnp.bfloat16),
            pltpu.VMEM((3 * ins, rows * LANES), jnp.bfloat16),
            pltpu.SemaphoreType.DMA((3, 3)),
        ],
        compiler_params=pltpu.CompilerParams(vmem_limit_bytes=VMEM_LIMIT),
        cost_estimate=pl.CostEstimate(
            flops=2 * 9 * outs * ins * rows * LANES // COST_DIVISOR,
            bytes_accessed=2 * 9 * outs * ins // COST_DIVISOR,
            transcendentals=0,
        ),
        name="norm_conv",
    )(flags, sums, *xs, affine, conv_w)


def split_kernel(own_ref, split_ref):
    rows, channels, _ = own_ref.shape
    half = channels // 2
    to = lax.broadcasted_iota(jnp.int32, (channels, channels), 0)
    source = lax.broadcasted_iota(jnp.int32, (channels, channels), 1)
    wanted = jnp.where(to < half, 2 * to, 2 * (to - half) + 1)
    chosen = (source == wanted).astype(jnp.bfloat16)
    for r in range(rows):
        y = jnp.dot(chosen, own_ref[r], preferred_element_type=jnp.float32).astype(jnp.bfloat16)
        split_ref[0, r] = y[:half]
        split_ref[1, r] = y[half:]


def split_call(own):
    rows, channels, _ = own.shape
    return pl.pallas_call(
        split_kernel,
        in_specs=[pl.BlockSpec(memory_space=pltpu.VMEM)],
        out_specs=pl.BlockSpec(memory_space=pltpu.VMEM),
        out_shape=jax.ShapeDtypeStruct((2, rows, channels // 2, LANES), jnp.bfloat16),
        compiler_params=pltpu.CompilerParams(vmem_limit_bytes=VMEM_LIMIT),
        name="parity_split",
    )(own)


def project_kernel(parts, order_ref, *refs):
    part_refs = refs[:parts]
    affine_ref, w_ref, q_ref, kv_ref, normed_ref = refs[parts:]
    rows, channels, _ = part_refs[0].shape
    total = parts * channels
    step = pl.program_id(0)

    @pl.when(step == 0)
    def _():
        for r in range(rows):
            x = [ref[r].astype(jnp.float32) for ref in part_refs]
            mean = sum(jnp.sum(a, axis=0, keepdims=True) for a in x) / total
            var = sum(jnp.sum(a * a, axis=0, keepdims=True) for a in x) / total - mean * mean
            inverse = lax.rsqrt(var + epsilon)
            for j in range(parts):
                at = pl.ds(pl.multiple_of(order_ref[j] * channels, LANES), channels)
                z = (x[j] - mean) * inverse * affine_ref[at, 0:1] + affine_ref[at, 1:2]
                normed_ref[r * LANES : (r + 1) * LANES, at] = z.astype(jnp.bfloat16).T

    y = jnp.dot(normed_ref[...], w_ref[0], preferred_element_type=jnp.float32)
    y = y.astype(jnp.bfloat16)

    @pl.when(step == 0)
    def _():
        q_ref[...] = y * SCORE_SCALE

    @pl.when(step > 0)
    def _():
        kv_ref[0] = y


def project_call(order, parts, affine, w):
    rows, channels, _ = parts[0].shape
    positions = rows * LANES
    _, depth, features = w.shape
    whole = lambda shape: pl.BlockSpec(shape, lambda i: (0,) * len(shape))
    return pl.pallas_call(
        functools.partial(project_kernel, len(parts)),
        grid=(3,),
        in_specs=[
            pl.BlockSpec(memory_space=pltpu.SMEM),
            *[whole(part.shape) for part in parts],
            whole(affine.shape),
            pl.BlockSpec((1, depth, features), lambda i: (i, 0, 0)),
        ],
        out_specs=(
            whole((positions, features)),
            pl.BlockSpec((1, positions, features), lambda i: (jnp.maximum(i - 1, 0), 0, 0)),
        ),
        out_shape=(
            jax.ShapeDtypeStruct((positions, features), jnp.bfloat16),
            jax.ShapeDtypeStruct((2, positions, features), jnp.bfloat16),
        ),
        scratch_shapes=[pltpu.VMEM((positions, depth), jnp.bfloat16)],
        compiler_params=pltpu.CompilerParams(vmem_limit_bytes=VMEM_LIMIT),
        cost_estimate=pl.CostEstimate(
            flops=6 * positions * depth * features // COST_DIVISOR,
            bytes_accessed=6 * depth * features // COST_DIVISOR,
            transcendentals=0,
        ),
        name="norm_project",
    )(order, *parts, affine, w)


def attention_kernel(blocks, carried, final, *refs):
    q_ref = refs[0]
    kv_refs = refs[1 : 1 + 2 * blocks]
    at = 1 + 2 * blocks
    if carried:
        m_in, acc_in = refs[at : at + 2]
        at += 2
    if final:
        w_ref = refs[at]
        at += 1
        out_refs = refs[at:-1]
        joined_ref = refs[-1]
    else:
        m_out, acc_out = refs[at:]
    positions = q_ref.shape[0]
    tile = min(256, positions)
    starts = range(0, positions, tile)
    lanes = lambda array, low: (lax.broadcasted_iota(jnp.int32, array.shape, 1) < HD) == low

    def scores(item):
        start, head, block = item
        q = q_ref[start : start + tile, :]
        q = jnp.where(lanes(q, head == 0), q, jnp.zeros_like(q))
        return lax.dot_general(
            q,
            kv_refs[2 * block][0],
            (((1,), (1,)), ((), ())),
            preferred_element_type=jnp.float32,
        )

    items = [(start, head, block) for start in starts for block in range(blocks) for head in (0, 1)]
    state = {}
    upcoming = scores(items[0])
    for number, item in enumerate(items):
        s = upcoming
        if number + 1 < len(items):
            upcoming = scores(items[number + 1])
        start, head, block = item
        rows = slice(start, start + tile)
        if block == 0 and carried:
            peak, acc = m_in[0, head, rows, :], acc_in[0, head, rows, :]
        elif block == 0:
            peak = acc = None
        else:
            peak, acc = state[start, head]
        v = kv_refs[2 * block + 1][0]
        v = jnp.where(lanes(v, head == 0), v, jnp.ones_like(v))
        top = jnp.broadcast_to(jnp.max(s, axis=1, keepdims=True), (tile, LANES))
        new_peak = top if peak is None else jnp.maximum(peak, top)
        wide = jnp.concatenate([new_peak] * (s.shape[1] // LANES), axis=1)
        p = jnp.exp(s - wide).astype(jnp.bfloat16)
        term = jnp.dot(p, v, preferred_element_type=jnp.float32)
        acc = term if acc is None else acc * jnp.exp(peak - new_peak) + term
        state[start, head] = new_peak, acc
        if block < blocks - 1:
            continue
        if not final:
            m_out[0, head, rows, :] = new_peak
            acc_out[0, head, rows, :] = acc
        elif head == 1:
            parts = [state[start, h][1] for h in (0, 1)]
            parts = [a / pltpu.roll(a, HD, axis=1) for a in parts]
            pair = jnp.where(lanes(acc, True), parts[0], parts[1]).astype(jnp.bfloat16)
            joined_ref[pl.program_id(0), rows, :] = pair

    if final:
        tiles, _, _ = joined_ref.shape

        @pl.when(pl.program_id(0) == tiles - 1)
        def _():
            joined = jnp.concatenate([joined_ref[i] for i in range(tiles)], axis=1)
            for j in range(w_ref.shape[0]):
                y = lax.dot_general(
                    w_ref[j],
                    joined,
                    (((1,), (1,)), ((), ())),
                    preferred_element_type=jnp.float32,
                )
                out = out_refs[j] if len(out_refs) > 1 else out_refs[0].at[j]
                half = w_ref.shape[1] // 2
                for parity in range(2):
                    for r in range(positions // LANES):
                        out[parity, r] = y[
                            parity * half : (parity + 1) * half, r * LANES : (r + 1) * LANES
                        ].astype(out.dtype)


def attention_call(q, pairs, state, w=None, own_apart=False):
    positions, features = q.shape
    tiles = features // LANES
    final = w is not None
    carry = pl.BlockSpec((1, 2, positions, LANES), lambda i: (i, 0, 0, 0))
    carry_shape = jax.ShapeDtypeStruct((tiles, 2, positions, LANES), jnp.float32)
    operands = [q]
    specs = [pl.BlockSpec((positions, LANES), lambda i: (0, i))]
    for pair in pairs:
        for array, place in pair:
            operands.append(array)
            specs.append(
                pl.BlockSpec((1, positions, LANES), functools.partial(lambda p, i: (p, 0, i), place))
            )
    if state is not None:
        operands += list(state)
        specs += [carry, carry]
    scratch = []
    if final:
        operands.append(w)
        specs.append(pl.BlockSpec(w.shape, lambda i: (0, 0, 0)))
        shape = (2, positions // LANES, w.shape[1] // 2, LANES)
        if own_apart:
            out_shape = (
                jax.ShapeDtypeStruct(shape, jnp.bfloat16),
                jax.ShapeDtypeStruct(shape, jnp.float32),
            )
        else:
            out_shape = (jax.ShapeDtypeStruct((w.shape[0],) + shape, jnp.bfloat16),)
        out_specs = tuple(
            pl.BlockSpec(o.shape, functools.partial(lambda n, i: (0,) * n, len(o.shape)))
            for o in out_shape
        )
        scratch = [pltpu.VMEM((tiles, positions, LANES), jnp.bfloat16)]
    else:
        out_shape = (carry_shape, carry_shape)
        out_specs = (carry, carry)
    keys = positions * len(pairs)
    return pl.pallas_call(
        functools.partial(attention_kernel, len(pairs), state is not None, final),
        grid=(tiles,),
        in_specs=specs,
        out_specs=out_specs,
        out_shape=out_shape,
        scratch_shapes=scratch,
        compiler_params=pltpu.CompilerParams(vmem_limit_bytes=VMEM_LIMIT),
        cost_estimate=pl.CostEstimate(
            flops=16 * positions * keys * features // COST_DIVISOR,
            bytes_accessed=4 * keys * features // COST_DIVISOR,
            transcendentals=0,
        ),
        name="attend",
    )(*operands)


def per_device(
    latent,
    stale_kv,
    timestep,
    w_time,
    gn_gain,
    gn_bias,
    conv_w,
    conv_b,
    ln_gain,
    ln_bias,
    w_qkv,
    w_out,
):
    latent_rows = latent[0]
    rows_count = lax.axis_size("rows")
    tp_count = lax.axis_size("tp")
    span_rows, local_channels, grid_width = latent_rows.shape
    positions = span_rows * grid_width
    group_width = D // GROUPS
    local_groups = local_channels // group_width
    my_block = lax.axis_index("rows")
    cfg = lax.axis_index("cfg")
    tp = lax.axis_index("tp")

    latent32 = latent_rows.astype(jnp.float32)
    values32 = latent32.reshape(span_rows, local_groups, group_width, grid_width)
    sums = jnp.stack(
        [jnp.sum(values32, axis=(0, 2, 3)), jnp.sum(values32 * values32, axis=(0, 2, 3))]
    )
    table = jnp.zeros((2, 2, GROUPS), jnp.float32)
    table = lax.dynamic_update_slice(table, sums[None], (cfg, 0, tp * local_groups))
    table = summed(table.reshape(-1), ("cfg", "rows", "tp"))

    up_pairs = [(i, i + 1) for i in range(rows_count - 1)]
    down_pairs = [(i + 1, i) for i in range(rows_count - 1)]
    before = lax.ppermute(latent_rows[span_rows - 1 :], "rows", up_pairs)
    after = lax.ppermute(latent_rows[:1], "rows", down_pairs)
    pair = stale_kv[0].reshape(2, positions, -1)
    pair, table, before, after = lax.optimization_barrier((pair, table, before, after))
    rimmed = jnp.concatenate([before, latent_rows, after], axis=0)
    x_mine, x_other = halves_of_inputs(rimmed)

    forward, backward = ring_pairs(rows_count)
    hops = [(pair, pair)]

    def next_hop(*after):
        ahead, behind = hops[-1]
        if len(hops) == rows_count // 2:
            ahead, behind = ahead[:1], behind[1:]
        ahead, behind, *_ = lax.optimization_barrier((ahead, behind) + after)
        hops.append(
            (lax.ppermute(ahead, "rows", forward), lax.ppermute(behind, "rows", backward))
        )

    def blocks_of(hop):
        ahead, behind = hops[hop]
        if hop == rows_count // 2:
            return [((ahead, 0), (behind, 0))]
        return [((ahead, 0), (ahead, 1)), ((behind, 0), (behind, 1))]

    next_hop()

    vectors = gather_tp(jnp.stack([gn_gain, gn_bias, ln_gain, ln_bias]), 1).astype(jnp.float32)
    amount = span_rows * rows_count * grid_width * group_width
    half = D // 2
    gn_affine = lax.dynamic_slice_in_dim(vectors[:2], cfg * half, half, 1).T
    ln_affine = vectors[2:].T
    flags = jnp.stack([my_block > 0, my_block < rows_count - 1, tp == cfg]).astype(jnp.int32)
    place = cfg * (GROUPS // 2)
    flags_mine = jnp.append(flags, cfg * 2 * GROUPS + place)
    flags_other = jnp.append(flags, (1 - cfg) * 2 * GROUPS + place)

    local_features = w_qkv.shape[2]
    w_project = w_qkv.transpose(1, 0, 2)
    w_back = w_out.T.reshape(tp_count, local_channels // 2, 2, local_features)
    w_back = w_back.transpose(0, 2, 1, 3).reshape(tp_count, local_channels, local_features)
    if tp_count == 2:
        w_back = jnp.where(tp == 0, w_back[::-1], w_back)
    gn_affine, w_back = lax.optimization_barrier((gn_affine, w_back))

    conv_sent = conv_call(flags_other, table, amount, x_other, gn_affine, conv_w, jnp.bfloat16)
    conv_received = swapped(conv_sent, "cfg")
    flags_mine, *_ = lax.optimization_barrier((flags_mine,) + hops[1])
    next_hop(conv_sent)
    conv_own = conv_call(flags_mine, table, amount, x_mine, gn_affine, conv_w, jnp.float32)

    half_width = TEMB // 2
    frequencies = jnp.exp(
        -math.log(10000.0) * jnp.arange(half_width, dtype=jnp.float32) / half_width
    )
    angles = timestep.astype(jnp.float32)[0] * frequencies
    embedding = jnp.concatenate([jnp.cos(angles), jnp.sin(angles)])
    time_bias = jnp.dot(
        jax.nn.silu(embedding)[None, :], w_time.astype(jnp.float32), precision=lax.Precision.HIGHEST
    )[0]
    bias = conv_b.astype(jnp.float32) + time_bias
    resid = (
        latent32 + (conv_own + conv_received.astype(jnp.float32) + bias[None, :, None])
    ).astype(jnp.bfloat16)

    if tp_count == 2:
        parts = [resid, swapped(resid, "tp")]
        order = jnp.stack([tp, 1 - tp]).astype(jnp.int32)
    else:
        parts = [lax.all_gather(resid, "tp", axis=1, tiled=True)]
        order = jnp.zeros((1,), jnp.int32)
    queries, fresh = project_call(order, parts, ln_affine, w_project)
    resid_split = split_call(resid)
    fresh_kv = fresh.reshape(1, 2, span_rows, grid_width, local_features)

    last = rows_count // 2
    state = attention_call(queries, [((fresh, 0), (fresh, 1))], None)
    next_hop(state[0])
    group = blocks_of(1) + blocks_of(2)
    for hop in range(3, last + 1):
        state = attention_call(queries, group, state)
        if hop < last:
            next_hop(state[0])
        group = blocks_of(hop)
    if tp_count == 2:
        sent, kept_terms = attention_call(queries, group, state, w_back, True)
        terms = kept_terms + swapped(sent, "tp").astype(jnp.float32)
    else:
        (sent,) = attention_call(queries, group, state, w_back)
        terms = lax.psum_scatter(sent, "tp", scatter_dimension=0).astype(jnp.float32)

    def branch_out(parity):
        term = lax.dynamic_index_in_dim(terms, parity, 0, keepdims=False)
        base = lax.dynamic_index_in_dim(resid_split, parity, 0, keepdims=False)
        return (base.astype(jnp.float32) + term).astype(jnp.bfloat16)

    other_branch = swapped(branch_out(1 - cfg), "cfg")
    kept = branch_out(cfg)
    is_cond = cfg == 0
    cond_out = jnp.where(is_cond, kept, other_branch).astype(jnp.float32)
    uncond_out = jnp.where(is_cond, other_branch, kept).astype(jnp.float32)
    guided = (uncond_out + guidance * (cond_out - uncond_out)).astype(jnp.bfloat16)
    return (guided[:, :, None, :], fresh_kv)


def solution(mesh):
    in_specs = (
        P("cfg", "rows", "tp", None),
        P("cfg", None, "rows", None, "tp"),
        P(),
        P(None, "tp"),
        P("tp"),
        P("tp"),
        P(None, None, "tp", "cfg"),
        P("tp"),
        P("tp"),
        P("tp"),
        P(None, None, "tp"),
        P("tp", None),
    )
    out_specs = (P("rows", "tp", "cfg", None), P("cfg", None, "rows", None, "tp"))
    return jax.shard_map(
        per_device, mesh=mesh, in_specs=in_specs, out_specs=out_specs, check_vma=False
    )
```

```python
import functools
import math

import jax
import jax.numpy as jnp
from jax import lax
from jax.experimental import pallas as pl
from jax.experimental.pallas import tpu as pltpu
from jax.sharding import PartitionSpec as P

D = 1280
HD = 64
GROUPS = 32
TEMB = 320
LANES = 128

epsilon = 1e-05
guidance = 5.0
SCORE_SCALE = 1.0 / math.sqrt(HD)
VMEM_LIMIT = 32 * 1024 * 1024
COST_SHARE = 0.02


def cost(work):
    return pl.CostEstimate(flops=int(work * 1e6 * COST_SHARE), bytes_accessed=1000, transcendentals=0)


def swapped(array, axis):
    return lax.ppermute(array, axis, [(i, i ^ 1) for i in range(lax.axis_size(axis))])


def ring_pairs(count):
    order = list(range(0, count, 2)) + list(range(count - 1, 0, -2))
    forward = [(order[i], order[(i + 1) % count]) for i in range(count)]
    backward = [(j, i) for i, j in forward]
    return forward, backward


def gather_tp(array, axis):
    if lax.axis_size("tp") != 2:
        return lax.all_gather(array, "tp", axis=axis, tiled=True)
    other = swapped(array, "tp")
    first = lax.axis_index("tp") == 0
    return jnp.concatenate(
        [jnp.where(first, array, other), jnp.where(first, other, array)], axis=axis
    )


def summed(array, axes):
    count = lax.axis_size(axes)
    spread = jnp.broadcast_to(array[None], (count,) + array.shape)
    return jnp.sum(lax.all_to_all(spread, axes, 0, 0, tiled=True), axis=0)


def need(array, others):
    return lax.optimization_barrier((array,) + tuple(others))[0]


def halves_of_inputs(own, others):
    cfg = lax.axis_index("cfg")
    if lax.axis_size("tp") != 2:
        full = lax.all_gather(own, "tp", axis=1, tiled=True)
        half = full.shape[1] // 2
        mine = lax.dynamic_slice_in_dim(full, cfg * half, half, 1)
        sent = lax.dynamic_slice_in_dim(full, (1 - cfg) * half, half, 1)
        return [mine], [swapped(sent, "cfg")]
    across = lax.ppermute(own, ("cfg", "tp"), [(1, 3), (2, 0)])
    pairs = [(0, 1), (3, 2)]
    own_side = lax.ppermute(need(own, others), ("cfg", "tp"), pairs)
    across_side = lax.ppermute(need(across, others), ("cfg", "tp"), pairs)
    return [own, own_side], [across, across_side]


def conv_kernel(choices, amount, flags_ref, sums_ref, *refs):
    x_refs = refs[:choices]
    affine_ref, w_hbm, out_ref, w_ref, act_ref, sems = refs[choices:]
    rows = out_ref.shape[0]
    ins = affine_ref.shape[0]
    copies = {}
    for b in (1, 0, 2):
        for a in range(3):
            copies[a, b] = pltpu.make_async_copy(
                w_hbm.at[a, b], w_ref.at[b, :, a * ins : (a + 1) * ins], sems.at[a, b]
            )
            copies[a, b].start()

    groups = ins // (D // GROUPS)
    base = flags_ref[3]

    def column(offset):
        return jnp.concatenate(
            [jnp.full((D // GROUPS, 1), sums_ref[base + offset + g], jnp.float32) for g in range(groups)],
            axis=0,
        )

    mean = column(0) / amount
    variance = column(GROUPS) / amount - mean * mean
    scale = lax.rsqrt(variance + epsilon) * affine_ref[:, 0:1]
    shift = affine_ref[:, 1:2]
    for r in range(rows + 2):
        x = x_refs[0][r]
        if choices == 2:
            x = jnp.where(flags_ref[2] == 1, x, x_refs[1][r])
        z = (x.astype(jnp.float32) - mean) * scale + shift
        z = z * jax.nn.sigmoid(z)
        if r == 0:
            z = jnp.where(flags_ref[0] == 1, z, 0.0)
        if r == rows + 1:
            z = jnp.where(flags_ref[1] == 1, z, 0.0)
        z = z.astype(jnp.bfloat16)
        for a in range(3):
            if 0 <= r - a < rows:
                act_ref[a * ins : (a + 1) * ins, (r - a) * LANES : (r - a + 1) * LANES] = z

    width = min(2, rows)
    lane = lax.broadcasted_iota(jnp.int32, (out_ref.shape[1], LANES), 1)
    for start in range(0, rows, width):
        cols = slice(start * LANES, (start + width) * LANES)
        total = [0.0] * width
        for b in (1, 0, 2):
            if start == 0:
                for a in range(3):
                    copies[a, b].wait()
            y = jnp.dot(w_ref[b], act_ref[:, cols], preferred_element_type=jnp.float32)
            for r in range(width):
                part = y[:, r * LANES : (r + 1) * LANES]
                if b == 0:
                    part = jnp.where(lane == 0, 0.0, pltpu.roll(part, 1, axis=1))
                if b == 2:
                    part = jnp.where(lane == LANES - 1, 0.0, pltpu.roll(part, LANES - 1, axis=1))
                total[r] = total[r] + part
        for r in range(width):
            out_ref[start + r] = total[r].astype(out_ref.dtype)


def conv_call(flags, sums, amount, xs, affine, conv_w, out_dtype):
    x = xs[0]
    rows = x.shape[0] - 2
    outs, ins = conv_w.shape[2:]
    return pl.pallas_call(
        functools.partial(conv_kernel, len(xs), amount),
        in_specs=[
            pl.BlockSpec(memory_space=pltpu.SMEM),
            pl.BlockSpec(memory_space=pltpu.SMEM),
            *[pl.BlockSpec(memory_space=pltpu.VMEM)] * (len(xs) + 1),
            pl.BlockSpec(memory_space=pltpu.HBM),
        ],
        out_specs=pl.BlockSpec(memory_space=pltpu.VMEM),
        out_shape=jax.ShapeDtypeStruct((rows, outs, LANES), out_dtype),
        scratch_shapes=[
            pltpu.VMEM((3, outs, 3 * ins), jnp.bfloat16),
            pltpu.VMEM((3 * ins, rows * LANES), jnp.bfloat16),
            pltpu.SemaphoreType.DMA((3, 3)),
        ],
        compiler_params=pltpu.CompilerParams(vmem_limit_bytes=VMEM_LIMIT),
        cost_estimate=cost(9000),
        name="norm_conv",
    )(flags, sums, *xs, affine, conv_w)


def split_kernel(own_ref, split_ref):
    rows, channels, _ = own_ref.shape
    half = channels // 2
    to = lax.broadcasted_iota(jnp.int32, (channels, channels), 0)
    source = lax.broadcasted_iota(jnp.int32, (channels, channels), 1)
    wanted = jnp.where(to < half, 2 * to, 2 * (to - half) + 1)
    chosen = (source == wanted).astype(jnp.bfloat16)
    for r in range(rows):
        y = jnp.dot(chosen, own_ref[r], preferred_element_type=jnp.float32).astype(jnp.bfloat16)
        split_ref[0, r] = y[:half]
        split_ref[1, r] = y[half:]


def split_call(own):
    rows, channels, _ = own.shape
    return pl.pallas_call(
        split_kernel,
        in_specs=[pl.BlockSpec(memory_space=pltpu.VMEM)],
        out_specs=pl.BlockSpec(memory_space=pltpu.VMEM),
        out_shape=jax.ShapeDtypeStruct((2, rows, channels // 2, LANES), jnp.bfloat16),
        compiler_params=pltpu.CompilerParams(vmem_limit_bytes=VMEM_LIMIT),
        cost_estimate=cost(1000),
        name="parity_split",
    )(own)


def project_kernel(parts, order_ref, *refs):
    part_refs = refs[:parts]
    affine_ref, w_hbm, q_ref, kv_ref, w_ref, normed_ref, sems = refs[parts:]
    rows, channels, _ = part_refs[0].shape
    total = parts * channels
    copies = [pltpu.make_async_copy(w_hbm.at[i], w_ref.at[i], sems.at[i]) for i in range(3)]
    for copy in copies:
        copy.start()
    for r in range(rows):
        x = [ref[r].astype(jnp.float32) for ref in part_refs]
        mean = sum(jnp.sum(a, axis=0, keepdims=True) for a in x) / total
        var = sum(jnp.sum(a * a, axis=0, keepdims=True) for a in x) / total - mean * mean
        inverse = lax.rsqrt(var + epsilon)
        for j in range(parts):
            at = pl.ds(pl.multiple_of(order_ref[j] * channels, LANES), channels)
            z = (x[j] - mean) * inverse * affine_ref[at, 0:1] + affine_ref[at, 1:2]
            normed_ref[r * LANES : (r + 1) * LANES, at] = z.astype(jnp.bfloat16).T
    for i in range(3):
        copies[i].wait()
        y = jnp.dot(normed_ref[...], w_ref[i], preferred_element_type=jnp.float32)
        y = y.astype(jnp.bfloat16)
        if i == 0:
            q_ref[...] = y * SCORE_SCALE
        else:
            kv_ref[i - 1] = y


def project_call(order, parts, affine, w):
    rows = parts[0].shape[0]
    positions = rows * LANES
    _, depth, features = w.shape
    vmem = pl.BlockSpec(memory_space=pltpu.VMEM)
    return pl.pallas_call(
        functools.partial(project_kernel, len(parts)),
        in_specs=[
            pl.BlockSpec(memory_space=pltpu.SMEM),
            *[vmem] * (len(parts) + 1),
            pl.BlockSpec(memory_space=pltpu.HBM),
        ],
        out_specs=(vmem, vmem),
        out_shape=(
            jax.ShapeDtypeStruct((positions, features), jnp.bfloat16),
            jax.ShapeDtypeStruct((2, positions, features), jnp.bfloat16),
        ),
        scratch_shapes=[
            pltpu.VMEM((3, depth, features), jnp.bfloat16),
            pltpu.VMEM((positions, depth), jnp.bfloat16),
            pltpu.SemaphoreType.DMA((3,)),
        ],
        compiler_params=pltpu.CompilerParams(vmem_limit_bytes=VMEM_LIMIT),
        cost_estimate=cost(6500),
        name="norm_project",
    )(order, *parts, affine, w)


def branch_kernel(parity_ref, resid_ref, *refs):
    total = resid_ref[0].astype(jnp.float32)
    for ref in refs[:-1]:
        total = total + ref[0].astype(jnp.float32)
    refs[-1][...] = total.astype(jnp.bfloat16)


def branch_call(parity, resid_split, terms):
    shape = resid_split.shape
    block = pl.BlockSpec((1,) + shape[1:], lambda i, parity: (parity[0], 0, 0, 0))
    return pl.pallas_call(
        branch_kernel,
        grid_spec=pltpu.PrefetchScalarGridSpec(
            num_scalar_prefetch=1,
            grid=(1,),
            in_specs=[block] * (1 + len(terms)),
            out_specs=pl.BlockSpec(shape[1:], lambda i, parity: (0, 0, 0)),
        ),
        out_shape=jax.ShapeDtypeStruct(shape[1:], jnp.bfloat16),
        compiler_params=pltpu.CompilerParams(vmem_limit_bytes=VMEM_LIMIT),
        cost_estimate=cost(1000),
        name="branch_out",
    )(parity.astype(jnp.int32).reshape(1), resid_split, *terms)


def attention_kernel(blocks, carried, final, *refs):
    q_ref = refs[0]
    kv_refs = refs[1 : 1 + 2 * blocks]
    at = 1 + 2 * blocks
    if carried:
        m_in, acc_in = refs[at : at + 2]
        at += 2
    if final:
        w_ref = refs[at]
        at += 1
        out_refs = refs[at:-1]
        joined_ref = refs[-1]
    else:
        m_out, acc_out = refs[at:]
    positions = q_ref.shape[0]
    tile = min(256, positions)
    starts = range(0, positions, tile)
    lanes = lambda array, low: (lax.broadcasted_iota(jnp.int32, array.shape, 1) < HD) == low

    def scores(item):
        start, head, block = item
        q = q_ref[start : start + tile, :]
        q = jnp.where(lanes(q, head == 0), q, jnp.zeros_like(q))
        return lax.dot_general(
            q,
            kv_refs[2 * block][0],
            (((1,), (1,)), ((), ())),
            preferred_element_type=jnp.float32,
        )

    items = [(start, head, block) for start in starts for block in range(blocks) for head in (0, 1)]
    state = {}
    upcoming = scores(items[0])
    for number, item in enumerate(items):
        s = upcoming
        if number + 1 < len(items):
            upcoming = scores(items[number + 1])
        start, head, block = item
        rows = slice(start, start + tile)
        if block == 0 and carried:
            peak, acc = m_in[0, head, rows, :], acc_in[0, head, rows, :]
        elif block == 0:
            peak = acc = None
        else:
            peak, acc = state[start, head]
        v = kv_refs[2 * block + 1][0]
        v = jnp.where(lanes(v, head == 0), v, jnp.ones_like(v))
        top = jnp.broadcast_to(jnp.max(s, axis=1, keepdims=True), (tile, LANES))
        new_peak = top if peak is None else jnp.maximum(peak, top)
        wide = jnp.concatenate([new_peak] * (s.shape[1] // LANES), axis=1)
        p = jnp.exp(s - wide).astype(jnp.bfloat16)
        term = jnp.dot(p, v, preferred_element_type=jnp.float32)
        acc = term if acc is None else acc * jnp.exp(peak - new_peak) + term
        state[start, head] = new_peak, acc
        if block < blocks - 1:
            continue
        if not final:
            m_out[0, head, rows, :] = new_peak
            acc_out[0, head, rows, :] = acc
        elif head == 1:
            parts = [state[start, h][1] for h in (0, 1)]
            parts = [a / pltpu.roll(a, HD, axis=1) for a in parts]
            pair = jnp.where(lanes(acc, True), parts[0], parts[1]).astype(jnp.bfloat16)
            joined_ref[pl.program_id(0), rows, :] = pair

    if final:
        tiles, _, _ = joined_ref.shape

        @pl.when(pl.program_id(0) == tiles - 1)
        def _():
            joined = jnp.concatenate([joined_ref[i] for i in range(tiles)], axis=1)
            for j in range(w_ref.shape[0]):
                y = lax.dot_general(
                    w_ref[j],
                    joined,
                    (((1,), (1,)), ((), ())),
                    preferred_element_type=jnp.float32,
                )
                out = out_refs[j] if len(out_refs) > 1 else out_refs[0].at[j]
                half = w_ref.shape[1] // 2
                for parity in range(2):
                    for r in range(positions // LANES):
                        out[parity, r] = y[
                            parity * half : (parity + 1) * half, r * LANES : (r + 1) * LANES
                        ].astype(out.dtype)


def attention_call(q, pairs, state, w=None, own_apart=False):
    positions, features = q.shape
    tiles = features // LANES
    final = w is not None
    carry = pl.BlockSpec((1, 2, positions, LANES), lambda i: (i, 0, 0, 0))
    carry_shape = jax.ShapeDtypeStruct((tiles, 2, positions, LANES), jnp.float32)
    operands = [q]
    specs = [pl.BlockSpec((positions, LANES), lambda i: (0, i))]
    for pair in pairs:
        for array, place in pair:
            operands.append(array)
            specs.append(
                pl.BlockSpec((1, positions, LANES), functools.partial(lambda p, i: (p, 0, i), place))
            )
    if state is not None:
        operands += list(state)
        specs += [carry, carry]
    scratch = []
    if final:
        operands.append(w)
        specs.append(pl.BlockSpec(w.shape, lambda i: (0, 0, 0)))
        shape = (2, positions // LANES, w.shape[1] // 2, LANES)
        if own_apart:
            out_shape = (
                jax.ShapeDtypeStruct(shape, jnp.bfloat16),
                jax.ShapeDtypeStruct(shape, jnp.float32),
            )
        else:
            out_shape = (jax.ShapeDtypeStruct((w.shape[0],) + shape, jnp.bfloat16),)
        out_specs = tuple(
            pl.BlockSpec(o.shape, functools.partial(lambda n, i: (0,) * n, len(o.shape)))
            for o in out_shape
        )
        scratch = [pltpu.VMEM((tiles, positions, LANES), jnp.bfloat16)]
    else:
        out_shape = (carry_shape, carry_shape)
        out_specs = (carry, carry)
    keys = positions * len(pairs)
    return pl.pallas_call(
        functools.partial(attention_kernel, len(pairs), state is not None, final),
        grid=(tiles,),
        in_specs=specs,
        out_specs=out_specs,
        out_shape=out_shape,
        scratch_shapes=scratch,
        compiler_params=pltpu.CompilerParams(vmem_limit_bytes=VMEM_LIMIT),
        cost_estimate=cost(1000 + 3200 * len(pairs)),
        name="attend",
    )(*operands)


def per_device(
    latent,
    stale_kv,
    timestep,
    w_time,
    gn_gain,
    gn_bias,
    conv_w,
    conv_b,
    ln_gain,
    ln_bias,
    w_qkv,
    w_out,
):
    latent_rows = latent[0]
    rows_count = lax.axis_size("rows")
    tp_count = lax.axis_size("tp")
    span_rows, local_channels, grid_width = latent_rows.shape
    positions = span_rows * grid_width
    group_width = D // GROUPS
    local_groups = local_channels // group_width
    my_block = lax.axis_index("rows")
    cfg = lax.axis_index("cfg")
    tp = lax.axis_index("tp")

    latent32 = latent_rows.astype(jnp.float32)
    values32 = latent32.reshape(span_rows, local_groups, group_width, grid_width)
    sums = jnp.stack(
        [jnp.sum(values32, axis=(0, 2, 3)), jnp.sum(values32 * values32, axis=(0, 2, 3))]
    )
    table = jnp.zeros((2, 2, GROUPS), jnp.float32)
    table = lax.dynamic_update_slice(table, sums[None], (cfg, 0, tp * local_groups))
    table = summed(table.reshape(-1), ("cfg", "rows", "tp"))

    up_pairs = [(i, i + 1) for i in range(rows_count - 1)]
    down_pairs = [(i + 1, i) for i in range(rows_count - 1)]
    before = lax.ppermute(latent_rows[span_rows - 1 :], "rows", up_pairs)
    after = lax.ppermute(latent_rows[:1], "rows", down_pairs)
    rimmed = jnp.concatenate([before, latent_rows, after], axis=0)

    forward, backward = ring_pairs(rows_count)
    last = rows_count // 2
    stale = stale_kv[0].reshape(2, 1, positions, -1)
    hops = [[(stale[which], stale[which])] for which in range(2)]

    def next_hop(which, *after):
        ahead, behind = hops[which][-1]
        if after:
            ahead, behind, *_ = lax.optimization_barrier((ahead, behind) + after)
        final = len(hops[which]) == last
        if not (final and which == 1):
            ahead = lax.ppermute(ahead, "rows", forward)
        if not (final and which == 0):
            behind = lax.ppermute(behind, "rows", backward)
        hops[which].append((ahead, behind))

    def blocks_of(hop):
        keys, values = hops[0][hop], hops[1][hop]
        if hop == last:
            return [((keys[0], 0), (values[1], 0))]
        return [((keys[0], 0), (values[0], 0)), ((keys[1], 0), (values[1], 0))]

    next_hop(0)
    x_mine, x_other = halves_of_inputs(rimmed, hops[0][1])
    next_hop(1, table)
    next_hop(0, table)

    vectors = gather_tp(jnp.stack([gn_gain, gn_bias, ln_gain, ln_bias]), 1).astype(jnp.float32)
    amount = span_rows * rows_count * grid_width * group_width
    half = D // 2
    gn_affine = lax.dynamic_slice_in_dim(vectors[:2], cfg * half, half, 1).T
    ln_affine = vectors[2:].T
    flags = jnp.stack([my_block > 0, my_block < rows_count - 1, tp == cfg]).astype(jnp.int32)
    place = cfg * (GROUPS // 2)
    flags_mine = jnp.append(flags, cfg * 2 * GROUPS + place)
    flags_other = jnp.append(flags, (1 - cfg) * 2 * GROUPS + place)

    local_features = w_qkv.shape[2]
    w_project = w_qkv.transpose(1, 0, 2)
    w_back = w_out.T.reshape(tp_count, local_channels // 2, 2, local_features)
    w_back = w_back.transpose(0, 2, 1, 3).reshape(tp_count, local_channels, local_features)
    if tp_count == 2:
        w_back = jnp.where(tp == 0, w_back[::-1], w_back)
    gn_affine, w_back = lax.optimization_barrier((gn_affine, w_back))

    conv_sent = conv_call(flags_other, table, amount, x_other, gn_affine, conv_w, jnp.bfloat16)
    conv_received = swapped(conv_sent, "cfg")
    next_hop(1, conv_sent)
    flags_mine = need(flags_mine, hops[1][1] + hops[0][2])
    conv_own = conv_call(flags_mine, table, amount, x_mine, gn_affine, conv_w, jnp.float32)

    half_width = TEMB // 2
    frequencies = jnp.exp(
        -math.log(10000.0) * jnp.arange(half_width, dtype=jnp.float32) / half_width
    )
    angles = timestep.astype(jnp.float32)[0] * frequencies
    embedding = jnp.concatenate([jnp.cos(angles), jnp.sin(angles)])
    time_bias = jnp.dot(
        jax.nn.silu(embedding)[None, :], w_time.astype(jnp.float32), precision=lax.Precision.HIGHEST
    )[0]
    bias = conv_b.astype(jnp.float32) + time_bias
    resid = (
        latent32 + (conv_own + conv_received.astype(jnp.float32) + bias[None, :, None])
    ).astype(jnp.bfloat16)

    next_hop(0, conv_sent)
    if tp_count == 2:
        parts = [resid, swapped(resid, "tp")]
        order = jnp.stack([tp, 1 - tp]).astype(jnp.int32)
    else:
        parts = [lax.all_gather(resid, "tp", axis=1, tiled=True)]
        order = jnp.zeros((1,), jnp.int32)
    next_hop(1, resid)
    order = need(order, hops[1][2])
    queries, fresh = project_call(order, parts, ln_affine, w_project)
    while len(hops[0]) <= last:
        next_hop(0, queries)
    resid_split = split_call(resid)
    fresh_kv = fresh.reshape(1, 2, span_rows, grid_width, local_features)

    queries = need(queries, hops[0][3])
    state = attention_call(queries, [((fresh, 0), (fresh, 1))], None)
    while len(hops[1]) <= last:
        next_hop(1, state[0])
    for hop in range(1, last):
        if hop == 2:
            queries = need(queries, hops[1][3])
        state = attention_call(queries, blocks_of(hop), state)
    if tp_count == 2:
        sent, kept_terms = attention_call(queries, blocks_of(last), state, w_back, True)
        terms = (kept_terms, swapped(sent, "tp"))
    else:
        (sent,) = attention_call(queries, blocks_of(last), state, w_back)
        terms = (lax.psum_scatter(sent, "tp", scatter_dimension=0),)

    other_branch = swapped(branch_call(1 - cfg, resid_split, terms), "cfg")
    kept = branch_call(cfg, resid_split, terms)
    is_cond = cfg == 0
    cond_out = jnp.where(is_cond, kept, other_branch).astype(jnp.float32)
    uncond_out = jnp.where(is_cond, other_branch, kept).astype(jnp.float32)
    guided = (uncond_out + guidance * (cond_out - uncond_out)).astype(jnp.bfloat16)
    return (guided[:, :, None, :], fresh_kv)


def solution(mesh):
    in_specs = (
        P("cfg", "rows", "tp", None),
        P("cfg", None, "rows", None, "tp"),
        P(),
        P(None, "tp"),
        P("tp"),
        P("tp"),
        P(None, None, "tp", "cfg"),
        P("tp"),
        P("tp"),
        P("tp"),
        P(None, None, "tp"),
        P("tp", None),
    )
    out_specs = (P("rows", "tp", "cfg", None), P("cfg", None, "rows", None, "tp"))
    return jax.shard_map(
        per_device, mesh=mesh, in_specs=in_specs, out_specs=out_specs, check_vma=False
    )
```

```python
import functools
import math

import jax
import jax.numpy as jnp
from jax import lax
from jax.experimental import pallas as pl
from jax.experimental.pallas import tpu as pltpu
from jax.sharding import PartitionSpec as P

D = 1280
HD = 64
GROUPS = 32
TEMB = 320
LANES = 128

epsilon = 1e-05
guidance = 5.0
SCORE_SCALE = 1.0 / math.sqrt(HD)
MIB = 1024 * 1024
VMEM_LIMIT = 32 * MIB
COST_SHARE = 0.02


def cost(work):
    return pl.CostEstimate(flops=int(work * 1e6 * COST_SHARE), bytes_accessed=1000, transcendentals=0)


def swapped(array, axis):
    return lax.ppermute(array, axis, [(i, i ^ 1) for i in range(lax.axis_size(axis))])


def ring_pairs(count):
    order = list(range(0, count, 2)) + list(range(count - 1, 0, -2))
    forward = [(order[i], order[(i + 1) % count]) for i in range(count)]
    backward = [(j, i) for i, j in forward]
    return forward, backward


def gather_tp(array, axis):
    if lax.axis_size("tp") != 2:
        return lax.all_gather(array, "tp", axis=axis, tiled=True)
    other = swapped(array, "tp")
    first = lax.axis_index("tp") == 0
    return jnp.concatenate(
        [jnp.where(first, array, other), jnp.where(first, other, array)], axis=axis
    )


def summed(array, axes):
    count = lax.axis_size(axes)
    spread = jnp.broadcast_to(array[None], (count,) + array.shape)
    return jnp.sum(lax.all_to_all(spread, axes, 0, 0, tiled=True), axis=0)


def need(array, others):
    return lax.optimization_barrier((array,) + tuple(others))[0]


def halves_of_inputs(own):
    cfg = lax.axis_index("cfg")
    if lax.axis_size("tp") != 2:
        full = lax.all_gather(own, "tp", axis=1, tiled=True)
        half = full.shape[1] // 2
        mine = lax.dynamic_slice_in_dim(full, cfg * half, half, 1)
        sent = lax.dynamic_slice_in_dim(full, (1 - cfg) * half, half, 1)
        return [mine], [swapped(sent, "cfg")]
    across = lax.ppermute(own, ("cfg", "tp"), [(1, 3), (2, 0)])
    pairs = [(0, 1), (3, 2)]
    own_side = lax.ppermute(own, ("cfg", "tp"), pairs)
    across_side = lax.ppermute(across, ("cfg", "tp"), pairs)
    return [own, own_side], [across, across_side]


def conv_kernel(choices, amount, flags_ref, sums_ref, *refs):
    x_refs = refs[:choices]
    affine_ref, w_hbm, out_ref, w_ref, act_ref, sems = refs[choices:]
    rows = out_ref.shape[0]
    ins = affine_ref.shape[0]
    copies = {}
    for b in (1, 0, 2):
        for a in range(3):
            copies[a, b] = pltpu.make_async_copy(
                w_hbm.at[a, b], w_ref.at[b, :, a * ins : (a + 1) * ins], sems.at[a, b]
            )
            copies[a, b].start()

    groups = ins // (D // GROUPS)
    base = flags_ref[3]

    def column(offset):
        return jnp.concatenate(
            [jnp.full((D // GROUPS, 1), sums_ref[base + offset + g], jnp.float32) for g in range(groups)],
            axis=0,
        )

    mean = column(0) / amount
    variance = column(GROUPS) / amount - mean * mean
    scale = lax.rsqrt(variance + epsilon) * affine_ref[:, 0:1]
    shift = affine_ref[:, 1:2]
    for r in range(rows + 2):
        x = x_refs[0][r]
        if choices == 2:
            x = jnp.where(flags_ref[2] == 1, x, x_refs[1][r])
        z = (x.astype(jnp.float32) - mean) * scale + shift
        z = z * jax.nn.sigmoid(z)
        if r == 0:
            z = jnp.where(flags_ref[0] == 1, z, 0.0)
        if r == rows + 1:
            z = jnp.where(flags_ref[1] == 1, z, 0.0)
        z = z.astype(jnp.bfloat16)
        for a in range(3):
            if 0 <= r - a < rows:
                act_ref[a * ins : (a + 1) * ins, (r - a) * LANES : (r - a + 1) * LANES] = z

    width = min(2, rows)
    lane = lax.broadcasted_iota(jnp.int32, (out_ref.shape[1], LANES), 1)
    for start in range(0, rows, width):
        cols = slice(start * LANES, (start + width) * LANES)
        total = [0.0] * width
        for b in (1, 0, 2):
            if start == 0:
                for a in range(3):
                    copies[a, b].wait()
            y = jnp.dot(w_ref[b], act_ref[:, cols], preferred_element_type=jnp.float32)
            for r in range(width):
                part = y[:, r * LANES : (r + 1) * LANES]
                if b == 0:
                    part = jnp.where(lane == 0, 0.0, pltpu.roll(part, 1, axis=1))
                if b == 2:
                    part = jnp.where(lane == LANES - 1, 0.0, pltpu.roll(part, LANES - 1, axis=1))
                total[r] = total[r] + part
        for r in range(width):
            out_ref[start + r] = total[r].astype(out_ref.dtype)


def conv_call(flags, sums, amount, xs, affine, conv_w, out_dtype):
    x = xs[0]
    rows = x.shape[0] - 2
    outs, ins = conv_w.shape[2:]
    return pl.pallas_call(
        functools.partial(conv_kernel, len(xs), amount),
        in_specs=[
            pl.BlockSpec(memory_space=pltpu.SMEM),
            pl.BlockSpec(memory_space=pltpu.SMEM),
            *[pl.BlockSpec(memory_space=pltpu.VMEM)] * (len(xs) + 1),
            pl.BlockSpec(memory_space=pltpu.HBM),
        ],
        out_specs=pl.BlockSpec(memory_space=pltpu.VMEM),
        out_shape=jax.ShapeDtypeStruct((rows, outs, LANES), out_dtype),
        scratch_shapes=[
            pltpu.VMEM((3, outs, 3 * ins), jnp.bfloat16),
            pltpu.VMEM((3 * ins, rows * LANES), jnp.bfloat16),
            pltpu.SemaphoreType.DMA((3, 3)),
        ],
        compiler_params=pltpu.CompilerParams(vmem_limit_bytes=57 * MIB),
        cost_estimate=cost(9000),
        name="norm_conv",
    )(flags, sums, *xs, affine, conv_w)


def parity_matrix(channels):
    half = channels // 2
    to = lax.broadcasted_iota(jnp.int32, (channels, channels), 0)
    source = lax.broadcasted_iota(jnp.int32, (channels, channels), 1)
    wanted = jnp.where(to < half, 2 * to, 2 * (to - half) + 1)
    return (source == wanted).astype(jnp.bfloat16)


def split_kernel(own_ref, split_ref):
    rows, channels, _ = own_ref.shape
    half = channels // 2
    chosen = parity_matrix(channels)
    for r in range(rows):
        y = jnp.dot(chosen, own_ref[r], preferred_element_type=jnp.float32).astype(jnp.bfloat16)
        split_ref[0, r] = y[:half]
        split_ref[1, r] = y[half:]


def split_call(own):
    rows, channels, _ = own.shape
    return pl.pallas_call(
        split_kernel,
        in_specs=[pl.BlockSpec(memory_space=pltpu.VMEM)],
        out_specs=pl.BlockSpec(memory_space=pltpu.VMEM),
        out_shape=jax.ShapeDtypeStruct((2, rows, channels // 2, LANES), jnp.bfloat16),
        compiler_params=pltpu.CompilerParams(vmem_limit_bytes=VMEM_LIMIT),
        cost_estimate=cost(1000),
        name="parity_split",
    )(own)


def arrange_kernel(flip_ref, w_ref, out_ref):
    count, channels, _ = out_ref.shape
    chosen = parity_matrix(channels)
    for i in range(count):
        y = lax.dot_general(
            chosen,
            w_ref[:, i * channels : (i + 1) * channels],
            (((1,), (1,)), ((), ())),
            preferred_element_type=jnp.float32,
        )
        out_ref[jnp.where(flip_ref[0] == 1, count - 1 - i, i)] = y.astype(jnp.bfloat16)


def arrange_call(flip, w_out, count):
    features, channels = w_out.shape
    return pl.pallas_call(
        arrange_kernel,
        in_specs=[
            pl.BlockSpec(memory_space=pltpu.SMEM),
            pl.BlockSpec(memory_space=pltpu.VMEM),
        ],
        out_specs=pl.BlockSpec(memory_space=pltpu.VMEM),
        out_shape=jax.ShapeDtypeStruct((count, channels // count, features), jnp.bfloat16),
        compiler_params=pltpu.CompilerParams(vmem_limit_bytes=VMEM_LIMIT),
        cost_estimate=cost(2000),
        name="arrange",
    )(flip.astype(jnp.int32).reshape(1), w_out)


def project_kernel(parts, order_ref, *refs):
    part_refs = refs[:parts]
    affine_ref, w_hbm, q_ref, kv_ref, w_ref, normed_ref, sems = refs[parts:]
    rows, channels, _ = part_refs[0].shape
    total = parts * channels
    copies = [pltpu.make_async_copy(w_hbm.at[i], w_ref.at[i], sems.at[i]) for i in range(3)]
    for copy in copies:
        copy.start()
    for r in range(rows):
        x = [ref[r].astype(jnp.float32) for ref in part_refs]
        mean = sum(jnp.sum(a, axis=0, keepdims=True) for a in x) / total
        var = sum(jnp.sum(a * a, axis=0, keepdims=True) for a in x) / total - mean * mean
        inverse = lax.rsqrt(var + epsilon)
        for j in range(parts):
            at = pl.ds(pl.multiple_of(order_ref[j] * channels, LANES), channels)
            z = (x[j] - mean) * inverse * affine_ref[at, 0:1] + affine_ref[at, 1:2]
            normed_ref[r * LANES : (r + 1) * LANES, at] = z.astype(jnp.bfloat16).T
    for i in range(3):
        copies[i].wait()
        y = jnp.dot(normed_ref[...], w_ref[i], preferred_element_type=jnp.float32)
        y = y.astype(jnp.bfloat16)
        if i == 0:
            q_ref[...] = y * SCORE_SCALE
        else:
            kv_ref[i - 1] = y


def project_call(order, parts, affine, w):
    rows = parts[0].shape[0]
    positions = rows * LANES
    _, depth, features = w.shape
    vmem = pl.BlockSpec(memory_space=pltpu.VMEM)
    return pl.pallas_call(
        functools.partial(project_kernel, len(parts)),
        in_specs=[
            pl.BlockSpec(memory_space=pltpu.SMEM),
            *[vmem] * (len(parts) + 1),
            pl.BlockSpec(memory_space=pltpu.HBM),
        ],
        out_specs=(vmem, vmem),
        out_shape=(
            jax.ShapeDtypeStruct((positions, features), jnp.bfloat16),
            jax.ShapeDtypeStruct((2, positions, features), jnp.bfloat16),
        ),
        scratch_shapes=[
            pltpu.VMEM((3, depth, features), jnp.bfloat16),
            pltpu.VMEM((positions, depth), jnp.bfloat16),
            pltpu.SemaphoreType.DMA((3,)),
        ],
        compiler_params=pltpu.CompilerParams(vmem_limit_bytes=60 * MIB),
        cost_estimate=cost(6500),
        name="norm_project",
    )(order, *parts, affine, w)


def branch_kernel(parity_ref, resid_ref, *refs):
    total = resid_ref[0].astype(jnp.float32)
    for ref in refs[:-1]:
        total = total + ref[0].astype(jnp.float32)
    refs[-1][...] = total.astype(jnp.bfloat16)


def branch_call(parity, resid_split, terms):
    shape = resid_split.shape
    block = pl.BlockSpec((1,) + shape[1:], lambda i, parity: (parity[0], 0, 0, 0))
    return pl.pallas_call(
        branch_kernel,
        grid_spec=pltpu.PrefetchScalarGridSpec(
            num_scalar_prefetch=1,
            grid=(1,),
            in_specs=[block] * (1 + len(terms)),
            out_specs=pl.BlockSpec(shape[1:], lambda i, parity: (0, 0, 0)),
        ),
        out_shape=jax.ShapeDtypeStruct(shape[1:], jnp.bfloat16),
        compiler_params=pltpu.CompilerParams(vmem_limit_bytes=VMEM_LIMIT),
        cost_estimate=cost(1000),
        name="branch_out",
    )(parity.astype(jnp.int32).reshape(1), resid_split, *terms)


def attention_kernel(blocks, carried, final, *refs):
    q_ref = refs[0]
    kv_refs = refs[1 : 1 + 2 * blocks]
    at = 1 + 2 * blocks
    if carried:
        m_in, acc_in = refs[at : at + 2]
        at += 2
    if final:
        w_ref = refs[at]
        at += 1
        out_refs = refs[at:-1]
        joined_ref = refs[-1]
    else:
        m_out, acc_out = refs[at:]
    positions = q_ref.shape[0]
    tile = min(256, positions)
    starts = range(0, positions, tile)
    lanes = lambda array, low: (lax.broadcasted_iota(jnp.int32, array.shape, 1) < HD) == low

    def scores(item):
        start, head, block = item
        q = q_ref[start : start + tile, :]
        q = jnp.where(lanes(q, head == 0), q, jnp.zeros_like(q))
        return lax.dot_general(
            q,
            kv_refs[2 * block][0],
            (((1,), (1,)), ((), ())),
            preferred_element_type=jnp.float32,
        )

    items = [(start, head, block) for start in starts for block in range(blocks) for head in (0, 1)]
    state = {}
    upcoming = scores(items[0])
    for number, item in enumerate(items):
        s = upcoming
        if number + 1 < len(items):
            upcoming = scores(items[number + 1])
        start, head, block = item
        rows = slice(start, start + tile)
        if block == 0 and carried:
            peak, acc = m_in[0, head, rows, :], acc_in[0, head, rows, :]
        elif block == 0:
            peak = acc = None
        else:
            peak, acc = state[start, head]
        v = kv_refs[2 * block + 1][0]
        v = jnp.where(lanes(v, head == 0), v, jnp.ones_like(v))
        top = jnp.broadcast_to(jnp.max(s, axis=1, keepdims=True), (tile, LANES))
        new_peak = top if peak is None else jnp.maximum(peak, top)
        wide = jnp.concatenate([new_peak] * (s.shape[1] // LANES), axis=1)
        p = jnp.exp(s - wide).astype(jnp.bfloat16)
        term = jnp.dot(p, v, preferred_element_type=jnp.float32)
        acc = term if acc is None else acc * jnp.exp(peak - new_peak) + term
        state[start, head] = new_peak, acc
        if block < blocks - 1:
            continue
        if not final:
            m_out[0, head, rows, :] = new_peak
            acc_out[0, head, rows, :] = acc
        elif head == 1:
            parts = [state[start, h][1] for h in (0, 1)]
            parts = [a / pltpu.roll(a, HD, axis=1) for a in parts]
            pair = jnp.where(lanes(acc, True), parts[0], parts[1]).astype(jnp.bfloat16)
            joined_ref[pl.program_id(0), rows, :] = pair

    if final:
        tiles, _, _ = joined_ref.shape

        @pl.when(pl.program_id(0) == tiles - 1)
        def _():
            joined = jnp.concatenate([joined_ref[i] for i in range(tiles)], axis=1)
            for j in range(w_ref.shape[0]):
                y = lax.dot_general(
                    w_ref[j],
                    joined,
                    (((1,), (1,)), ((), ())),
                    preferred_element_type=jnp.float32,
                )
                out = out_refs[j] if len(out_refs) > 1 else out_refs[0].at[j]
                half = w_ref.shape[1] // 2
                for parity in range(2):
                    for r in range(positions // LANES):
                        out[parity, r] = y[
                            parity * half : (parity + 1) * half, r * LANES : (r + 1) * LANES
                        ].astype(out.dtype)


def attention_call(q, pairs, state, w=None, own_apart=False):
    positions, features = q.shape
    tiles = features // LANES
    final = w is not None
    carry = pl.BlockSpec((1, 2, positions, LANES), lambda i: (i, 0, 0, 0))
    carry_shape = jax.ShapeDtypeStruct((tiles, 2, positions, LANES), jnp.float32)
    operands = [q]
    specs = [pl.BlockSpec((positions, LANES), lambda i: (0, i))]
    for pair in pairs:
        for array, place in pair:
            operands.append(array)
            specs.append(
                pl.BlockSpec((1, positions, LANES), functools.partial(lambda p, i: (p, 0, i), place))
            )
    if state is not None:
        operands += list(state)
        specs += [carry, carry]
    scratch = []
    if final:
        operands.append(w)
        specs.append(pl.BlockSpec(w.shape, lambda i: (0, 0, 0)))
        shape = (2, positions // LANES, w.shape[1] // 2, LANES)
        if own_apart:
            out_shape = (
                jax.ShapeDtypeStruct(shape, jnp.bfloat16),
                jax.ShapeDtypeStruct(shape, jnp.float32),
            )
        else:
            out_shape = (jax.ShapeDtypeStruct((w.shape[0],) + shape, jnp.bfloat16),)
        out_specs = tuple(
            pl.BlockSpec(o.shape, functools.partial(lambda n, i: (0,) * n, len(o.shape)))
            for o in out_shape
        )
        scratch = [pltpu.VMEM((tiles, positions, LANES), jnp.bfloat16)]
    else:
        out_shape = (carry_shape, carry_shape)
        out_specs = (carry, carry)
    keys = positions * len(pairs)
    return pl.pallas_call(
        functools.partial(attention_kernel, len(pairs), state is not None, final),
        grid=(tiles,),
        in_specs=specs,
        out_specs=out_specs,
        out_shape=out_shape,
        scratch_shapes=scratch,
        compiler_params=pltpu.CompilerParams(vmem_limit_bytes=VMEM_LIMIT),
        cost_estimate=cost(1000 + 3200 * len(pairs)),
        name="attend",
    )(*operands)


def per_device(
    latent,
    stale_kv,
    timestep,
    w_time,
    gn_gain,
    gn_bias,
    conv_w,
    conv_b,
    ln_gain,
    ln_bias,
    w_qkv,
    w_out,
):
    latent_rows = latent[0]
    rows_count = lax.axis_size("rows")
    tp_count = lax.axis_size("tp")
    span_rows, local_channels, grid_width = latent_rows.shape
    positions = span_rows * grid_width
    group_width = D // GROUPS
    local_groups = local_channels // group_width
    my_block = lax.axis_index("rows")
    cfg = lax.axis_index("cfg")
    tp = lax.axis_index("tp")

    latent32 = latent_rows.astype(jnp.float32)
    values32 = latent32.reshape(span_rows, local_groups, group_width, grid_width)
    sums = jnp.stack(
        [jnp.sum(values32, axis=(0, 2, 3)), jnp.sum(values32 * values32, axis=(0, 2, 3))]
    )
    table = jnp.zeros((2, 2, GROUPS), jnp.float32)
    table = lax.dynamic_update_slice(table, sums[None], (cfg, 0, tp * local_groups))
    table = summed(table.reshape(-1), ("cfg", "rows", "tp"))

    up_pairs = [(i, i + 1) for i in range(rows_count - 1)]
    down_pairs = [(i + 1, i) for i in range(rows_count - 1)]
    before = lax.ppermute(latent_rows[span_rows - 1 :], "rows", up_pairs)
    after = lax.ppermute(latent_rows[:1], "rows", down_pairs)
    rimmed = jnp.concatenate([before, latent_rows, after], axis=0)

    x_mine, x_other = halves_of_inputs(rimmed)

    forward, backward = ring_pairs(rows_count)
    last = rows_count // 2
    pair = stale_kv[0].reshape(2, positions, -1)
    hops = [(pair, pair)]

    def next_hop(*after):
        ahead, behind = hops[-1]
        if len(hops) == last:
            ahead, behind = ahead[:1], behind[1:]
        if after:
            ahead, behind, *_ = lax.optimization_barrier((ahead, behind) + after)
        hops.append(
            (lax.ppermute(ahead, "rows", forward), lax.ppermute(behind, "rows", backward))
        )

    def blocks_of(hop):
        ahead, behind = hops[hop]
        if hop == last:
            return [((ahead, 0), (behind, 0))]
        return [((ahead, 0), (ahead, 1)), ((behind, 0), (behind, 1))]

    next_hop()

    vectors = gather_tp(jnp.stack([gn_gain, gn_bias, ln_gain, ln_bias]), 1).astype(jnp.float32)
    amount = span_rows * rows_count * grid_width * group_width
    half = D // 2
    gn_affine = lax.dynamic_slice_in_dim(vectors[:2], cfg * half, half, 1).T
    ln_affine = vectors[2:].T
    flags = jnp.stack([my_block > 0, my_block < rows_count - 1, tp == cfg]).astype(jnp.int32)
    place = cfg * (GROUPS // 2)
    flags_mine = jnp.append(flags, cfg * 2 * GROUPS + place)
    flags_other = jnp.append(flags, (1 - cfg) * 2 * GROUPS + place)

    local_features = w_qkv.shape[2]
    w_project = w_qkv.transpose(1, 0, 2)
    flip = jnp.logical_and(tp_count == 2, tp == 0)
    w_back = arrange_call(flip, w_out, tp_count)
    gn_affine, w_back = lax.optimization_barrier((gn_affine, w_back))

    flags_other = need(flags_other, hops[1])
    conv_sent = conv_call(flags_other, table, amount, x_other, gn_affine, conv_w, jnp.bfloat16)
    conv_received = swapped(conv_sent, "cfg")
    next_hop()
    conv_own = conv_call(flags_mine, table, amount, x_mine, gn_affine, conv_w, jnp.float32)

    half_width = TEMB // 2
    frequencies = jnp.exp(
        -math.log(10000.0) * jnp.arange(half_width, dtype=jnp.float32) / half_width
    )
    angles = timestep.astype(jnp.float32)[0] * frequencies
    embedding = jnp.concatenate([jnp.cos(angles), jnp.sin(angles)])
    time_bias = jnp.dot(
        jax.nn.silu(embedding)[None, :], w_time.astype(jnp.float32), precision=lax.Precision.HIGHEST
    )[0]
    bias = conv_b.astype(jnp.float32) + time_bias
    resid = (
        latent32 + (conv_own + conv_received.astype(jnp.float32) + bias[None, :, None])
    ).astype(jnp.bfloat16)

    if tp_count == 2:
        parts = [resid, need(swapped(resid, "tp"), hops[2])]
        order = jnp.stack([tp, 1 - tp]).astype(jnp.int32)
    else:
        parts = [lax.all_gather(resid, "tp", axis=1, tiled=True)]
        order = jnp.zeros((1,), jnp.int32)
    next_hop(resid)
    queries, fresh = project_call(order, parts, ln_affine, w_project)
    resid_split = split_call(resid)
    fresh_kv = fresh.reshape(1, 2, span_rows, grid_width, local_features)

    group = [((fresh, 0), (fresh, 1))] + blocks_of(1)
    state = None
    for hop in range(2, last + 1):
        state = attention_call(queries, group, state)
        while len(hops) <= last:
            next_hop(state[0])
        group = blocks_of(hop)
    if tp_count == 2:
        sent, kept_terms = attention_call(queries, group, state, w_back, True)
        terms = (kept_terms, swapped(sent, "tp"))
    else:
        (sent,) = attention_call(queries, group, state, w_back)
        terms = (lax.psum_scatter(sent, "tp", scatter_dimension=0),)

    other_branch = swapped(branch_call(1 - cfg, resid_split, terms), "cfg")
    kept = branch_call(cfg, resid_split, terms)
    is_cond = cfg == 0
    cond_out = jnp.where(is_cond, kept, other_branch).astype(jnp.float32)
    uncond_out = jnp.where(is_cond, other_branch, kept).astype(jnp.float32)
    guided = (uncond_out + guidance * (cond_out - uncond_out)).astype(jnp.bfloat16)
    return (guided[:, :, None, :], fresh_kv)


def solution(mesh):
    in_specs = (
        P("cfg", "rows", "tp", None),
        P("cfg", None, "rows", None, "tp"),
        P(),
        P(None, "tp"),
        P("tp"),
        P("tp"),
        P(None, None, "tp", "cfg"),
        P("tp"),
        P("tp"),
        P("tp"),
        P(None, None, "tp"),
        P("tp", None),
    )
    out_specs = (P("rows", "tp", "cfg", None), P("cfg", None, "rows", None, "tp"))
    return jax.shard_map(
        per_device, mesh=mesh, in_specs=in_specs, out_specs=out_specs, check_vma=False
    )
```

```python
import functools
import math

import jax
import jax.numpy as jnp
from jax import lax
from jax.experimental import pallas as pl
from jax.experimental.pallas import tpu as pltpu
from jax.sharding import PartitionSpec as P

D = 1280
HD = 64
GROUPS = 32
TEMB = 320
LANES = 128

epsilon = 1e-05
guidance = 5.0
SCORE_SCALE = 1.0 / math.sqrt(HD)
MIB = 1024 * 1024
VMEM_LIMIT = 32 * MIB
COST_SHARE = 0.02


def cost(work):
    return pl.CostEstimate(flops=int(work * 1e6 * COST_SHARE), bytes_accessed=1000, transcendentals=0)


def swapped(array, axis):
    return lax.ppermute(array, axis, [(i, i ^ 1) for i in range(lax.axis_size(axis))])


def ring_pairs(count):
    order = list(range(0, count, 2)) + list(range(count - 1, 0, -2))
    forward = [(order[i], order[(i + 1) % count]) for i in range(count)]
    backward = [(j, i) for i, j in forward]
    return forward, backward


def gather_tp(array, axis):
    if lax.axis_size("tp") != 2:
        return lax.all_gather(array, "tp", axis=axis, tiled=True)
    other = swapped(array, "tp")
    first = lax.axis_index("tp") == 0
    return jnp.concatenate(
        [jnp.where(first, array, other), jnp.where(first, other, array)], axis=axis
    )


def summed(array, axes):
    count = lax.axis_size(axes)
    spread = jnp.broadcast_to(array[None], (count,) + array.shape)
    return jnp.sum(lax.all_to_all(spread, axes, 0, 0, tiled=True), axis=0)


def need(array, others):
    return lax.optimization_barrier((array,) + tuple(others))[0] if others else array


def halves_of_inputs(own, others=()):
    cfg = lax.axis_index("cfg")
    if lax.axis_size("tp") != 2:
        full = lax.all_gather(own, "tp", axis=1, tiled=True)
        half = full.shape[1] // 2
        mine = lax.dynamic_slice_in_dim(full, cfg * half, half, 1)
        sent = lax.dynamic_slice_in_dim(full, (1 - cfg) * half, half, 1)
        return [mine], [swapped(sent, "cfg")]
    across = lax.ppermute(own, ("cfg", "tp"), [(1, 3), (2, 0)])
    pairs = [(0, 1), (3, 2)]
    own_side = lax.ppermute(own, ("cfg", "tp"), pairs)
    across_side = lax.ppermute(need(across, others), ("cfg", "tp"), pairs)
    return [own, own_side], [across, across_side]


def conv_kernel(choices, amount, flags_ref, sums_ref, *refs):
    x_refs = refs[:choices]
    edge_refs = refs[choices : 2 * choices]
    affine_ref, w_hbm, out_ref, w_ref, act_ref, sems = refs[2 * choices :]
    rows = out_ref.shape[0]
    ins = affine_ref.shape[0]
    copies = {}
    for b in (1, 0, 2):
        for a in range(3):
            copies[a, b] = pltpu.make_async_copy(
                w_hbm.at[a, b], w_ref.at[b, :, a * ins : (a + 1) * ins], sems.at[a, b]
            )
            copies[a, b].start()

    groups = ins // (D // GROUPS)
    base = flags_ref[3]

    def column(offset):
        return jnp.concatenate(
            [jnp.full((D // GROUPS, 1), sums_ref[base + offset + g], jnp.float32) for g in range(groups)],
            axis=0,
        )

    mean = column(0) / amount
    variance = column(GROUPS) / amount - mean * mean
    scale = lax.rsqrt(variance + epsilon) * affine_ref[:, 0:1]
    shift = affine_ref[:, 1:2]
    for r in range(rows + 2):
        if 0 < r <= rows:
            x = [ref[r - 1] for ref in x_refs]
        else:
            x = [ref[0 if r == 0 else 1] for ref in edge_refs]
        x = x[0] if choices == 1 else jnp.where(flags_ref[2] == 1, x[0], x[1])
        z = ((x.astype(jnp.float32) - mean) * scale + shift) * 0.5
        z = z + z * jnp.tanh(z)
        if r == 0:
            z = jnp.where(flags_ref[0] == 1, z, 0.0)
        if r == rows + 1:
            z = jnp.where(flags_ref[1] == 1, z, 0.0)
        z = z.astype(jnp.bfloat16)
        for a in range(3):
            if 0 <= r - a < rows:
                act_ref[a * ins : (a + 1) * ins, (r - a) * LANES : (r - a + 1) * LANES] = z

    width = min(2, rows)
    lane = lax.broadcasted_iota(jnp.int32, (out_ref.shape[1], LANES), 1)
    for start in range(0, rows, width):
        cols = slice(start * LANES, (start + width) * LANES)
        total = [0.0] * width
        for b in (1, 0, 2):
            if start == 0:
                for a in range(3):
                    copies[a, b].wait()
            y = jnp.dot(w_ref[b], act_ref[:, cols], preferred_element_type=jnp.float32)
            for r in range(width):
                part = y[:, r * LANES : (r + 1) * LANES]
                if b == 0:
                    part = jnp.where(lane == 0, 0.0, pltpu.roll(part, 1, axis=1))
                if b == 2:
                    part = jnp.where(lane == LANES - 1, 0.0, pltpu.roll(part, LANES - 1, axis=1))
                total[r] = total[r] + part
        for r in range(width):
            out_ref[start + r] = total[r].astype(out_ref.dtype)


def conv_call(flags, sums, amount, xs, edges, affine, conv_w, out_dtype):
    rows = xs[0].shape[0]
    outs, ins = conv_w.shape[2:]
    return pl.pallas_call(
        functools.partial(conv_kernel, len(xs), amount),
        in_specs=[
            pl.BlockSpec(memory_space=pltpu.SMEM),
            pl.BlockSpec(memory_space=pltpu.SMEM),
            *[pl.BlockSpec(memory_space=pltpu.VMEM)] * (2 * len(xs) + 1),
            pl.BlockSpec(memory_space=pltpu.HBM),
        ],
        out_specs=pl.BlockSpec(memory_space=pltpu.VMEM),
        out_shape=jax.ShapeDtypeStruct((rows, outs, LANES), out_dtype),
        scratch_shapes=[
            pltpu.VMEM((3, outs, 3 * ins), jnp.bfloat16),
            pltpu.VMEM((3 * ins, rows * LANES), jnp.bfloat16),
            pltpu.SemaphoreType.DMA((3, 3)),
        ],
        compiler_params=pltpu.CompilerParams(vmem_limit_bytes=57 * MIB),
        cost_estimate=cost(9000),
        name="norm_conv",
    )(flags, sums, *xs, *edges, affine, conv_w)


def parity_matrix(channels):
    half = channels // 2
    to = lax.broadcasted_iota(jnp.int32, (channels, channels), 0)
    source = lax.broadcasted_iota(jnp.int32, (channels, channels), 1)
    wanted = jnp.where(to < half, 2 * to, 2 * (to - half) + 1)
    return (source == wanted).astype(jnp.bfloat16)


def split_kernel(own_ref, split_ref):
    rows, channels, _ = own_ref.shape
    half = channels // 2
    chosen = parity_matrix(channels)
    for r in range(rows):
        y = jnp.dot(chosen, own_ref[r], preferred_element_type=jnp.float32).astype(jnp.bfloat16)
        split_ref[0, r] = y[:half]
        split_ref[1, r] = y[half:]


def split_call(own):
    rows, channels, _ = own.shape
    return pl.pallas_call(
        split_kernel,
        in_specs=[pl.BlockSpec(memory_space=pltpu.VMEM)],
        out_specs=pl.BlockSpec(memory_space=pltpu.VMEM),
        out_shape=jax.ShapeDtypeStruct((2, rows, channels // 2, LANES), jnp.bfloat16),
        compiler_params=pltpu.CompilerParams(vmem_limit_bytes=VMEM_LIMIT),
        cost_estimate=cost(1000),
        name="parity_split",
    )(own)


def arrange_kernel(flip_ref, w_ref, out_ref):
    count, channels, _ = out_ref.shape
    chosen = parity_matrix(channels)
    for i in range(count):
        y = lax.dot_general(
            chosen,
            w_ref[:, i * channels : (i + 1) * channels],
            (((1,), (1,)), ((), ())),
            preferred_element_type=jnp.float32,
        )
        out_ref[jnp.where(flip_ref[0] == 1, count - 1 - i, i)] = y.astype(jnp.bfloat16)


def arrange_call(flip, w_out, count):
    features, channels = w_out.shape
    return pl.pallas_call(
        arrange_kernel,
        in_specs=[
            pl.BlockSpec(memory_space=pltpu.SMEM),
            pl.BlockSpec(memory_space=pltpu.VMEM),
        ],
        out_specs=pl.BlockSpec(memory_space=pltpu.VMEM),
        out_shape=jax.ShapeDtypeStruct((count, channels // count, features), jnp.bfloat16),
        compiler_params=pltpu.CompilerParams(vmem_limit_bytes=VMEM_LIMIT),
        cost_estimate=cost(2000),
        name="arrange",
    )(flip.astype(jnp.int32).reshape(1), w_out)


def project_kernel(parts, order_ref, *refs):
    part_refs = refs[:parts]
    affine_ref, w_hbm, q_ref, kv_ref, w_ref, normed_ref, sems = refs[parts:]
    rows, channels, _ = part_refs[0].shape
    total = parts * channels
    copies = [pltpu.make_async_copy(w_hbm.at[i], w_ref.at[i], sems.at[i]) for i in range(3)]
    for copy in copies:
        copy.start()
    for r in range(rows):
        x = [ref[r].astype(jnp.float32) for ref in part_refs]
        mean = sum(jnp.sum(a, axis=0, keepdims=True) for a in x) / total
        var = sum(jnp.sum(a * a, axis=0, keepdims=True) for a in x) / total - mean * mean
        inverse = lax.rsqrt(var + epsilon)
        for j in range(parts):
            at = pl.ds(pl.multiple_of(order_ref[j] * channels, LANES), channels)
            z = (x[j] - mean) * inverse * affine_ref[at, 0:1] + affine_ref[at, 1:2]
            normed_ref[r * LANES : (r + 1) * LANES, at] = z.astype(jnp.bfloat16).T
    for i in range(3):
        copies[i].wait()
        y = jnp.dot(normed_ref[...], w_ref[i], preferred_element_type=jnp.float32)
        y = y.astype(jnp.bfloat16)
        if i == 0:
            q_ref[...] = y * SCORE_SCALE
        else:
            kv_ref[i - 1] = y


def project_call(order, parts, affine, w):
    rows = parts[0].shape[0]
    positions = rows * LANES
    _, depth, features = w.shape
    vmem = pl.BlockSpec(memory_space=pltpu.VMEM)
    return pl.pallas_call(
        functools.partial(project_kernel, len(parts)),
        in_specs=[
            pl.BlockSpec(memory_space=pltpu.SMEM),
            *[vmem] * (len(parts) + 1),
            pl.BlockSpec(memory_space=pltpu.HBM),
        ],
        out_specs=(vmem, vmem),
        out_shape=(
            jax.ShapeDtypeStruct((positions, features), jnp.bfloat16),
            jax.ShapeDtypeStruct((2, positions, features), jnp.bfloat16),
        ),
        scratch_shapes=[
            pltpu.VMEM((3, depth, features), jnp.bfloat16),
            pltpu.VMEM((positions, depth), jnp.bfloat16),
            pltpu.SemaphoreType.DMA((3,)),
        ],
        compiler_params=pltpu.CompilerParams(vmem_limit_bytes=55 * MIB),
        cost_estimate=cost(6500),
        name="norm_project",
    )(order, *parts, affine, w)


def branch_kernel(parity_ref, resid_ref, *refs):
    total = resid_ref[0].astype(jnp.float32)
    for ref in refs[:-1]:
        total = total + ref[0].astype(jnp.float32)
    refs[-1][...] = total.astype(jnp.bfloat16)


def branch_call(parity, resid_split, terms):
    shape = resid_split.shape
    block = pl.BlockSpec((1,) + shape[1:], lambda i, parity: (parity[0], 0, 0, 0))
    return pl.pallas_call(
        branch_kernel,
        grid_spec=pltpu.PrefetchScalarGridSpec(
            num_scalar_prefetch=1,
            grid=(1,),
            in_specs=[block] * (1 + len(terms)),
            out_specs=pl.BlockSpec(shape[1:], lambda i, parity: (0, 0, 0)),
        ),
        out_shape=jax.ShapeDtypeStruct(shape[1:], jnp.bfloat16),
        compiler_params=pltpu.CompilerParams(vmem_limit_bytes=VMEM_LIMIT),
        cost_estimate=cost(1000),
        name="branch_out",
    )(parity.astype(jnp.int32).reshape(1), resid_split, *terms)


def attention_kernel(blocks, carried, final, *refs):
    q_ref = refs[0]
    kv_refs = refs[1 : 1 + 2 * blocks]
    at = 1 + 2 * blocks
    if carried:
        m_in, acc_in = refs[at : at + 2]
        at += 2
    if final:
        w_ref = refs[at]
        at += 1
        out_refs = refs[at:-1]
        joined_ref = refs[-1]
    else:
        m_out, acc_out = refs[at:]
    positions = q_ref.shape[0]
    tile = min(256, positions)
    starts = range(0, positions, tile)
    lanes = lambda array, low: (lax.broadcasted_iota(jnp.int32, array.shape, 1) < HD) == low

    def scores(item):
        start, head, block = item
        q = q_ref[start : start + tile, :]
        q = jnp.where(lanes(q, head == 0), q, jnp.zeros_like(q))
        return lax.dot_general(
            q,
            kv_refs[2 * block][0],
            (((1,), (1,)), ((), ())),
            preferred_element_type=jnp.float32,
        )

    items = [(start, head, block) for start in starts for block in range(blocks) for head in (0, 1)]
    state = {}
    upcoming = scores(items[0])
    for number, item in enumerate(items):
        s = upcoming
        if number + 1 < len(items):
            upcoming = scores(items[number + 1])
        start, head, block = item
        rows = slice(start, start + tile)
        if block == 0 and carried:
            peak, acc = m_in[0, head, rows, :], acc_in[0, head, rows, :]
        elif block == 0:
            peak = acc = None
        else:
            peak, acc = state[start, head]
        v = kv_refs[2 * block + 1][0]
        v = jnp.where(lanes(v, head == 0), v, jnp.ones_like(v))
        top = jnp.broadcast_to(jnp.max(s, axis=1, keepdims=True), (tile, LANES))
        new_peak = top if peak is None else jnp.maximum(peak, top)
        wide = jnp.concatenate([new_peak] * (s.shape[1] // LANES), axis=1)
        p = jnp.exp(s - wide).astype(jnp.bfloat16)
        term = jnp.dot(p, v, preferred_element_type=jnp.float32)
        acc = term if acc is None else acc * jnp.exp(peak - new_peak) + term
        state[start, head] = new_peak, acc
        if block < blocks - 1:
            continue
        if not final:
            m_out[0, head, rows, :] = new_peak
            acc_out[0, head, rows, :] = acc
        elif head == 1:
            parts = [state[start, h][1] for h in (0, 1)]
            parts = [a / pltpu.roll(a, HD, axis=1) for a in parts]
            pair = jnp.where(lanes(acc, True), parts[0], parts[1]).astype(jnp.bfloat16)
            joined_ref[pl.program_id(0), rows, :] = pair

    if final:
        tiles, _, _ = joined_ref.shape

        @pl.when(pl.program_id(0) == tiles - 1)
        def _():
            joined = jnp.concatenate([joined_ref[i] for i in range(tiles)], axis=1)
            for j in range(w_ref.shape[0]):
                y = lax.dot_general(
                    w_ref[j],
                    joined,
                    (((1,), (1,)), ((), ())),
                    preferred_element_type=jnp.float32,
                )
                out = out_refs[j] if len(out_refs) > 1 else out_refs[0].at[j]
                half = w_ref.shape[1] // 2
                for parity in range(2):
                    for r in range(positions // LANES):
                        out[parity, r] = y[
                            parity * half : (parity + 1) * half, r * LANES : (r + 1) * LANES
                        ].astype(out.dtype)


def attention_call(q, pairs, state, w=None, own_apart=False):
    positions, features = q.shape
    tiles = features // LANES
    final = w is not None
    carry = pl.BlockSpec((1, 2, positions, LANES), lambda i: (i, 0, 0, 0))
    carry_shape = jax.ShapeDtypeStruct((tiles, 2, positions, LANES), jnp.float32)
    operands = [q]
    specs = [pl.BlockSpec((positions, LANES), lambda i: (0, i))]
    for pair in pairs:
        for array, place in pair:
            operands.append(array)
            specs.append(
                pl.BlockSpec((1, positions, LANES), functools.partial(lambda p, i: (p, 0, i), place))
            )
    if state is not None:
        operands += list(state)
        specs += [carry, carry]
    scratch = []
    if final:
        operands.append(w)
        specs.append(pl.BlockSpec(w.shape, lambda i: (0, 0, 0)))
        shape = (2, positions // LANES, w.shape[1] // 2, LANES)
        if own_apart:
            out_shape = (
                jax.ShapeDtypeStruct(shape, jnp.bfloat16),
                jax.ShapeDtypeStruct(shape, jnp.float32),
            )
        else:
            out_shape = (jax.ShapeDtypeStruct((w.shape[0],) + shape, jnp.bfloat16),)
        out_specs = tuple(
            pl.BlockSpec(o.shape, functools.partial(lambda n, i: (0,) * n, len(o.shape)))
            for o in out_shape
        )
        scratch = [pltpu.VMEM((tiles, positions, LANES), jnp.bfloat16)]
    else:
        out_shape = (carry_shape, carry_shape)
        out_specs = (carry, carry)
    keys = positions * len(pairs)
    return pl.pallas_call(
        functools.partial(attention_kernel, len(pairs), state is not None, final),
        grid=(tiles,),
        in_specs=specs,
        out_specs=out_specs,
        out_shape=out_shape,
        scratch_shapes=scratch,
        compiler_params=pltpu.CompilerParams(vmem_limit_bytes=VMEM_LIMIT),
        cost_estimate=cost(1000 + 3200 * len(pairs)),
        name="attend",
    )(*operands)


def per_device(
    latent,
    stale_kv,
    timestep,
    w_time,
    gn_gain,
    gn_bias,
    conv_w,
    conv_b,
    ln_gain,
    ln_bias,
    w_qkv,
    w_out,
):
    latent_rows = latent[0]
    rows_count = lax.axis_size("rows")
    tp_count = lax.axis_size("tp")
    span_rows, local_channels, grid_width = latent_rows.shape
    positions = span_rows * grid_width
    group_width = D // GROUPS
    local_groups = local_channels // group_width
    my_block = lax.axis_index("rows")
    cfg = lax.axis_index("cfg")
    tp = lax.axis_index("tp")

    latent32 = latent_rows.astype(jnp.float32)
    values32 = latent32.reshape(span_rows, local_groups, group_width, grid_width)
    sums = jnp.stack(
        [jnp.sum(values32, axis=(0, 2, 3)), jnp.sum(values32 * values32, axis=(0, 2, 3))]
    )
    table = jnp.zeros((2, 2, GROUPS), jnp.float32)
    table = lax.dynamic_update_slice(table, sums[None], (cfg, 0, tp * local_groups))
    table = summed(table.reshape(-1), ("cfg", "rows", "tp"))

    up_pairs = [(i, i + 1) for i in range(rows_count - 1)]
    down_pairs = [(i + 1, i) for i in range(rows_count - 1)]
    before = lax.ppermute(latent_rows[span_rows - 1 :], "rows", up_pairs)
    after = lax.ppermute(latent_rows[:1], "rows", down_pairs)
    x_mine, x_other = halves_of_inputs(latent_rows, (table,))
    edges_mine, edges_other = halves_of_inputs(jnp.concatenate([before, after], axis=0))

    forward, backward = ring_pairs(rows_count)
    last = rows_count // 2
    pair = stale_kv[0].reshape(2, positions, -1)
    hops = [(pair, pair)]

    def next_hop(*after):
        ahead, behind = hops[-1]
        if len(hops) == last:
            ahead, behind = ahead[:1], behind[1:]
        if after:
            ahead, behind, *_ = lax.optimization_barrier((ahead, behind) + after)
        hops.append(
            (lax.ppermute(ahead, "rows", forward), lax.ppermute(behind, "rows", backward))
        )

    def blocks_of(hop):
        ahead, behind = hops[hop]
        if hop == last:
            return [((ahead, 0), (behind, 0))]
        return [((ahead, 0), (ahead, 1)), ((behind, 0), (behind, 1))]

    next_hop(table)

    vectors = gather_tp(jnp.stack([gn_gain, gn_bias, ln_gain, ln_bias]), 1).astype(jnp.float32)
    amount = span_rows * rows_count * grid_width * group_width
    half = D // 2
    gn_affine = lax.dynamic_slice_in_dim(vectors[:2], cfg * half, half, 1).T
    ln_affine = vectors[2:].T
    flags = jnp.stack([my_block > 0, my_block < rows_count - 1, tp == cfg]).astype(jnp.int32)
    place = cfg * (GROUPS // 2)
    flags_mine = jnp.append(flags, cfg * 2 * GROUPS + place)
    flags_other = jnp.append(flags, (1 - cfg) * 2 * GROUPS + place)

    local_features = w_qkv.shape[2]
    w_project = w_qkv.transpose(1, 0, 2)
    flip = jnp.logical_and(tp_count == 2, tp == 0)
    w_back = arrange_call(flip, w_out, tp_count)
    gn_affine, w_back = lax.optimization_barrier((gn_affine, w_back))

    conv_sent = conv_call(flags_other, table, amount, x_other, edges_other, gn_affine, conv_w, jnp.bfloat16)
    conv_received = swapped(conv_sent, "cfg")
    next_hop(conv_sent)
    conv_own = conv_call(flags_mine, table, amount, x_mine, edges_mine, gn_affine, conv_w, jnp.float32)

    half_width = TEMB // 2
    frequencies = jnp.exp(
        -math.log(10000.0) * jnp.arange(half_width, dtype=jnp.float32) / half_width
    )
    angles = timestep.astype(jnp.float32)[0] * frequencies
    embedding = jnp.concatenate([jnp.cos(angles), jnp.sin(angles)])
    time_bias = jnp.dot(
        jax.nn.silu(embedding)[None, :], w_time.astype(jnp.float32), precision=lax.Precision.HIGHEST
    )[0]
    bias = conv_b.astype(jnp.float32) + time_bias
    resid = (
        latent32 + (conv_own + conv_received.astype(jnp.float32) + bias[None, :, None])
    ).astype(jnp.bfloat16)

    if tp_count == 2:
        parts = [resid, need(swapped(resid, "tp"), hops[2])]
        order = jnp.stack([tp, 1 - tp]).astype(jnp.int32)
    else:
        parts = [lax.all_gather(resid, "tp", axis=1, tiled=True)]
        order = jnp.zeros((1,), jnp.int32)
    next_hop(resid)
    queries, fresh = project_call(order, parts, ln_affine, w_project)
    resid_split = split_call(resid)
    fresh_kv = fresh.reshape(1, 2, span_rows, grid_width, local_features)

    group = [((fresh, 0), (fresh, 1))] + blocks_of(1)
    state = None
    for hop in range(2, last + 1):
        state = attention_call(queries, group, state)
        while len(hops) <= last:
            next_hop(state[0])
        group = blocks_of(hop)
    if tp_count == 2:
        sent, kept_terms = attention_call(queries, group, state, w_back, True)
        terms = (kept_terms, swapped(sent, "tp"))
    else:
        (sent,) = attention_call(queries, group, state, w_back)
        terms = (lax.psum_scatter(sent, "tp", scatter_dimension=0),)

    other_branch = swapped(branch_call(1 - cfg, resid_split, terms), "cfg")
    kept = branch_call(cfg, resid_split, terms)
    is_cond = cfg == 0
    cond_out = jnp.where(is_cond, kept, other_branch).astype(jnp.float32)
    uncond_out = jnp.where(is_cond, other_branch, kept).astype(jnp.float32)
    guided = (uncond_out + guidance * (cond_out - uncond_out)).astype(jnp.bfloat16)
    return (guided[:, :, None, :], fresh_kv)


def solution(mesh):
    in_specs = (
        P("cfg", "rows", "tp", None),
        P("cfg", None, "rows", None, "tp"),
        P(),
        P(None, "tp"),
        P("tp"),
        P("tp"),
        P(None, None, "tp", "cfg"),
        P("tp"),
        P("tp"),
        P("tp"),
        P(None, None, "tp"),
        P("tp", None),
    )
    out_specs = (P("rows", "tp", "cfg", None), P("cfg", None, "rows", None, "tp"))
    return jax.shard_map(
        per_device, mesh=mesh, in_specs=in_specs, out_specs=out_specs, check_vma=False
    )
```

```python
import functools
import math

import jax
import jax.numpy as jnp
from jax import lax
from jax.experimental import pallas as pl
from jax.experimental.pallas import tpu as pltpu
from jax.sharding import PartitionSpec as P

D = 1280
HD = 64
GROUPS = 32
TEMB = 320
LANES = 128

epsilon = 1e-05
guidance = 5.0
SCORE_SCALE = 1.0 / math.sqrt(HD)
MIB = 1024 * 1024
VMEM_LIMIT = 32 * MIB
COST_SHARE = 0.02


def cost(work):
    return pl.CostEstimate(flops=int(work * 1e6 * COST_SHARE), bytes_accessed=1000, transcendentals=0)


def swapped(array, axis):
    return lax.ppermute(array, axis, [(i, i ^ 1) for i in range(lax.axis_size(axis))])


def ring_pairs(count):
    order = list(range(0, count, 2)) + list(range(count - 1, 0, -2))
    forward = [(order[i], order[(i + 1) % count]) for i in range(count)]
    backward = [(j, i) for i, j in forward]
    return forward, backward


def summed(array, axes):
    count = lax.axis_size(axes)
    spread = jnp.broadcast_to(array[None], (count,) + array.shape)
    return jnp.sum(lax.all_to_all(spread, axes, 0, 0, tiled=True), axis=0)


def need(array, others):
    return lax.optimization_barrier((array,) + tuple(others))[0] if others else array


def halves_of_inputs(own, others=()):
    cfg = lax.axis_index("cfg")
    if lax.axis_size("tp") != 2:
        full = lax.all_gather(own, "tp", axis=1, tiled=True)
        half = full.shape[1] // 2
        mine = lax.dynamic_slice_in_dim(full, cfg * half, half, 1)
        sent = lax.dynamic_slice_in_dim(full, (1 - cfg) * half, half, 1)
        return [mine], [swapped(sent, "cfg")]
    across = lax.ppermute(own, ("cfg", "tp"), [(1, 3), (2, 0)])
    pairs = [(0, 1), (3, 2)]
    own_side = lax.ppermute(own, ("cfg", "tp"), pairs)
    across_side = lax.ppermute(need(across, others), ("cfg", "tp"), pairs)
    return [own, own_side], [across, across_side]


def conv_kernel(choices, amount, flags_ref, sums_ref, *refs):
    x_refs = refs[:choices]
    edge_refs = refs[choices : 2 * choices]
    affine_ref, w_hbm, out_ref, w_ref, act_ref, sems = refs[2 * choices :]
    rows = out_ref.shape[0]
    ins = affine_ref.shape[0]
    copies = {}
    for b in (1, 0, 2):
        for a in range(3):
            copies[a, b] = pltpu.make_async_copy(
                w_hbm.at[a, b], w_ref.at[b, :, a * ins : (a + 1) * ins], sems.at[a, b]
            )
            copies[a, b].start()

    groups = ins // (D // GROUPS)
    base = flags_ref[3]

    def column(offset):
        return jnp.concatenate(
            [jnp.full((D // GROUPS, 1), sums_ref[base + offset + g], jnp.float32) for g in range(groups)],
            axis=0,
        )

    mean = column(0) / amount
    variance = column(GROUPS) / amount - mean * mean
    scale = lax.rsqrt(variance + epsilon) * affine_ref[:, 0:1]
    shift = affine_ref[:, 1:2]
    for r in range(rows + 2):
        if 0 < r <= rows:
            x = [ref[r - 1] for ref in x_refs]
        else:
            x = [ref[0 if r == 0 else 1] for ref in edge_refs]
        x = x[0] if choices == 1 else jnp.where(flags_ref[2] == 1, x[0], x[1])
        z = ((x.astype(jnp.float32) - mean) * scale + shift) * 0.5
        z = z + z * jnp.tanh(z)
        if r == 0:
            z = jnp.where(flags_ref[0] == 1, z, 0.0)
        if r == rows + 1:
            z = jnp.where(flags_ref[1] == 1, z, 0.0)
        z = z.astype(jnp.bfloat16)
        for a in range(3):
            if 0 <= r - a < rows:
                act_ref[a * ins : (a + 1) * ins, (r - a) * LANES : (r - a + 1) * LANES] = z

    width = min(2, rows)
    lane = lax.broadcasted_iota(jnp.int32, (out_ref.shape[1], LANES), 1)
    for start in range(0, rows, width):
        cols = slice(start * LANES, (start + width) * LANES)
        total = [0.0] * width
        for b in (1, 0, 2):
            if start == 0:
                for a in range(3):
                    copies[a, b].wait()
            y = jnp.dot(w_ref[b], act_ref[:, cols], preferred_element_type=jnp.float32)
            for r in range(width):
                part = y[:, r * LANES : (r + 1) * LANES]
                if b == 0:
                    part = jnp.where(lane == 0, 0.0, pltpu.roll(part, 1, axis=1))
                if b == 2:
                    part = jnp.where(lane == LANES - 1, 0.0, pltpu.roll(part, LANES - 1, axis=1))
                total[r] = total[r] + part
        for r in range(width):
            out_ref[start + r] = total[r].astype(out_ref.dtype)


def conv_call(flags, sums, amount, xs, edges, affine, conv_w, out_dtype):
    rows = xs[0].shape[0]
    outs, ins = conv_w.shape[2:]
    return pl.pallas_call(
        functools.partial(conv_kernel, len(xs), amount),
        in_specs=[
            pl.BlockSpec(memory_space=pltpu.SMEM),
            pl.BlockSpec(memory_space=pltpu.SMEM),
            *[pl.BlockSpec(memory_space=pltpu.VMEM)] * (2 * len(xs) + 1),
            pl.BlockSpec(memory_space=pltpu.HBM),
        ],
        out_specs=pl.BlockSpec(memory_space=pltpu.VMEM),
        out_shape=jax.ShapeDtypeStruct((rows, outs, LANES), out_dtype),
        scratch_shapes=[
            pltpu.VMEM((3, outs, 3 * ins), jnp.bfloat16),
            pltpu.VMEM((3 * ins, rows * LANES), jnp.bfloat16),
            pltpu.SemaphoreType.DMA((3, 3)),
        ],
        compiler_params=pltpu.CompilerParams(vmem_limit_bytes=57 * MIB),
        cost_estimate=cost(9000),
        name="norm_conv",
    )(flags, sums, *xs, *edges, affine, conv_w)


def parity_matrix(channels):
    half = channels // 2
    to = lax.broadcasted_iota(jnp.int32, (channels, channels), 0)
    source = lax.broadcasted_iota(jnp.int32, (channels, channels), 1)
    wanted = jnp.where(to < half, 2 * to, 2 * (to - half) + 1)
    return (source == wanted).astype(jnp.bfloat16)


def split_kernel(own_ref, split_ref):
    rows, channels, _ = own_ref.shape
    half = channels // 2
    chosen = parity_matrix(channels)
    for r in range(rows):
        y = jnp.dot(chosen, own_ref[r], preferred_element_type=jnp.float32).astype(jnp.bfloat16)
        split_ref[0, r] = y[:half]
        split_ref[1, r] = y[half:]


def split_call(own):
    rows, channels, _ = own.shape
    return pl.pallas_call(
        split_kernel,
        in_specs=[pl.BlockSpec(memory_space=pltpu.VMEM)],
        out_specs=pl.BlockSpec(memory_space=pltpu.VMEM),
        out_shape=jax.ShapeDtypeStruct((2, rows, channels // 2, LANES), jnp.bfloat16),
        compiler_params=pltpu.CompilerParams(vmem_limit_bytes=VMEM_LIMIT),
        cost_estimate=cost(1000),
        name="parity_split",
    )(own)


def arrange_kernel(flip_ref, w_ref, out_ref):
    count, channels, _ = out_ref.shape
    chosen = parity_matrix(channels)
    for i in range(count):
        y = lax.dot_general(
            chosen,
            w_ref[:, i * channels : (i + 1) * channels],
            (((1,), (1,)), ((), ())),
            preferred_element_type=jnp.float32,
        )
        out_ref[jnp.where(flip_ref[0] == 1, count - 1 - i, i)] = y.astype(jnp.bfloat16)


def arrange_call(flip, w_out, count):
    features, channels = w_out.shape
    return pl.pallas_call(
        arrange_kernel,
        in_specs=[
            pl.BlockSpec(memory_space=pltpu.SMEM),
            pl.BlockSpec(memory_space=pltpu.VMEM),
        ],
        out_specs=pl.BlockSpec(memory_space=pltpu.VMEM),
        out_shape=jax.ShapeDtypeStruct((count, channels // count, features), jnp.bfloat16),
        compiler_params=pltpu.CompilerParams(vmem_limit_bytes=VMEM_LIMIT),
        cost_estimate=cost(2000),
        name="arrange",
    )(flip.astype(jnp.int32).reshape(1), w_out)


def project_kernel(parts, order_ref, *refs):
    part_refs = refs[:parts]
    affine_ref, w_hbm, q_ref, kv_ref, w_ref, normed_ref, sems = refs[parts:]
    rows, channels, _ = part_refs[0].shape
    total = parts * channels
    copies = [pltpu.make_async_copy(w_hbm.at[i], w_ref.at[i], sems.at[i]) for i in range(3)]
    for copy in copies:
        copy.start()
    for r in range(rows):
        x = [ref[r].astype(jnp.float32) for ref in part_refs]
        mean = sum(jnp.sum(a, axis=0, keepdims=True) for a in x) / total
        var = sum(jnp.sum(a * a, axis=0, keepdims=True) for a in x) / total - mean * mean
        inverse = lax.rsqrt(var + epsilon)
        for j in range(parts):
            at = pl.ds(pl.multiple_of(order_ref[j] * channels, LANES), channels)
            z = (x[j] - mean) * inverse * affine_ref[at, 0:1] + affine_ref[at, 1:2]
            normed_ref[r * LANES : (r + 1) * LANES, at] = z.astype(jnp.bfloat16).T
    for i in range(3):
        copies[i].wait()
        y = jnp.dot(normed_ref[...], w_ref[i], preferred_element_type=jnp.float32)
        y = y.astype(jnp.bfloat16)
        if i == 0:
            q_ref[...] = y * SCORE_SCALE
        else:
            kv_ref[i - 1] = y


def project_call(order, parts, affine, w):
    rows = parts[0].shape[0]
    positions = rows * LANES
    _, depth, features = w.shape
    vmem = pl.BlockSpec(memory_space=pltpu.VMEM)
    return pl.pallas_call(
        functools.partial(project_kernel, len(parts)),
        in_specs=[
            pl.BlockSpec(memory_space=pltpu.SMEM),
            *[vmem] * (len(parts) + 1),
            pl.BlockSpec(memory_space=pltpu.HBM),
        ],
        out_specs=(vmem, vmem),
        out_shape=(
            jax.ShapeDtypeStruct((positions, features), jnp.bfloat16),
            jax.ShapeDtypeStruct((2, positions, features), jnp.bfloat16),
        ),
        scratch_shapes=[
            pltpu.VMEM((3, depth, features), jnp.bfloat16),
            pltpu.VMEM((positions, depth), jnp.bfloat16),
            pltpu.SemaphoreType.DMA((3,)),
        ],
        compiler_params=pltpu.CompilerParams(vmem_limit_bytes=55 * MIB),
        cost_estimate=cost(6500),
        name="norm_project",
    )(order, *parts, affine, w)


def branch_kernel(parity_ref, resid_ref, *refs):
    total = resid_ref[0].astype(jnp.float32)
    for ref in refs[:-1]:
        total = total + ref[0].astype(jnp.float32)
    refs[-1][...] = total.astype(jnp.bfloat16)


def branch_call(parity, resid_split, terms):
    shape = resid_split.shape
    block = pl.BlockSpec((1,) + shape[1:], lambda i, parity: (parity[0], 0, 0, 0))
    return pl.pallas_call(
        branch_kernel,
        grid_spec=pltpu.PrefetchScalarGridSpec(
            num_scalar_prefetch=1,
            grid=(1,),
            in_specs=[block] * (1 + len(terms)),
            out_specs=pl.BlockSpec(shape[1:], lambda i, parity: (0, 0, 0)),
        ),
        out_shape=jax.ShapeDtypeStruct(shape[1:], jnp.bfloat16),
        compiler_params=pltpu.CompilerParams(vmem_limit_bytes=VMEM_LIMIT),
        cost_estimate=cost(1000),
        name="branch_out",
    )(parity.astype(jnp.int32).reshape(1), resid_split, *terms)


def attention_kernel(blocks, carried, final, *refs):
    q_ref = refs[0]
    kv_refs = refs[1 : 1 + 2 * blocks]
    at = 1 + 2 * blocks
    if carried:
        m_in, acc_in = refs[at : at + 2]
        at += 2
    if final:
        w_ref = refs[at]
        at += 1
        out_refs = refs[at:-1]
        joined_ref = refs[-1]
    else:
        m_out, acc_out = refs[at:]
    positions = q_ref.shape[0]
    tile = min(256, positions)
    starts = range(0, positions, tile)
    lanes = lambda array, low: (lax.broadcasted_iota(jnp.int32, array.shape, 1) < HD) == low

    def scores(item):
        start, head, block = item
        q = q_ref[start : start + tile, :]
        q = jnp.where(lanes(q, head == 0), q, jnp.zeros_like(q))
        return lax.dot_general(
            q,
            kv_refs[2 * block][0],
            (((1,), (1,)), ((), ())),
            preferred_element_type=jnp.float32,
        )

    items = [(start, head, block) for start in starts for block in range(blocks) for head in (0, 1)]
    state = {}
    upcoming = scores(items[0])
    for number, item in enumerate(items):
        s = upcoming
        if number + 1 < len(items):
            upcoming = scores(items[number + 1])
        start, head, block = item
        rows = slice(start, start + tile)
        if block == 0 and carried:
            peak, acc = m_in[0, head, rows, :], acc_in[0, head, rows, :]
        elif block == 0:
            peak = acc = None
        else:
            peak, acc = state[start, head]
        v = kv_refs[2 * block + 1][0]
        v = jnp.where(lanes(v, head == 0), v, jnp.ones_like(v))
        top = jnp.broadcast_to(jnp.max(s, axis=1, keepdims=True), (tile, LANES))
        new_peak = top if peak is None else jnp.maximum(peak, top)
        wide = jnp.concatenate([new_peak] * (s.shape[1] // LANES), axis=1)
        p = jnp.exp(s - wide).astype(jnp.bfloat16)
        term = jnp.dot(p, v, preferred_element_type=jnp.float32)
        acc = term if acc is None else acc * jnp.exp(peak - new_peak) + term
        state[start, head] = new_peak, acc
        if block < blocks - 1:
            continue
        if not final:
            m_out[0, head, rows, :] = new_peak
            acc_out[0, head, rows, :] = acc
        elif head == 1:
            parts = [state[start, h][1] for h in (0, 1)]
            parts = [a / pltpu.roll(a, HD, axis=1) for a in parts]
            pair = jnp.where(lanes(acc, True), parts[0], parts[1]).astype(jnp.bfloat16)
            joined_ref[pl.program_id(0), rows, :] = pair

    if final:
        tiles, _, _ = joined_ref.shape

        @pl.when(pl.program_id(0) == tiles - 1)
        def _():
            joined = jnp.concatenate([joined_ref[i] for i in range(tiles)], axis=1)
            for j in range(w_ref.shape[0]):
                y = lax.dot_general(
                    w_ref[j],
                    joined,
                    (((1,), (1,)), ((), ())),
                    preferred_element_type=jnp.float32,
                )
                out = out_refs[j] if len(out_refs) > 1 else out_refs[0].at[j]
                half = w_ref.shape[1] // 2
                for parity in range(2):
                    for r in range(positions // LANES):
                        out[parity, r] = y[
                            parity * half : (parity + 1) * half, r * LANES : (r + 1) * LANES
                        ].astype(out.dtype)


def attention_call(q, pairs, state, w=None, own_apart=False):
    positions, features = q.shape
    tiles = features // LANES
    final = w is not None
    carry = pl.BlockSpec((1, 2, positions, LANES), lambda i: (i, 0, 0, 0))
    carry_shape = jax.ShapeDtypeStruct((tiles, 2, positions, LANES), jnp.float32)
    operands = [q]
    specs = [pl.BlockSpec((positions, LANES), lambda i: (0, i))]
    for pair in pairs:
        for array, place in pair:
            operands.append(array)
            specs.append(
                pl.BlockSpec((1, positions, LANES), functools.partial(lambda p, i: (p, 0, i), place))
            )
    if state is not None:
        operands += list(state)
        specs += [carry, carry]
    scratch = []
    if final:
        operands.append(w)
        specs.append(pl.BlockSpec(w.shape, lambda i: (0, 0, 0)))
        shape = (2, positions // LANES, w.shape[1] // 2, LANES)
        if own_apart:
            out_shape = (
                jax.ShapeDtypeStruct(shape, jnp.bfloat16),
                jax.ShapeDtypeStruct(shape, jnp.float32),
            )
        else:
            out_shape = (jax.ShapeDtypeStruct((w.shape[0],) + shape, jnp.bfloat16),)
        out_specs = tuple(
            pl.BlockSpec(o.shape, functools.partial(lambda n, i: (0,) * n, len(o.shape)))
            for o in out_shape
        )
        scratch = [pltpu.VMEM((tiles, positions, LANES), jnp.bfloat16)]
    else:
        out_shape = (carry_shape, carry_shape)
        out_specs = (carry, carry)
    keys = positions * len(pairs)
    return pl.pallas_call(
        functools.partial(attention_kernel, len(pairs), state is not None, final),
        grid=(tiles,),
        in_specs=specs,
        out_specs=out_specs,
        out_shape=out_shape,
        scratch_shapes=scratch,
        compiler_params=pltpu.CompilerParams(vmem_limit_bytes=VMEM_LIMIT),
        cost_estimate=cost(1000 + 3200 * len(pairs)),
        name="attend",
    )(*operands)


def per_device(
    latent,
    stale_kv,
    timestep,
    w_time,
    gn_gain,
    gn_bias,
    conv_w,
    conv_b,
    ln_gain,
    ln_bias,
    w_qkv,
    w_out,
):
    latent_rows = latent[0]
    rows_count = lax.axis_size("rows")
    tp_count = lax.axis_size("tp")
    span_rows, local_channels, grid_width = latent_rows.shape
    positions = span_rows * grid_width
    group_width = D // GROUPS
    local_groups = local_channels // group_width
    my_block = lax.axis_index("rows")
    cfg = lax.axis_index("cfg")
    tp = lax.axis_index("tp")

    latent32 = latent_rows.astype(jnp.float32)
    values32 = latent32.reshape(span_rows, local_groups, group_width, grid_width)
    sums = jnp.stack(
        [jnp.sum(values32, axis=(0, 2, 3)), jnp.sum(values32 * values32, axis=(0, 2, 3))]
    )
    table = jnp.zeros((2, 2, GROUPS), jnp.float32)
    table = lax.dynamic_update_slice(table, sums[None], (cfg, 0, tp * local_groups))
    table = summed(table.reshape(-1), ("cfg", "rows", "tp"))

    up_pairs = [(i, i + 1) for i in range(rows_count - 1)]
    down_pairs = [(i + 1, i) for i in range(rows_count - 1)]
    before = lax.ppermute(latent_rows[span_rows - 1 :], "rows", up_pairs)
    after = lax.ppermute(latent_rows[:1], "rows", down_pairs)
    x_mine, x_other = halves_of_inputs(latent_rows)
    edges_mine, edges_other = halves_of_inputs(jnp.concatenate([before, after], axis=0))

    joined = jnp.concatenate([gn_gain, gn_bias, ln_gain, ln_bias])
    if tp_count == 2:
        other = swapped(joined, "tp").reshape(4, 1, -1)
        pieces = [joined.reshape(4, 1, -1), other]
        vectors = jnp.where(
            tp == 0, jnp.concatenate(pieces, axis=1), jnp.concatenate(pieces[::-1], axis=1)
        ).reshape(4, -1)
    else:
        vectors = lax.all_gather(joined.reshape(4, -1), "tp", axis=1, tiled=True)
    vectors = vectors.astype(jnp.float32)

    forward, backward = ring_pairs(rows_count)
    last = rows_count // 2
    pair = stale_kv[0].reshape(2, positions, -1)
    hops = [(pair, pair)]

    def next_hop(*after):
        ahead, behind = hops[-1]
        if len(hops) == last:
            ahead, behind = ahead[:1], behind[1:]
        if after:
            ahead, behind, *_ = lax.optimization_barrier((ahead, behind) + after)
        hops.append(
            (lax.ppermute(ahead, "rows", forward), lax.ppermute(behind, "rows", backward))
        )

    def blocks_of(hop):
        ahead, behind = hops[hop]
        if hop == last:
            return [((ahead, 0), (behind, 0))]
        return [((ahead, 0), (ahead, 1)), ((behind, 0), (behind, 1))]

    next_hop(vectors)

    amount = span_rows * rows_count * grid_width * group_width
    half = D // 2
    gn_affine = lax.dynamic_slice_in_dim(vectors[:2], cfg * half, half, 1).T
    ln_affine = vectors[2:].T
    flags = jnp.stack([my_block > 0, my_block < rows_count - 1, tp == cfg]).astype(jnp.int32)
    place = cfg * (GROUPS // 2)
    flags_mine = jnp.append(flags, cfg * 2 * GROUPS + place)
    flags_other = jnp.append(flags, (1 - cfg) * 2 * GROUPS + place)

    local_features = w_qkv.shape[2]
    w_project = w_qkv.transpose(1, 0, 2)
    flip = jnp.logical_and(tp_count == 2, tp == 0)
    w_back = arrange_call(flip, w_out, tp_count)
    order = jnp.stack([tp, 1 - tp]).astype(jnp.int32) if tp_count == 2 else jnp.zeros((1,), jnp.int32)
    gn_affine, ln_affine, order, w_back = lax.optimization_barrier(
        (gn_affine, ln_affine, order, w_back)
    )
    flags_other = need(flags_other, tuple(x_mine[1:] + edges_mine[1:]) + hops[1])
    next_hop()

    conv_sent = conv_call(flags_other, table, amount, x_other, edges_other, gn_affine, conv_w, jnp.bfloat16)
    conv_received = swapped(conv_sent, "cfg")
    conv_own = conv_call(flags_mine, table, amount, x_mine, edges_mine, gn_affine, conv_w, jnp.float32)

    half_width = TEMB // 2
    frequencies = jnp.exp(
        -math.log(10000.0) * jnp.arange(half_width, dtype=jnp.float32) / half_width
    )
    angles = timestep.astype(jnp.float32)[0] * frequencies
    embedding = jnp.concatenate([jnp.cos(angles), jnp.sin(angles)])
    time_bias = jnp.dot(
        jax.nn.silu(embedding)[None, :], w_time.astype(jnp.float32), precision=lax.Precision.HIGHEST
    )[0]
    bias = conv_b.astype(jnp.float32) + time_bias
    resid = (
        latent32 + (conv_own + conv_received.astype(jnp.float32) + bias[None, :, None])
    ).astype(jnp.bfloat16)

    if tp_count == 2:
        parts = [resid, need(swapped(resid, "tp"), hops[2])]
    else:
        parts = [lax.all_gather(resid, "tp", axis=1, tiled=True)]
    next_hop(resid)
    queries, fresh = project_call(order, parts, ln_affine, w_project)
    resid_split = split_call(resid)
    fresh_kv = fresh.reshape(1, 2, span_rows, grid_width, local_features)

    group = [((fresh, 0), (fresh, 1))] + blocks_of(1) + blocks_of(2)
    state = None
    for hop in range(3, last + 1):
        state = attention_call(queries, group, state)
        while len(hops) <= last:
            next_hop(state[0])
        group = blocks_of(hop)
    if tp_count == 2:
        sent, kept_terms = attention_call(queries, group, state, w_back, True)
        terms = (kept_terms, swapped(sent, "tp"))
    else:
        (sent,) = attention_call(queries, group, state, w_back)
        terms = (lax.psum_scatter(sent, "tp", scatter_dimension=0),)

    other_branch = swapped(branch_call(1 - cfg, resid_split, terms), "cfg")
    kept = branch_call(cfg, resid_split, terms)
    is_cond = cfg == 0
    cond_out = jnp.where(is_cond, kept, other_branch).astype(jnp.float32)
    uncond_out = jnp.where(is_cond, other_branch, kept).astype(jnp.float32)
    guided = (uncond_out + guidance * (cond_out - uncond_out)).astype(jnp.bfloat16)
    return (guided[:, :, None, :], fresh_kv)


def solution(mesh):
    in_specs = (
        P("cfg", "rows", "tp", None),
        P("cfg", None, "rows", None, "tp"),
        P(),
        P(None, "tp"),
        P("tp"),
        P("tp"),
        P(None, None, "tp", "cfg"),
        P("tp"),
        P("tp"),
        P("tp"),
        P(None, None, "tp"),
        P("tp", None),
    )
    out_specs = (P("rows", "tp", "cfg", None), P("cfg", None, "rows", None, "tp"))
    return jax.shard_map(
        per_device, mesh=mesh, in_specs=in_specs, out_specs=out_specs, check_vma=False
    )
```

```python
import functools
import math

import jax
import jax.numpy as jnp
from jax import lax
from jax.experimental import pallas as pl
from jax.experimental.pallas import tpu as pltpu
from jax.sharding import PartitionSpec as P

D = 1280
HD = 64
GROUPS = 32
TEMB = 320
LANES = 128

epsilon = 1e-05
guidance = 5.0
SCORE_SCALE = 1.0 / math.sqrt(HD)
MIB = 1024 * 1024
VMEM_LIMIT = 32 * MIB
COST_SHARE = 0.02


def cost(work):
    return pl.CostEstimate(flops=int(work * 1e6 * COST_SHARE), bytes_accessed=1000, transcendentals=0)


def swapped(array, axis):
    return lax.ppermute(array, axis, [(i, i ^ 1) for i in range(lax.axis_size(axis))])


def ring_pairs(count):
    order = list(range(0, count, 2)) + list(range(count - 1, 0, -2))
    forward = [(order[i], order[(i + 1) % count]) for i in range(count)]
    backward = [(j, i) for i, j in forward]
    return forward, backward


def summed(array, axes):
    count = lax.axis_size(axes)
    spread = jnp.broadcast_to(array[None], (count,) + array.shape)
    return jnp.sum(lax.all_to_all(spread, axes, 0, 0, tiled=True), axis=0)


def need(array, others):
    return lax.optimization_barrier((array,) + tuple(others))[0] if others else array


def halves_of_inputs(own, gain, bias):
    cfg = lax.axis_index("cfg")
    if lax.axis_size("tp") != 2:
        full = lax.all_gather(own, "tp", axis=1, tiled=True)
        half = full.shape[1] // 2
        vectors = lax.all_gather(jnp.stack([gain, bias]), "tp", axis=1, tiled=True)
        vectors = lax.dynamic_slice_in_dim(vectors, cfg * half, half, 1)
        rows = vector_rows(vectors[0], vectors[1])
        mine = lax.dynamic_slice_in_dim(full, cfg * half, half, 1)
        sent = lax.dynamic_slice_in_dim(full, (1 - cfg) * half, half, 1)
        return [attached(mine, rows)], [attached(swapped(sent, "cfg"), rows)]
    across = lax.ppermute(own, ("cfg", "tp"), [(1, 3), (2, 0)])
    pairs = [(0, 1), (3, 2)]
    own_side = lax.ppermute(own, ("cfg", "tp"), pairs)
    across_side = lax.ppermute(across, ("cfg", "tp"), pairs)
    return [own, own_side], [across, across_side]


def conv_kernel(choices, amount, flags_ref, sums_ref, *refs):
    x_refs = refs[:choices]
    w_hbm, out_ref, w_ref, act_ref, sems = refs[choices:]
    rows = out_ref.shape[0]
    ins = w_hbm.shape[3]
    copies = {}
    for b in (1, 0, 2):
        for a in range(3):
            copies[a, b] = pltpu.make_async_copy(
                w_hbm.at[a, b], w_ref.at[b, :, a * ins : (a + 1) * ins], sems.at[a, b]
            )
            copies[a, b].start()

    groups = ins // (D // GROUPS)
    base = flags_ref[3]

    def column(offset):
        return jnp.concatenate(
            [jnp.full((D // GROUPS, 1), sums_ref[base + offset + g], jnp.float32) for g in range(groups)],
            axis=0,
        )

    mean = column(0) / amount
    variance = column(GROUPS) / amount - mean * mean

    def chosen(r, at):
        x = [ref[r, at] for ref in x_refs]
        return x[0] if choices == 1 else jnp.where(flags_ref[2] == 1, x[0], x[1])

    gain, shift = columns_of(chosen(0, slice(ins, None)), ins)
    scale = lax.rsqrt(variance + epsilon) * gain
    for r in range(rows + 2):
        x = chosen(r, slice(0, ins))
        z = ((x.astype(jnp.float32) - mean) * scale + shift) * 0.5
        z = z + z * jnp.tanh(z)
        if r == 0:
            z = jnp.where(flags_ref[0] == 1, z, 0.0)
        if r == rows + 1:
            z = jnp.where(flags_ref[1] == 1, z, 0.0)
        z = z.astype(jnp.bfloat16)
        for a in range(3):
            if 0 <= r - a < rows:
                act_ref[a * ins : (a + 1) * ins, (r - a) * LANES : (r - a + 1) * LANES] = z

    width = min(2, rows)
    lane = lax.broadcasted_iota(jnp.int32, (out_ref.shape[1], LANES), 1)
    for start in range(0, rows, width):
        cols = slice(start * LANES, (start + width) * LANES)
        total = [0.0] * width
        for b in (1, 0, 2):
            if start == 0:
                for a in range(3):
                    copies[a, b].wait()
            y = jnp.dot(w_ref[b], act_ref[:, cols], preferred_element_type=jnp.float32)
            for r in range(width):
                part = y[:, r * LANES : (r + 1) * LANES]
                if b == 0:
                    part = jnp.where(lane == 0, 0.0, pltpu.roll(part, 1, axis=1))
                if b == 2:
                    part = jnp.where(lane == LANES - 1, 0.0, pltpu.roll(part, LANES - 1, axis=1))
                total[r] = total[r] + part
        for r in range(width):
            out_ref[start + r] = total[r].astype(out_ref.dtype)


def conv_call(flags, sums, amount, xs, conv_w, out_dtype):
    rows = xs[0].shape[0] - 2
    outs, ins = conv_w.shape[2:]
    return pl.pallas_call(
        functools.partial(conv_kernel, len(xs), amount),
        in_specs=[
            pl.BlockSpec(memory_space=pltpu.SMEM),
            pl.BlockSpec(memory_space=pltpu.SMEM),
            *[pl.BlockSpec(memory_space=pltpu.VMEM)] * len(xs),
            pl.BlockSpec(memory_space=pltpu.HBM),
        ],
        out_specs=pl.BlockSpec(memory_space=pltpu.VMEM),
        out_shape=jax.ShapeDtypeStruct((rows, outs, LANES), out_dtype),
        scratch_shapes=[
            pltpu.VMEM((3, outs, 3 * ins), jnp.bfloat16),
            pltpu.VMEM((3 * ins, rows * LANES), jnp.bfloat16),
            pltpu.SemaphoreType.DMA((3, 3)),
        ],
        compiler_params=pltpu.CompilerParams(vmem_limit_bytes=57 * MIB),
        cost_estimate=cost(9000),
        name="norm_conv",
    )(flags, sums, *xs, conv_w)


def extra_rows(channels):
    return -(-2 * channels // (16 * LANES)) * 16


def vector_rows(gain, bias):
    rows = jnp.concatenate([gain, bias]).reshape(-1, LANES)
    return jnp.pad(rows, ((0, extra_rows(gain.shape[0]) - rows.shape[0]), (0, 0)))


def columns_of(rows, channels):
    turned = rows.astype(jnp.float32).T
    count = channels // LANES
    column = lambda at: jnp.concatenate([turned[:, at + j : at + j + 1] for j in range(count)], axis=0)
    return column(0), column(count)


def attached(array, rows):
    shape = (array.shape[0],) + rows.shape
    return jnp.concatenate([array, jnp.broadcast_to(rows[None], shape)], axis=1)


def rim_kernel(before_ref, x_ref, after_ref, vector_ref, out_ref):
    rows, channels, _ = x_ref.shape
    out_ref[0, :channels] = before_ref[0]
    out_ref[rows + 1, :channels] = after_ref[0]
    for r in range(rows):
        out_ref[r + 1, :channels] = x_ref[r]
    for r in range(rows + 2):
        out_ref[r, channels:] = vector_ref[...]


def small_call(kernel, out_shape, name, *operands):
    vmem = pl.BlockSpec(memory_space=pltpu.VMEM)
    return pl.pallas_call(
        kernel,
        in_specs=[vmem] * len(operands),
        out_specs=vmem,
        out_shape=jax.ShapeDtypeStruct(out_shape, jnp.bfloat16),
        compiler_params=pltpu.CompilerParams(vmem_limit_bytes=VMEM_LIMIT),
        cost_estimate=cost(1000),
        name=name,
    )(*operands)


def resid_kernel(own_ref, received_ref, x_ref, bias_ref, vector_ref, out_ref):
    rows, channels, _ = x_ref.shape
    for r in range(rows):
        hidden = own_ref[r] + received_ref[r].astype(jnp.float32) + bias_ref[...]
        out_ref[r, :channels] = (x_ref[r].astype(jnp.float32) + hidden).astype(jnp.bfloat16)
        out_ref[r, channels:] = vector_ref[...]


def parity_matrix(channels):
    half = channels // 2
    to = lax.broadcasted_iota(jnp.int32, (channels, channels), 0)
    source = lax.broadcasted_iota(jnp.int32, (channels, channels), 1)
    wanted = jnp.where(to < half, 2 * to, 2 * (to - half) + 1)
    return (source == wanted).astype(jnp.bfloat16)


def split_kernel(own_ref, split_ref):
    _, rows, half, _ = split_ref.shape
    chosen = parity_matrix(2 * half)
    for r in range(rows):
        y = jnp.dot(chosen, own_ref[r, : 2 * half], preferred_element_type=jnp.float32)
        y = y.astype(jnp.bfloat16)
        split_ref[0, r] = y[:half]
        split_ref[1, r] = y[half:]


def arrange_kernel(flip_ref, w_ref, out_ref):
    count, channels, _ = out_ref.shape
    chosen = parity_matrix(channels)
    for i in range(count):
        y = lax.dot_general(
            chosen,
            w_ref[:, i * channels : (i + 1) * channels],
            (((1,), (1,)), ((), ())),
            preferred_element_type=jnp.float32,
        )
        out_ref[jnp.where(flip_ref[0] == 1, count - 1 - i, i)] = y.astype(jnp.bfloat16)


def arrange_call(flip, w_out, count):
    features, channels = w_out.shape
    return pl.pallas_call(
        arrange_kernel,
        in_specs=[
            pl.BlockSpec(memory_space=pltpu.SMEM),
            pl.BlockSpec(memory_space=pltpu.VMEM),
        ],
        out_specs=pl.BlockSpec(memory_space=pltpu.VMEM),
        out_shape=jax.ShapeDtypeStruct((count, channels // count, features), jnp.bfloat16),
        compiler_params=pltpu.CompilerParams(vmem_limit_bytes=VMEM_LIMIT),
        cost_estimate=cost(2000),
        name="arrange",
    )(flip.astype(jnp.int32).reshape(1), w_out)


def project_kernel(parts, order_ref, *refs):
    part_refs = refs[:parts]
    w_hbm, q_ref, kv_ref, w_ref, normed_ref, sems = refs[parts:]
    rows = part_refs[0].shape[0]
    channels = w_hbm.shape[1] // parts
    total = parts * channels
    copies = [pltpu.make_async_copy(w_hbm.at[i], w_ref.at[i], sems.at[i]) for i in range(3)]
    for copy in copies:
        copy.start()
    affine = [columns_of(ref[0, channels:], channels) for ref in part_refs]
    for r in range(rows):
        x = [ref[r, :channels].astype(jnp.float32) for ref in part_refs]
        mean = sum(jnp.sum(a, axis=0, keepdims=True) for a in x) / total
        var = sum(jnp.sum(a * a, axis=0, keepdims=True) for a in x) / total - mean * mean
        inverse = lax.rsqrt(var + epsilon)
        for j in range(parts):
            at = pl.ds(pl.multiple_of(order_ref[j] * channels, LANES), channels)
            z = (x[j] - mean) * inverse * affine[j][0] + affine[j][1]
            normed_ref[r * LANES : (r + 1) * LANES, at] = z.astype(jnp.bfloat16).T
    for i in range(3):
        copies[i].wait()
        y = jnp.dot(normed_ref[...], w_ref[i], preferred_element_type=jnp.float32)
        y = y.astype(jnp.bfloat16)
        if i == 0:
            q_ref[...] = y * SCORE_SCALE
        else:
            kv_ref[i - 1] = y


def project_call(order, parts, w):
    rows = parts[0].shape[0]
    positions = rows * LANES
    _, depth, features = w.shape
    vmem = pl.BlockSpec(memory_space=pltpu.VMEM)
    return pl.pallas_call(
        functools.partial(project_kernel, len(parts)),
        in_specs=[
            pl.BlockSpec(memory_space=pltpu.SMEM),
            *[vmem] * len(parts),
            pl.BlockSpec(memory_space=pltpu.HBM),
        ],
        out_specs=(vmem, vmem),
        out_shape=(
            jax.ShapeDtypeStruct((positions, features), jnp.bfloat16),
            jax.ShapeDtypeStruct((2, positions, features), jnp.bfloat16),
        ),
        scratch_shapes=[
            pltpu.VMEM((3, depth, features), jnp.bfloat16),
            pltpu.VMEM((positions, depth), jnp.bfloat16),
            pltpu.SemaphoreType.DMA((3,)),
        ],
        compiler_params=pltpu.CompilerParams(vmem_limit_bytes=55 * MIB),
        cost_estimate=cost(6500),
        name="norm_project",
    )(order, *parts, w)


def branch_kernel(parity_ref, resid_ref, *refs):
    total = resid_ref[0].astype(jnp.float32)
    for ref in refs[:-1]:
        total = total + ref[0].astype(jnp.float32)
    refs[-1][...] = total.astype(jnp.bfloat16)


def branch_call(parity, resid_split, terms):
    shape = resid_split.shape
    block = pl.BlockSpec((1,) + shape[1:], lambda i, parity: (parity[0], 0, 0, 0))
    return pl.pallas_call(
        branch_kernel,
        grid_spec=pltpu.PrefetchScalarGridSpec(
            num_scalar_prefetch=1,
            grid=(1,),
            in_specs=[block] * (1 + len(terms)),
            out_specs=pl.BlockSpec(shape[1:], lambda i, parity: (0, 0, 0)),
        ),
        out_shape=jax.ShapeDtypeStruct(shape[1:], jnp.bfloat16),
        compiler_params=pltpu.CompilerParams(vmem_limit_bytes=VMEM_LIMIT),
        cost_estimate=cost(1000),
        name="branch_out",
    )(parity.astype(jnp.int32).reshape(1), resid_split, *terms)


def attention_kernel(blocks, carried, final, *refs):
    q_ref = refs[0]
    kv_refs = refs[1 : 1 + 2 * blocks]
    at = 1 + 2 * blocks
    if carried:
        m_in, acc_in = refs[at : at + 2]
        at += 2
    if final:
        w_ref = refs[at]
        at += 1
        out_refs = refs[at:-1]
        joined_ref = refs[-1]
    else:
        m_out, acc_out = refs[at:]
    positions = q_ref.shape[0]
    tile = min(256, positions)
    starts = range(0, positions, tile)
    lanes = lambda array, low: (lax.broadcasted_iota(jnp.int32, array.shape, 1) < HD) == low

    def scores(item):
        start, head, block = item
        q = q_ref[start : start + tile, :]
        q = jnp.where(lanes(q, head == 0), q, jnp.zeros_like(q))
        return lax.dot_general(
            q,
            kv_refs[2 * block][0],
            (((1,), (1,)), ((), ())),
            preferred_element_type=jnp.float32,
        )

    items = [(start, head, block) for start in starts for block in range(blocks) for head in (0, 1)]
    state = {}
    upcoming = scores(items[0])
    for number, item in enumerate(items):
        s = upcoming
        if number + 1 < len(items):
            upcoming = scores(items[number + 1])
        start, head, block = item
        rows = slice(start, start + tile)
        if block == 0 and carried:
            peak, acc = m_in[0, head, rows, :], acc_in[0, head, rows, :]
        elif block == 0:
            peak = acc = None
        else:
            peak, acc = state[start, head]
        v = kv_refs[2 * block + 1][0]
        v = jnp.where(lanes(v, head == 0), v, jnp.ones_like(v))
        top = jnp.broadcast_to(jnp.max(s, axis=1, keepdims=True), (tile, LANES))
        new_peak = top if peak is None else jnp.maximum(peak, top)
        wide = jnp.concatenate([new_peak] * (s.shape[1] // LANES), axis=1)
        p = jnp.exp(s - wide).astype(jnp.bfloat16)
        term = jnp.dot(p, v, preferred_element_type=jnp.float32)
        acc = term if acc is None else acc * jnp.exp(peak - new_peak) + term
        state[start, head] = new_peak, acc
        if block < blocks - 1:
            continue
        if not final:
            m_out[0, head, rows, :] = new_peak
            acc_out[0, head, rows, :] = acc
        elif head == 1:
            parts = [state[start, h][1] for h in (0, 1)]
            parts = [a / pltpu.roll(a, HD, axis=1) for a in parts]
            pair = jnp.where(lanes(acc, True), parts[0], parts[1]).astype(jnp.bfloat16)
            joined_ref[pl.program_id(0), rows, :] = pair

    if final:
        tiles, _, _ = joined_ref.shape

        @pl.when(pl.program_id(0) == tiles - 1)
        def _():
            joined = jnp.concatenate([joined_ref[i] for i in range(tiles)], axis=1)
            for j in range(w_ref.shape[0]):
                y = lax.dot_general(
                    w_ref[j],
                    joined,
                    (((1,), (1,)), ((), ())),
                    preferred_element_type=jnp.float32,
                )
                out = out_refs[j] if len(out_refs) > 1 else out_refs[0].at[j]
                half = w_ref.shape[1] // 2
                for parity in range(2):
                    for r in range(positions // LANES):
                        out[parity, r] = y[
                            parity * half : (parity + 1) * half, r * LANES : (r + 1) * LANES
                        ].astype(out.dtype)


def attention_call(q, pairs, state, w=None, own_apart=False):
    positions, features = q.shape
    tiles = features // LANES
    final = w is not None
    carry = pl.BlockSpec((1, 2, positions, LANES), lambda i: (i, 0, 0, 0))
    carry_shape = jax.ShapeDtypeStruct((tiles, 2, positions, LANES), jnp.float32)
    operands = [q]
    specs = [pl.BlockSpec((positions, LANES), lambda i: (0, i))]
    for pair in pairs:
        for array, place in pair:
            operands.append(array)
            specs.append(
                pl.BlockSpec((1, positions, LANES), functools.partial(lambda p, i: (p, 0, i), place))
            )
    if state is not None:
        operands += list(state)
        specs += [carry, carry]
    scratch = []
    if final:
        operands.append(w)
        specs.append(pl.BlockSpec(w.shape, lambda i: (0, 0, 0)))
        shape = (2, positions // LANES, w.shape[1] // 2, LANES)
        if own_apart:
            out_shape = (
                jax.ShapeDtypeStruct(shape, jnp.bfloat16),
                jax.ShapeDtypeStruct(shape, jnp.float32),
            )
        else:
            out_shape = (jax.ShapeDtypeStruct((w.shape[0],) + shape, jnp.bfloat16),)
        out_specs = tuple(
            pl.BlockSpec(o.shape, functools.partial(lambda n, i: (0,) * n, len(o.shape)))
            for o in out_shape
        )
        scratch = [pltpu.VMEM((tiles, positions, LANES), jnp.bfloat16)]
    else:
        out_shape = (carry_shape, carry_shape)
        out_specs = (carry, carry)
    keys = positions * len(pairs)
    return pl.pallas_call(
        functools.partial(attention_kernel, len(pairs), state is not None, final),
        grid=(tiles,),
        in_specs=specs,
        out_specs=out_specs,
        out_shape=out_shape,
        scratch_shapes=scratch,
        compiler_params=pltpu.CompilerParams(vmem_limit_bytes=VMEM_LIMIT),
        cost_estimate=cost(1000 + 3200 * len(pairs)),
        name="attend",
    )(*operands)


def per_device(
    latent,
    stale_kv,
    timestep,
    w_time,
    gn_gain,
    gn_bias,
    conv_w,
    conv_b,
    ln_gain,
    ln_bias,
    w_qkv,
    w_out,
):
    latent_rows = latent[0]
    rows_count = lax.axis_size("rows")
    tp_count = lax.axis_size("tp")
    span_rows, local_channels, grid_width = latent_rows.shape
    positions = span_rows * grid_width
    group_width = D // GROUPS
    local_groups = local_channels // group_width
    my_block = lax.axis_index("rows")
    cfg = lax.axis_index("cfg")
    tp = lax.axis_index("tp")

    latent32 = latent_rows.astype(jnp.float32)
    values32 = latent32.reshape(span_rows, local_groups, group_width, grid_width)
    sums = jnp.stack(
        [jnp.sum(values32, axis=(0, 2, 3)), jnp.sum(values32 * values32, axis=(0, 2, 3))]
    )
    table = jnp.zeros((2, 2, GROUPS), jnp.float32)
    table = lax.dynamic_update_slice(table, sums[None], (cfg, 0, tp * local_groups))
    table = summed(table.reshape(-1), ("cfg", "rows", "tp"))

    up_pairs = [(i, i + 1) for i in range(rows_count - 1)]
    down_pairs = [(i + 1, i) for i in range(rows_count - 1)]
    before = lax.ppermute(latent_rows[span_rows - 1 :], "rows", up_pairs)
    after = lax.ppermute(latent_rows[:1], "rows", down_pairs)
    if tp_count == 2:
        shape = (span_rows + 2, local_channels + extra_rows(local_channels), grid_width)
        rimmed = small_call(
            rim_kernel, shape, "rim", before, latent_rows, after, vector_rows(gn_gain, gn_bias)
        )
        rimmed = need(rimmed, (table,))
    else:
        rimmed = jnp.concatenate([before, latent_rows, after], axis=0)
    x_mine, x_other = halves_of_inputs(rimmed, gn_gain, gn_bias)

    forward, backward = ring_pairs(rows_count)
    last = rows_count // 2
    pair = stale_kv[0].reshape(2, positions, -1)
    hops = [(pair, pair)]

    def next_hop(*after):
        ahead, behind = hops[-1]
        if len(hops) == last:
            ahead, behind = ahead[:1], behind[1:]
        if after:
            ahead, behind, *_ = lax.optimization_barrier((ahead, behind) + after)
        hops.append(
            (lax.ppermute(ahead, "rows", forward), lax.ppermute(behind, "rows", backward))
        )

    def blocks_of(hop):
        ahead, behind = hops[hop]
        if hop == last:
            return [((ahead, 0), (behind, 0))]
        return [((ahead, 0), (ahead, 1)), ((behind, 0), (behind, 1))]

    next_hop(table)

    amount = span_rows * rows_count * grid_width * group_width
    flags = jnp.stack([my_block > 0, my_block < rows_count - 1, tp == cfg]).astype(jnp.int32)
    place = cfg * (GROUPS // 2)
    flags_mine = jnp.append(flags, cfg * 2 * GROUPS + place)
    flags_other = jnp.append(flags, (1 - cfg) * 2 * GROUPS + place)

    local_features = w_qkv.shape[2]
    w_project = w_qkv.transpose(1, 0, 2)
    flip = jnp.logical_and(tp_count == 2, tp == 0)
    w_back = arrange_call(flip, w_out, tp_count)
    order = jnp.stack([tp, 1 - tp]).astype(jnp.int32) if tp_count == 2 else jnp.zeros((1,), jnp.int32)
    flags_other, order, w_back, *_ = lax.optimization_barrier(
        (flags_other, order, w_back) + tuple(x_mine[1:])
    )

    conv_sent = conv_call(flags_other, table, amount, x_other, conv_w, jnp.bfloat16)
    conv_received = swapped(conv_sent, "cfg")
    next_hop(conv_sent)
    conv_own = conv_call(flags_mine, table, amount, x_mine, conv_w, jnp.float32)

    half_width = TEMB // 2
    frequencies = jnp.exp(
        -math.log(10000.0) * jnp.arange(half_width, dtype=jnp.float32) / half_width
    )
    angles = timestep.astype(jnp.float32)[0] * frequencies
    embedding = jnp.concatenate([jnp.cos(angles), jnp.sin(angles)])
    time_bias = jnp.dot(
        jax.nn.silu(embedding)[None, :], w_time.astype(jnp.float32), precision=lax.Precision.HIGHEST
    )[0]
    bias = conv_b.astype(jnp.float32) + time_bias
    wide = tp_count == 2
    rows = vector_rows(ln_gain, ln_bias) if wide else jnp.zeros((16, LANES), jnp.bfloat16)
    resid = small_call(
        resid_kernel,
        (span_rows, local_channels + rows.shape[0], grid_width),
        "residual",
        conv_own,
        conv_received,
        latent_rows,
        bias[:, None],
        rows,
    )
    if tp_count == 2:
        parts = [resid, need(swapped(resid, "tp"), hops[2])]
    else:
        full = lax.all_gather(resid[:, :local_channels], "tp", axis=1, tiled=True)
        vectors = lax.all_gather(jnp.stack([ln_gain, ln_bias]), "tp", axis=1, tiled=True)
        parts = [attached(full, vector_rows(vectors[0], vectors[1]))]
    next_hop(resid)
    queries, fresh = project_call(order, parts, w_project)
    resid_split = small_call(
        split_kernel, (2, span_rows, local_channels // 2, grid_width), "parity_split", resid
    )
    fresh_kv = fresh.reshape(1, 2, span_rows, grid_width, local_features)

    group = [((fresh, 0), (fresh, 1))] + blocks_of(1) + blocks_of(2)
    state = None
    for hop in range(3, last + 1):
        state = attention_call(queries, group, state)
        while len(hops) <= last:
            next_hop(state[0])
        group = blocks_of(hop)
    if tp_count == 2:
        sent, kept_terms = attention_call(queries, group, state, w_back, True)
        terms = (kept_terms, swapped(sent, "tp"))
    else:
        (sent,) = attention_call(queries, group, state, w_back)
        terms = (lax.psum_scatter(sent, "tp", scatter_dimension=0),)

    other_branch = swapped(branch_call(1 - cfg, resid_split, terms), "cfg")
    kept = branch_call(cfg, resid_split, terms)
    is_cond = cfg == 0
    cond_out = jnp.where(is_cond, kept, other_branch).astype(jnp.float32)
    uncond_out = jnp.where(is_cond, other_branch, kept).astype(jnp.float32)
    guided = (uncond_out + guidance * (cond_out - uncond_out)).astype(jnp.bfloat16)
    return (guided[:, :, None, :], fresh_kv)


def solution(mesh):
    in_specs = (
        P("cfg", "rows", "tp", None),
        P("cfg", None, "rows", None, "tp"),
        P(),
        P(None, "tp"),
        P("tp"),
        P("tp"),
        P(None, None, "tp", "cfg"),
        P("tp"),
        P("tp"),
        P("tp"),
        P(None, None, "tp"),
        P("tp", None),
    )
    out_specs = (P("rows", "tp", "cfg", None), P("cfg", None, "rows", None, "tp"))
    return jax.shard_map(
        per_device, mesh=mesh, in_specs=in_specs, out_specs=out_specs, check_vma=False
    )
```

```python
import functools
import math

import jax
import jax.numpy as jnp
from jax import lax
from jax.experimental import pallas as pl
from jax.experimental.pallas import tpu as pltpu
from jax.sharding import PartitionSpec as P

D = 1280
HD = 64
GROUPS = 32
TEMB = 320
LANES = 128

epsilon = 1e-05
guidance = 5.0
SCORE_SCALE = 1.0 / math.sqrt(HD)
MIB = 1024 * 1024
VMEM_LIMIT = 32 * MIB
COST_SHARE = 0.02


def cost(work):
    return pl.CostEstimate(flops=int(work * 1e6 * COST_SHARE), bytes_accessed=1000, transcendentals=0)


def swapped(array, axis):
    return lax.ppermute(array, axis, [(i, i ^ 1) for i in range(lax.axis_size(axis))])


def ring_pairs(count):
    order = list(range(0, count, 2)) + list(range(count - 1, 0, -2))
    forward = [(order[i], order[(i + 1) % count]) for i in range(count)]
    backward = [(j, i) for i, j in forward]
    return forward, backward


def summed(array, axes):
    count = lax.axis_size(axes)
    spread = jnp.broadcast_to(array[None], (count,) + array.shape)
    return jnp.sum(lax.all_to_all(spread, axes, 0, 0, tiled=True), axis=0)


def need(array, others):
    return lax.optimization_barrier((array,) + tuple(others))[0] if others else array


def halves_of_inputs(own):
    cfg = lax.axis_index("cfg")
    if lax.axis_size("tp") != 2:
        full = lax.all_gather(own, "tp", axis=1, tiled=True)
        half = full.shape[1] // 2
        mine = lax.dynamic_slice_in_dim(full, cfg * half, half, 1)
        sent = lax.dynamic_slice_in_dim(full, (1 - cfg) * half, half, 1)
        return [mine], [swapped(sent, "cfg")]
    across = lax.ppermute(own, ("cfg", "tp"), [(1, 3), (2, 0)])
    pairs = [(0, 1), (3, 2)]
    own_side = lax.ppermute(own, ("cfg", "tp"), pairs)
    across_side = lax.ppermute(across, ("cfg", "tp"), pairs)
    return [own, own_side], [across, across_side]


def conv_kernel(choices, flags_ref, *refs):
    x_refs = refs[:choices]
    w_hbm, out_ref, w_ref, act_ref, sems = refs[choices:]
    rows = out_ref.shape[0]
    ins = w_hbm.shape[3]
    copies = {}
    for b in (1, 0, 2):
        for a in range(3):
            copies[a, b] = pltpu.make_async_copy(
                w_hbm.at[a, b], w_ref.at[b, :, a * ins : (a + 1) * ins], sems.at[a, b]
            )
            copies[a, b].start()
    for r in range(rows + 2):
        x = [ref[r] for ref in x_refs]
        x = x[0] if choices == 1 else jnp.where(flags_ref[2] == 1, x[0], x[1])
        for a in range(3):
            if 0 <= r - a < rows:
                act_ref[a * ins : (a + 1) * ins, (r - a) * LANES : (r - a + 1) * LANES] = x

    width = min(2, rows)
    lane = lax.broadcasted_iota(jnp.int32, (out_ref.shape[1], LANES), 1)
    for start in range(0, rows, width):
        cols = slice(start * LANES, (start + width) * LANES)
        total = [0.0] * width
        for b in (1, 0, 2):
            if start == 0:
                for a in range(3):
                    copies[a, b].wait()
            y = jnp.dot(w_ref[b], act_ref[:, cols], preferred_element_type=jnp.float32)
            for r in range(width):
                part = y[:, r * LANES : (r + 1) * LANES]
                if b == 0:
                    part = jnp.where(lane == 0, 0.0, pltpu.roll(part, 1, axis=1))
                if b == 2:
                    part = jnp.where(lane == LANES - 1, 0.0, pltpu.roll(part, LANES - 1, axis=1))
                total[r] = total[r] + part
        for r in range(width):
            out_ref[start + r] = total[r].astype(out_ref.dtype)


def conv_call(flags, xs, conv_w, out_dtype):
    rows = xs[0].shape[0] - 2
    outs, ins = conv_w.shape[2:]
    return pl.pallas_call(
        functools.partial(conv_kernel, len(xs)),
        in_specs=[
            pl.BlockSpec(memory_space=pltpu.SMEM),
            *[pl.BlockSpec(memory_space=pltpu.VMEM)] * len(xs),
            pl.BlockSpec(memory_space=pltpu.HBM),
        ],
        out_specs=pl.BlockSpec(memory_space=pltpu.VMEM),
        out_shape=jax.ShapeDtypeStruct((rows, outs, LANES), out_dtype),
        scratch_shapes=[
            pltpu.VMEM((3, outs, 3 * ins), jnp.bfloat16),
            pltpu.VMEM((3 * ins, rows * LANES), jnp.bfloat16),
            pltpu.SemaphoreType.DMA((3, 3)),
        ],
        compiler_params=pltpu.CompilerParams(vmem_limit_bytes=57 * MIB),
        cost_estimate=cost(9000),
        name="norm_conv",
    )(flags, *xs, conv_w)


def extra_rows(channels):
    return -(-2 * channels // (16 * LANES)) * 16


def vector_rows(gain, bias):
    rows = jnp.concatenate([gain, bias]).reshape(-1, LANES)
    return jnp.pad(rows, ((0, extra_rows(gain.shape[0]) - rows.shape[0]), (0, 0)))


def columns_of(rows, channels):
    turned = rows.astype(jnp.float32).T
    count = channels // LANES
    column = lambda at: jnp.concatenate([turned[:, at + j : at + j + 1] for j in range(count)], axis=0)
    return column(0), column(count)


def attached(array, rows):
    shape = (array.shape[0],) + rows.shape
    return jnp.concatenate([array, jnp.broadcast_to(rows[None], shape)], axis=1)


def activate_kernel(amount, flags_ref, sums_ref, before_ref, x_ref, after_ref, affine_ref, out_ref):
    rows, channels, _ = x_ref.shape
    width = D // GROUPS
    groups = channels // width

    def column(offset):
        return jnp.concatenate(
            [jnp.full((width, 1), sums_ref[offset + g], jnp.float32) for g in range(groups)], axis=0
        )

    mean = column(0) / amount
    variance = column(groups) / amount - mean * mean
    scale = lax.rsqrt(variance + epsilon) * affine_ref[:, 0:1]
    shift = affine_ref[:, 1:2]
    for r in range(rows + 2):
        x = before_ref[0] if r == 0 else after_ref[0] if r == rows + 1 else x_ref[r - 1]
        z = ((x.astype(jnp.float32) - mean) * scale + shift) * 0.5
        z = z + z * jnp.tanh(z)
        if r == 0:
            z = jnp.where(flags_ref[0] == 1, z, 0.0)
        if r == rows + 1:
            z = jnp.where(flags_ref[1] == 1, z, 0.0)
        out_ref[r] = z.astype(jnp.bfloat16)


def activate_call(flags, sums, amount, before, x, after, affine):
    rows, channels, _ = x.shape
    smem = pl.BlockSpec(memory_space=pltpu.SMEM)
    vmem = pl.BlockSpec(memory_space=pltpu.VMEM)
    return pl.pallas_call(
        functools.partial(activate_kernel, amount),
        in_specs=[smem, smem, vmem, vmem, vmem, vmem],
        out_specs=vmem,
        out_shape=jax.ShapeDtypeStruct((rows + 2, channels, LANES), jnp.bfloat16),
        compiler_params=pltpu.CompilerParams(vmem_limit_bytes=VMEM_LIMIT),
        cost_estimate=cost(1000),
        name="activate",
    )(flags, sums, before, x, after, affine)


def small_call(kernel, out_shape, name, *operands):
    vmem = pl.BlockSpec(memory_space=pltpu.VMEM)
    return pl.pallas_call(
        kernel,
        in_specs=[vmem] * len(operands),
        out_specs=vmem,
        out_shape=jax.ShapeDtypeStruct(out_shape, jnp.bfloat16),
        compiler_params=pltpu.CompilerParams(vmem_limit_bytes=VMEM_LIMIT),
        cost_estimate=cost(1000),
        name=name,
    )(*operands)


def resid_kernel(own_ref, received_ref, x_ref, bias_ref, vector_ref, out_ref):
    rows, channels, _ = x_ref.shape
    for r in range(rows):
        hidden = own_ref[r] + received_ref[r].astype(jnp.float32) + bias_ref[...]
        out_ref[r, :channels] = (x_ref[r].astype(jnp.float32) + hidden).astype(jnp.bfloat16)
        out_ref[r, channels:] = vector_ref[...]


def parity_matrix(channels):
    half = channels // 2
    to = lax.broadcasted_iota(jnp.int32, (channels, channels), 0)
    source = lax.broadcasted_iota(jnp.int32, (channels, channels), 1)
    wanted = jnp.where(to < half, 2 * to, 2 * (to - half) + 1)
    return (source == wanted).astype(jnp.bfloat16)


def split_kernel(own_ref, split_ref):
    _, rows, half, _ = split_ref.shape
    chosen = parity_matrix(2 * half)
    for r in range(rows):
        y = jnp.dot(chosen, own_ref[r, : 2 * half], preferred_element_type=jnp.float32)
        y = y.astype(jnp.bfloat16)
        split_ref[0, r] = y[:half]
        split_ref[1, r] = y[half:]


def arrange_kernel(flip_ref, w_ref, out_ref):
    count, channels, _ = out_ref.shape
    chosen = parity_matrix(channels)
    for i in range(count):
        y = lax.dot_general(
            chosen,
            w_ref[:, i * channels : (i + 1) * channels],
            (((1,), (1,)), ((), ())),
            preferred_element_type=jnp.float32,
        )
        out_ref[jnp.where(flip_ref[0] == 1, count - 1 - i, i)] = y.astype(jnp.bfloat16)


def arrange_call(flip, w_out, count):
    features, channels = w_out.shape
    return pl.pallas_call(
        arrange_kernel,
        in_specs=[
            pl.BlockSpec(memory_space=pltpu.SMEM),
            pl.BlockSpec(memory_space=pltpu.VMEM),
        ],
        out_specs=pl.BlockSpec(memory_space=pltpu.VMEM),
        out_shape=jax.ShapeDtypeStruct((count, channels // count, features), jnp.bfloat16),
        compiler_params=pltpu.CompilerParams(vmem_limit_bytes=VMEM_LIMIT),
        cost_estimate=cost(2000),
        name="arrange",
    )(flip.astype(jnp.int32).reshape(1), w_out)


def project_kernel(parts, order_ref, *refs):
    part_refs = refs[:parts]
    w_hbm, q_ref, kv_ref, w_ref, normed_ref, sems = refs[parts:]
    rows = part_refs[0].shape[0]
    channels = w_hbm.shape[1] // parts
    total = parts * channels
    copies = [pltpu.make_async_copy(w_hbm.at[i], w_ref.at[i], sems.at[i]) for i in range(3)]
    for copy in copies:
        copy.start()
    affine = [columns_of(ref[0, channels:], channels) for ref in part_refs]
    for r in range(rows):
        x = [ref[r, :channels].astype(jnp.float32) for ref in part_refs]
        mean = sum(jnp.sum(a, axis=0, keepdims=True) for a in x) / total
        var = sum(jnp.sum(a * a, axis=0, keepdims=True) for a in x) / total - mean * mean
        inverse = lax.rsqrt(var + epsilon)
        for j in range(parts):
            at = pl.ds(pl.multiple_of(order_ref[j] * channels, LANES), channels)
            z = (x[j] - mean) * inverse * affine[j][0] + affine[j][1]
            normed_ref[r * LANES : (r + 1) * LANES, at] = z.astype(jnp.bfloat16).T
    for i in range(3):
        copies[i].wait()
        y = jnp.dot(normed_ref[...], w_ref[i], preferred_element_type=jnp.float32)
        y = y.astype(jnp.bfloat16)
        if i == 0:
            q_ref[...] = y * SCORE_SCALE
        else:
            kv_ref[i - 1] = y


def project_call(order, parts, w):
    rows = parts[0].shape[0]
    positions = rows * LANES
    _, depth, features = w.shape
    vmem = pl.BlockSpec(memory_space=pltpu.VMEM)
    return pl.pallas_call(
        functools.partial(project_kernel, len(parts)),
        in_specs=[
            pl.BlockSpec(memory_space=pltpu.SMEM),
            *[vmem] * len(parts),
            pl.BlockSpec(memory_space=pltpu.HBM),
        ],
        out_specs=(vmem, vmem),
        out_shape=(
            jax.ShapeDtypeStruct((positions, features), jnp.bfloat16),
            jax.ShapeDtypeStruct((2, positions, features), jnp.bfloat16),
        ),
        scratch_shapes=[
            pltpu.VMEM((3, depth, features), jnp.bfloat16),
            pltpu.VMEM((positions, depth), jnp.bfloat16),
            pltpu.SemaphoreType.DMA((3,)),
        ],
        compiler_params=pltpu.CompilerParams(vmem_limit_bytes=55 * MIB),
        cost_estimate=cost(6500),
        name="norm_project",
    )(order, *parts, w)


def branch_kernel(parity_ref, resid_ref, *refs):
    total = resid_ref[0].astype(jnp.float32)
    for ref in refs[:-1]:
        total = total + ref[0].astype(jnp.float32)
    refs[-1][...] = total.astype(jnp.bfloat16)


def branch_call(parity, resid_split, terms):
    shape = resid_split.shape
    block = pl.BlockSpec((1,) + shape[1:], lambda i, parity: (parity[0], 0, 0, 0))
    return pl.pallas_call(
        branch_kernel,
        grid_spec=pltpu.PrefetchScalarGridSpec(
            num_scalar_prefetch=1,
            grid=(1,),
            in_specs=[block] * (1 + len(terms)),
            out_specs=pl.BlockSpec(shape[1:], lambda i, parity: (0, 0, 0)),
        ),
        out_shape=jax.ShapeDtypeStruct(shape[1:], jnp.bfloat16),
        compiler_params=pltpu.CompilerParams(vmem_limit_bytes=VMEM_LIMIT),
        cost_estimate=cost(1000),
        name="branch_out",
    )(parity.astype(jnp.int32).reshape(1), resid_split, *terms)


def attention_kernel(blocks, carried, final, *refs):
    q_ref = refs[0]
    kv_refs = refs[1 : 1 + 2 * blocks]
    at = 1 + 2 * blocks
    if carried:
        m_in, acc_in = refs[at : at + 2]
        at += 2
    if final:
        w_ref = refs[at]
        at += 1
        out_refs = refs[at:-1]
        joined_ref = refs[-1]
    else:
        m_out, acc_out = refs[at:]
    positions = q_ref.shape[0]
    tile = min(256, positions)
    starts = range(0, positions, tile)
    lanes = lambda array, low: (lax.broadcasted_iota(jnp.int32, array.shape, 1) < HD) == low

    def scores(item):
        start, head, block = item
        q = q_ref[start : start + tile, :]
        q = jnp.where(lanes(q, head == 0), q, jnp.zeros_like(q))
        return lax.dot_general(
            q,
            kv_refs[2 * block][0],
            (((1,), (1,)), ((), ())),
            preferred_element_type=jnp.float32,
        )

    items = [(start, head, block) for start in starts for block in range(blocks) for head in (0, 1)]
    state = {}
    upcoming = scores(items[0])
    for number, item in enumerate(items):
        s = upcoming
        if number + 1 < len(items):
            upcoming = scores(items[number + 1])
        start, head, block = item
        rows = slice(start, start + tile)
        if block == 0 and carried:
            peak, acc = m_in[0, head, rows, :], acc_in[0, head, rows, :]
        elif block == 0:
            peak = acc = None
        else:
            peak, acc = state[start, head]
        v = kv_refs[2 * block + 1][0]
        v = jnp.where(lanes(v, head == 0), v, jnp.ones_like(v))
        top = jnp.broadcast_to(jnp.max(s, axis=1, keepdims=True), (tile, LANES))
        new_peak = top if peak is None else jnp.maximum(peak, top)
        wide = jnp.concatenate([new_peak] * (s.shape[1] // LANES), axis=1)
        p = jnp.exp(s - wide).astype(jnp.bfloat16)
        term = jnp.dot(p, v, preferred_element_type=jnp.float32)
        acc = term if acc is None else acc * jnp.exp(peak - new_peak) + term
        state[start, head] = new_peak, acc
        if block < blocks - 1:
            continue
        if not final:
            m_out[0, head, rows, :] = new_peak
            acc_out[0, head, rows, :] = acc
        elif head == 1:
            parts = [state[start, h][1] for h in (0, 1)]
            parts = [a / pltpu.roll(a, HD, axis=1) for a in parts]
            pair = jnp.where(lanes(acc, True), parts[0], parts[1]).astype(jnp.bfloat16)
            joined_ref[pl.program_id(0), rows, :] = pair

    if final:
        tiles, _, _ = joined_ref.shape

        @pl.when(pl.program_id(0) == tiles - 1)
        def _():
            joined = jnp.concatenate([joined_ref[i] for i in range(tiles)], axis=1)
            for j in range(w_ref.shape[0]):
                y = lax.dot_general(
                    w_ref[j],
                    joined,
                    (((1,), (1,)), ((), ())),
                    preferred_element_type=jnp.float32,
                )
                out = out_refs[j] if len(out_refs) > 1 else out_refs[0].at[j]
                half = w_ref.shape[1] // 2
                for parity in range(2):
                    for r in range(positions // LANES):
                        out[parity, r] = y[
                            parity * half : (parity + 1) * half, r * LANES : (r + 1) * LANES
                        ].astype(out.dtype)


def attention_call(q, pairs, state, w=None, own_apart=False):
    positions, features = q.shape
    tiles = features // LANES
    final = w is not None
    carry = pl.BlockSpec((1, 2, positions, LANES), lambda i: (i, 0, 0, 0))
    carry_shape = jax.ShapeDtypeStruct((tiles, 2, positions, LANES), jnp.float32)
    operands = [q]
    specs = [pl.BlockSpec((positions, LANES), lambda i: (0, i))]
    for pair in pairs:
        for array, place in pair:
            operands.append(array)
            specs.append(
                pl.BlockSpec((1, positions, LANES), functools.partial(lambda p, i: (p, 0, i), place))
            )
    if state is not None:
        operands += list(state)
        specs += [carry, carry]
    scratch = []
    if final:
        operands.append(w)
        specs.append(pl.BlockSpec(w.shape, lambda i: (0, 0, 0)))
        shape = (2, positions // LANES, w.shape[1] // 2, LANES)
        if own_apart:
            out_shape = (
                jax.ShapeDtypeStruct(shape, jnp.bfloat16),
                jax.ShapeDtypeStruct(shape, jnp.float32),
            )
        else:
            out_shape = (jax.ShapeDtypeStruct((w.shape[0],) + shape, jnp.bfloat16),)
        out_specs = tuple(
            pl.BlockSpec(o.shape, functools.partial(lambda n, i: (0,) * n, len(o.shape)))
            for o in out_shape
        )
        scratch = [pltpu.VMEM((tiles, positions, LANES), jnp.bfloat16)]
    else:
        out_shape = (carry_shape, carry_shape)
        out_specs = (carry, carry)
    keys = positions * len(pairs)
    return pl.pallas_call(
        functools.partial(attention_kernel, len(pairs), state is not None, final),
        grid=(tiles,),
        in_specs=specs,
        out_specs=out_specs,
        out_shape=out_shape,
        scratch_shapes=scratch,
        compiler_params=pltpu.CompilerParams(vmem_limit_bytes=VMEM_LIMIT),
        cost_estimate=cost(1000 + 3200 * len(pairs)),
        name="attend",
    )(*operands)


def per_device(
    latent,
    stale_kv,
    timestep,
    w_time,
    gn_gain,
    gn_bias,
    conv_w,
    conv_b,
    ln_gain,
    ln_bias,
    w_qkv,
    w_out,
):
    latent_rows = latent[0]
    rows_count = lax.axis_size("rows")
    tp_count = lax.axis_size("tp")
    span_rows, local_channels, grid_width = latent_rows.shape
    positions = span_rows * grid_width
    group_width = D // GROUPS
    local_groups = local_channels // group_width
    my_block = lax.axis_index("rows")
    cfg = lax.axis_index("cfg")
    tp = lax.axis_index("tp")

    latent32 = latent_rows.astype(jnp.float32)
    values32 = latent32.reshape(span_rows, local_groups, group_width, grid_width)
    sums = jnp.stack(
        [jnp.sum(values32, axis=(0, 2, 3)), jnp.sum(values32 * values32, axis=(0, 2, 3))]
    )
    table = jnp.pad(sums.reshape(-1), (0, LANES - 2 * local_groups))
    table = summed(table, "rows")

    up_pairs = [(i, i + 1) for i in range(rows_count - 1)]
    down_pairs = [(i + 1, i) for i in range(rows_count - 1)]
    before = lax.ppermute(latent_rows[span_rows - 1 :], "rows", up_pairs)
    after = lax.ppermute(latent_rows[:1], "rows", down_pairs)
    flags = jnp.stack([my_block > 0, my_block < rows_count - 1, tp == cfg]).astype(jnp.int32)
    affine = jnp.stack([gn_gain, gn_bias], axis=1).astype(jnp.float32)
    amount = span_rows * rows_count * grid_width * group_width
    activated = activate_call(flags, table, amount, before, latent_rows, after, affine)
    x_mine, x_other = halves_of_inputs(activated)

    forward, backward = ring_pairs(rows_count)
    last = rows_count // 2
    pair = stale_kv[0].reshape(2, positions, -1)
    hops = [(pair, pair)]

    def next_hop(*after):
        ahead, behind = hops[-1]
        if len(hops) == last:
            ahead, behind = ahead[:1], behind[1:]
        if after:
            ahead, behind, *_ = lax.optimization_barrier((ahead, behind) + after)
        hops.append(
            (lax.ppermute(ahead, "rows", forward), lax.ppermute(behind, "rows", backward))
        )

    def blocks_of(hop):
        ahead, behind = hops[hop]
        if hop == last:
            return [((ahead, 0), (behind, 0))]
        return [((ahead, 0), (ahead, 1)), ((behind, 0), (behind, 1))]

    next_hop(table)

    local_features = w_qkv.shape[2]
    w_project = w_qkv.transpose(1, 0, 2)
    flip = jnp.logical_and(tp_count == 2, tp == 0)
    w_back = arrange_call(flip, w_out, tp_count)
    order = jnp.stack([tp, 1 - tp]).astype(jnp.int32) if tp_count == 2 else jnp.zeros((1,), jnp.int32)
    flags_other, order, w_back, *_ = lax.optimization_barrier(
        (flags, order, w_back) + tuple(x_mine[1:])
    )

    conv_sent = conv_call(flags_other, x_other, conv_w, jnp.bfloat16)
    conv_received = swapped(conv_sent, "cfg")
    next_hop(conv_sent)
    conv_own = conv_call(flags, x_mine, conv_w, jnp.float32)

    half_width = TEMB // 2
    frequencies = jnp.exp(
        -math.log(10000.0) * jnp.arange(half_width, dtype=jnp.float32) / half_width
    )
    angles = timestep.astype(jnp.float32)[0] * frequencies
    embedding = jnp.concatenate([jnp.cos(angles), jnp.sin(angles)])
    time_bias = jnp.dot(
        jax.nn.silu(embedding)[None, :], w_time.astype(jnp.float32), precision=lax.Precision.HIGHEST
    )[0]
    bias = conv_b.astype(jnp.float32) + time_bias
    wide = tp_count == 2
    rows = vector_rows(ln_gain, ln_bias) if wide else jnp.zeros((16, LANES), jnp.bfloat16)
    resid = small_call(
        resid_kernel,
        (span_rows, local_channels + rows.shape[0], grid_width),
        "residual",
        conv_own,
        conv_received,
        latent_rows,
        bias[:, None],
        rows,
    )
    if tp_count == 2:
        parts = [resid, need(swapped(resid, "tp"), hops[2])]
    else:
        full = lax.all_gather(resid[:, :local_channels], "tp", axis=1, tiled=True)
        vectors = lax.all_gather(jnp.stack([ln_gain, ln_bias]), "tp", axis=1, tiled=True)
        parts = [attached(full, vector_rows(vectors[0], vectors[1]))]
    next_hop(resid)
    queries, fresh = project_call(order, parts, w_project)
    resid_split = small_call(
        split_kernel, (2, span_rows, local_channels // 2, grid_width), "parity_split", resid
    )
    fresh_kv = fresh.reshape(1, 2, span_rows, grid_width, local_features)

    group = [((fresh, 0), (fresh, 1))] + blocks_of(1) + blocks_of(2)
    state = None
    for hop in range(3, last + 1):
        state = attention_call(queries, group, state)
        while len(hops) <= last:
            next_hop(state[0])
        group = blocks_of(hop)
    if tp_count == 2:
        sent, kept_terms = attention_call(queries, group, state, w_back, True)
        terms = (kept_terms, swapped(sent, "tp"))
    else:
        (sent,) = attention_call(queries, group, state, w_back)
        terms = (lax.psum_scatter(sent, "tp", scatter_dimension=0),)

    other_branch = swapped(branch_call(1 - cfg, resid_split, terms), "cfg")
    kept = branch_call(cfg, resid_split, terms)
    is_cond = cfg == 0
    cond_out = jnp.where(is_cond, kept, other_branch).astype(jnp.float32)
    uncond_out = jnp.where(is_cond, other_branch, kept).astype(jnp.float32)
    guided = (uncond_out + guidance * (cond_out - uncond_out)).astype(jnp.bfloat16)
    return (guided[:, :, None, :], fresh_kv)


def solution(mesh):
    in_specs = (
        P("cfg", "rows", "tp", None),
        P("cfg", None, "rows", None, "tp"),
        P(),
        P(None, "tp"),
        P("tp"),
        P("tp"),
        P(None, None, "tp", "cfg"),
        P("tp"),
        P("tp"),
        P("tp"),
        P(None, None, "tp"),
        P("tp", None),
    )
    out_specs = (P("rows", "tp", "cfg", None), P("cfg", None, "rows", None, "tp"))
    return jax.shard_map(
        per_device, mesh=mesh, in_specs=in_specs, out_specs=out_specs, check_vma=False
    )
```

```python
import functools
import math

import jax
import jax.numpy as jnp
from jax import lax
from jax.experimental import pallas as pl
from jax.experimental.pallas import tpu as pltpu
from jax.sharding import PartitionSpec as P

D = 1280
HD = 64
GROUPS = 32
TEMB = 320
LANES = 128

epsilon = 1e-05
guidance = 5.0
SCORE_SCALE = 1.0 / math.sqrt(HD)
MIB = 1024 * 1024
VMEM_LIMIT = 32 * MIB
COST_SHARE = 0.02


def cost(work):
    return pl.CostEstimate(flops=int(work * 1e6 * COST_SHARE), bytes_accessed=1000, transcendentals=0)


def swapped(array, axis):
    return lax.ppermute(array, axis, [(i, i ^ 1) for i in range(lax.axis_size(axis))])


def ring_pairs(count):
    order = list(range(0, count, 2)) + list(range(count - 1, 0, -2))
    forward = [(order[i], order[(i + 1) % count]) for i in range(count)]
    backward = [(j, i) for i, j in forward]
    return forward, backward


def summed(array, axes):
    count = lax.axis_size(axes)
    spread = jnp.broadcast_to(array[None], (count,) + array.shape)
    return jnp.sum(lax.all_to_all(spread, axes, 0, 0, tiled=True), axis=0)


def need(array, others):
    return lax.optimization_barrier((array,) + tuple(others))[0] if others else array


def halves_of_inputs(own):
    cfg = lax.axis_index("cfg")
    if lax.axis_size("tp") != 2:
        full = lax.all_gather(own, "tp", axis=1, tiled=True)
        half = full.shape[1] // 2
        mine = lax.dynamic_slice_in_dim(full, cfg * half, half, 1)
        sent = lax.dynamic_slice_in_dim(full, (1 - cfg) * half, half, 1)
        return [mine], [swapped(sent, "cfg")]
    across = lax.ppermute(own, ("cfg", "tp"), [(1, 3), (2, 0)])
    pairs = [(0, 1), (3, 2)]
    own_side = lax.ppermute(own, ("cfg", "tp"), pairs)
    across_side = lax.ppermute(across, ("cfg", "tp"), pairs)
    return [own, own_side], [across, across_side]


def conv_kernel(choices, flags_ref, *refs):
    x_refs = refs[:choices]
    w_hbm, out_ref, w_ref, act_ref, sems = refs[choices:]
    rows = out_ref.shape[0]
    ins = w_hbm.shape[3]
    copies = {}
    for b in (1, 0, 2):
        for a in range(3):
            copies[a, b] = pltpu.make_async_copy(
                w_hbm.at[a, b], w_ref.at[b, :, a * ins : (a + 1) * ins], sems.at[a, b]
            )
            copies[a, b].start()
    for r in range(rows + 2):
        x = [ref[r] for ref in x_refs]
        x = x[0] if choices == 1 else jnp.where(flags_ref[2] == 1, x[0], x[1])
        for a in range(3):
            if 0 <= r - a < rows:
                act_ref[a * ins : (a + 1) * ins, (r - a) * LANES : (r - a + 1) * LANES] = x

    width = min(2, rows)
    lane = lax.broadcasted_iota(jnp.int32, (out_ref.shape[1], LANES), 1)
    for start in range(0, rows, width):
        cols = slice(start * LANES, (start + width) * LANES)
        total = [0.0] * width
        for b in (1, 0, 2):
            if start == 0:
                for a in range(3):
                    copies[a, b].wait()
            y = jnp.dot(w_ref[b], act_ref[:, cols], preferred_element_type=jnp.float32)
            for r in range(width):
                part = y[:, r * LANES : (r + 1) * LANES]
                if b == 0:
                    part = jnp.where(lane == 0, 0.0, pltpu.roll(part, 1, axis=1))
                if b == 2:
                    part = jnp.where(lane == LANES - 1, 0.0, pltpu.roll(part, LANES - 1, axis=1))
                total[r] = total[r] + part
        for r in range(width):
            out_ref[start + r] = total[r].astype(out_ref.dtype)


def conv_call(flags, xs, conv_w, out_dtype):
    rows = xs[0].shape[0] - 2
    outs, ins = conv_w.shape[2:]
    return pl.pallas_call(
        functools.partial(conv_kernel, len(xs)),
        in_specs=[
            pl.BlockSpec(memory_space=pltpu.SMEM),
            *[pl.BlockSpec(memory_space=pltpu.VMEM)] * len(xs),
            pl.BlockSpec(memory_space=pltpu.HBM),
        ],
        out_specs=pl.BlockSpec(memory_space=pltpu.VMEM),
        out_shape=jax.ShapeDtypeStruct((rows, outs, LANES), out_dtype),
        scratch_shapes=[
            pltpu.VMEM((3, outs, 3 * ins), jnp.bfloat16),
            pltpu.VMEM((3 * ins, rows * LANES), jnp.bfloat16),
            pltpu.SemaphoreType.DMA((3, 3)),
        ],
        compiler_params=pltpu.CompilerParams(vmem_limit_bytes=57 * MIB),
        cost_estimate=cost(9000),
        name="norm_conv",
    )(flags, *xs, conv_w)


def extra_rows(channels):
    return -(-2 * channels // (16 * LANES)) * 16


def vector_rows(gain, bias):
    rows = jnp.concatenate([gain, bias]).reshape(-1, LANES)
    return jnp.pad(rows, ((0, extra_rows(gain.shape[0]) - rows.shape[0]), (0, 0)))


def columns_of(rows, channels):
    turned = rows.astype(jnp.float32).T
    count = channels // LANES
    column = lambda at: jnp.concatenate([turned[:, at + j : at + j + 1] for j in range(count)], axis=0)
    return column(0), column(count)


def attached(array, rows):
    shape = (array.shape[0],) + rows.shape
    return jnp.concatenate([array, jnp.broadcast_to(rows[None], shape)], axis=1)


def activate_kernel(amount, flags_ref, sums_ref, before_ref, x_ref, after_ref, affine_ref, out_ref):
    rows, channels, _ = x_ref.shape
    width = D // GROUPS
    groups = channels // width

    def column(offset):
        return jnp.concatenate(
            [jnp.full((width, 1), sums_ref[offset + g], jnp.float32) for g in range(groups)], axis=0
        )

    mean = column(0) / amount
    variance = column(groups) / amount - mean * mean
    scale = lax.rsqrt(variance + epsilon) * affine_ref[:, 0:1]
    shift = affine_ref[:, 1:2]
    for r in range(rows + 2):
        x = before_ref[0] if r == 0 else after_ref[0] if r == rows + 1 else x_ref[r - 1]
        z = ((x.astype(jnp.float32) - mean) * scale + shift) * 0.5
        z = z + z * jnp.tanh(z)
        if r == 0:
            z = jnp.where(flags_ref[0] == 1, z, 0.0)
        if r == rows + 1:
            z = jnp.where(flags_ref[1] == 1, z, 0.0)
        out_ref[r] = z.astype(jnp.bfloat16)


def activate_call(flags, sums, amount, before, x, after, affine):
    rows, channels, _ = x.shape
    smem = pl.BlockSpec(memory_space=pltpu.SMEM)
    vmem = pl.BlockSpec(memory_space=pltpu.VMEM)
    return pl.pallas_call(
        functools.partial(activate_kernel, amount),
        in_specs=[smem, smem, vmem, vmem, vmem, vmem],
        out_specs=vmem,
        out_shape=jax.ShapeDtypeStruct((rows + 2, channels, LANES), jnp.bfloat16),
        compiler_params=pltpu.CompilerParams(vmem_limit_bytes=VMEM_LIMIT),
        cost_estimate=cost(1000),
        name="activate",
    )(flags, sums, before, x, after, affine)


def small_call(kernel, out_shape, name, *operands):
    vmem = pl.BlockSpec(memory_space=pltpu.VMEM)
    return pl.pallas_call(
        kernel,
        in_specs=[vmem] * len(operands),
        out_specs=vmem,
        out_shape=jax.ShapeDtypeStruct(out_shape, jnp.bfloat16),
        compiler_params=pltpu.CompilerParams(vmem_limit_bytes=VMEM_LIMIT),
        cost_estimate=cost(1000),
        name=name,
    )(*operands)


def resid_kernel(own_ref, received_ref, x_ref, bias_ref, vector_ref, out_ref):
    rows, channels, _ = x_ref.shape
    for r in range(rows):
        hidden = own_ref[r] + received_ref[r].astype(jnp.float32) + bias_ref[...]
        out_ref[r, :channels] = (x_ref[r].astype(jnp.float32) + hidden).astype(jnp.bfloat16)
        out_ref[r, channels:] = vector_ref[...]


def parity_matrix(channels):
    half = channels // 2
    to = lax.broadcasted_iota(jnp.int32, (channels, channels), 0)
    source = lax.broadcasted_iota(jnp.int32, (channels, channels), 1)
    wanted = jnp.where(to < half, 2 * to, 2 * (to - half) + 1)
    return (source == wanted).astype(jnp.bfloat16)


def split_kernel(own_ref, split_ref):
    _, rows, half, _ = split_ref.shape
    chosen = parity_matrix(2 * half)
    for r in range(rows):
        y = jnp.dot(chosen, own_ref[r, : 2 * half], preferred_element_type=jnp.float32)
        y = y.astype(jnp.bfloat16)
        split_ref[0, r] = y[:half]
        split_ref[1, r] = y[half:]


def arrange_kernel(flip_ref, w_ref, out_ref):
    count, channels, _ = out_ref.shape
    chosen = parity_matrix(channels)
    for i in range(count):
        y = lax.dot_general(
            chosen,
            w_ref[:, i * channels : (i + 1) * channels],
            (((1,), (1,)), ((), ())),
            preferred_element_type=jnp.float32,
        )
        out_ref[jnp.where(flip_ref[0] == 1, count - 1 - i, i)] = y.astype(jnp.bfloat16)


def arrange_call(flip, w_out, count):
    features, channels = w_out.shape
    return pl.pallas_call(
        arrange_kernel,
        in_specs=[
            pl.BlockSpec(memory_space=pltpu.SMEM),
            pl.BlockSpec(memory_space=pltpu.VMEM),
        ],
        out_specs=pl.BlockSpec(memory_space=pltpu.VMEM),
        out_shape=jax.ShapeDtypeStruct((count, channels // count, features), jnp.bfloat16),
        compiler_params=pltpu.CompilerParams(vmem_limit_bytes=VMEM_LIMIT),
        cost_estimate=cost(2000),
        name="arrange",
    )(flip.astype(jnp.int32).reshape(1), w_out)


def project_kernel(parts, order_ref, *refs):
    part_refs = refs[:parts]
    w_hbm, q_ref, kv_ref, w_ref, normed_ref, sems = refs[parts:]
    rows = part_refs[0].shape[0]
    channels = w_hbm.shape[1] // parts
    total = parts * channels
    copies = [pltpu.make_async_copy(w_hbm.at[i], w_ref.at[i], sems.at[i]) for i in range(3)]
    for copy in copies:
        copy.start()
    affine = [columns_of(ref[0, channels:], channels) for ref in part_refs]
    for r in range(rows):
        x = [ref[r, :channels].astype(jnp.float32) for ref in part_refs]
        mean = sum(jnp.sum(a, axis=0, keepdims=True) for a in x) / total
        var = sum(jnp.sum(a * a, axis=0, keepdims=True) for a in x) / total - mean * mean
        inverse = lax.rsqrt(var + epsilon)
        for j in range(parts):
            at = pl.ds(pl.multiple_of(order_ref[j] * channels, LANES), channels)
            z = (x[j] - mean) * inverse * affine[j][0] + affine[j][1]
            normed_ref[r * LANES : (r + 1) * LANES, at] = z.astype(jnp.bfloat16).T
    for i in range(3):
        copies[i].wait()
        y = jnp.dot(normed_ref[...], w_ref[i], preferred_element_type=jnp.float32)
        y = y.astype(jnp.bfloat16)
        if i == 0:
            q_ref[...] = y * SCORE_SCALE
        else:
            kv_ref[i - 1] = y


def project_call(order, parts, w):
    rows = parts[0].shape[0]
    positions = rows * LANES
    _, depth, features = w.shape
    vmem = pl.BlockSpec(memory_space=pltpu.VMEM)
    return pl.pallas_call(
        functools.partial(project_kernel, len(parts)),
        in_specs=[
            pl.BlockSpec(memory_space=pltpu.SMEM),
            *[vmem] * len(parts),
            pl.BlockSpec(memory_space=pltpu.HBM),
        ],
        out_specs=(vmem, vmem),
        out_shape=(
            jax.ShapeDtypeStruct((positions, features), jnp.bfloat16),
            jax.ShapeDtypeStruct((2, positions, features), jnp.bfloat16),
        ),
        scratch_shapes=[
            pltpu.VMEM((3, depth, features), jnp.bfloat16),
            pltpu.VMEM((positions, depth), jnp.bfloat16),
            pltpu.SemaphoreType.DMA((3,)),
        ],
        compiler_params=pltpu.CompilerParams(vmem_limit_bytes=55 * MIB),
        cost_estimate=cost(6500),
        name="norm_project",
    )(order, *parts, w)


def branch_kernel(parity_ref, resid_ref, *refs):
    total = resid_ref[0].astype(jnp.float32)
    for ref in refs[:-1]:
        total = total + ref[0].astype(jnp.float32)
    refs[-1][...] = total.astype(jnp.bfloat16)


def branch_call(parity, resid_split, terms):
    shape = resid_split.shape
    block = pl.BlockSpec((1,) + shape[1:], lambda i, parity: (parity[0], 0, 0, 0))
    return pl.pallas_call(
        branch_kernel,
        grid_spec=pltpu.PrefetchScalarGridSpec(
            num_scalar_prefetch=1,
            grid=(1,),
            in_specs=[block] * (1 + len(terms)),
            out_specs=pl.BlockSpec(shape[1:], lambda i, parity: (0, 0, 0)),
        ),
        out_shape=jax.ShapeDtypeStruct(shape[1:], jnp.bfloat16),
        compiler_params=pltpu.CompilerParams(vmem_limit_bytes=VMEM_LIMIT),
        cost_estimate=cost(1000),
        name="branch_out",
    )(parity.astype(jnp.int32).reshape(1), resid_split, *terms)


def attention_kernel(blocks, carried, final, *refs):
    q_ref = refs[0]
    kv_refs = refs[1 : 1 + 2 * blocks]
    at = 1 + 2 * blocks
    if carried:
        m_in, acc_in = refs[at : at + 2]
        at += 2
    if final:
        w_ref = refs[at]
        at += 1
        out_refs = refs[at:-1]
        joined_ref = refs[-1]
    else:
        m_out, acc_out = refs[at:]
    positions = q_ref.shape[0]
    tile = min(256, positions)
    starts = range(0, positions, tile)
    lanes = lambda array, low: (lax.broadcasted_iota(jnp.int32, array.shape, 1) < HD) == low

    def scores(item):
        start, head, block = item
        q = q_ref[start : start + tile, :]
        q = jnp.where(lanes(q, head == 0), q, jnp.zeros_like(q))
        return lax.dot_general(
            q,
            kv_refs[2 * block][0],
            (((1,), (1,)), ((), ())),
            preferred_element_type=jnp.float32,
        )

    items = [(start, head, block) for start in starts for block in range(blocks) for head in (0, 1)]
    state = {}
    upcoming = scores(items[0])
    for number, item in enumerate(items):
        s = upcoming
        if number + 1 < len(items):
            upcoming = scores(items[number + 1])
        start, head, block = item
        rows = slice(start, start + tile)
        if block == 0 and carried:
            peak, acc = m_in[0, head, rows, :], acc_in[0, head, rows, :]
        elif block == 0:
            peak = acc = None
        else:
            peak, acc = state[start, head]
        v = kv_refs[2 * block + 1][0]
        v = jnp.where(lanes(v, head == 0), v, jnp.ones_like(v))
        top = jnp.broadcast_to(jnp.max(s, axis=1, keepdims=True), (tile, LANES))
        new_peak = top if peak is None else jnp.maximum(peak, top)
        wide = jnp.concatenate([new_peak] * (s.shape[1] // LANES), axis=1)
        p = jnp.exp(s - wide).astype(jnp.bfloat16)
        term = jnp.dot(p, v, preferred_element_type=jnp.float32)
        acc = term if acc is None else acc * jnp.exp(peak - new_peak) + term
        state[start, head] = new_peak, acc
        if block < blocks - 1:
            continue
        if not final:
            m_out[0, head, rows, :] = new_peak
            acc_out[0, head, rows, :] = acc
        elif head == 1:
            parts = [state[start, h][1] for h in (0, 1)]
            parts = [a / pltpu.roll(a, HD, axis=1) for a in parts]
            pair = jnp.where(lanes(acc, True), parts[0], parts[1]).astype(jnp.bfloat16)
            joined_ref[pl.program_id(0), rows, :] = pair

    if final:
        tiles, _, _ = joined_ref.shape

        @pl.when(pl.program_id(0) == tiles - 1)
        def _():
            joined = jnp.concatenate([joined_ref[i] for i in range(tiles)], axis=1)
            for j in range(w_ref.shape[0]):
                y = lax.dot_general(
                    w_ref[j],
                    joined,
                    (((1,), (1,)), ((), ())),
                    preferred_element_type=jnp.float32,
                )
                out = out_refs[j] if len(out_refs) > 1 else out_refs[0].at[j]
                half = w_ref.shape[1] // 2
                for parity in range(2):
                    for r in range(positions // LANES):
                        out[parity, r] = y[
                            parity * half : (parity + 1) * half, r * LANES : (r + 1) * LANES
                        ].astype(out.dtype)


def attention_call(q, pairs, state, w=None, own_apart=False):
    positions, features = q.shape
    tiles = features // LANES
    final = w is not None
    carry = pl.BlockSpec((1, 2, positions, LANES), lambda i: (i, 0, 0, 0))
    carry_shape = jax.ShapeDtypeStruct((tiles, 2, positions, LANES), jnp.float32)
    operands = [q]
    specs = [pl.BlockSpec((positions, LANES), lambda i: (0, i))]
    for pair in pairs:
        for array, place in pair:
            operands.append(array)
            specs.append(
                pl.BlockSpec((1, positions, LANES), functools.partial(lambda p, i: (p, 0, i), place))
            )
    if state is not None:
        operands += list(state)
        specs += [carry, carry]
    scratch = []
    if final:
        operands.append(w)
        specs.append(pl.BlockSpec(w.shape, lambda i: (0, 0, 0)))
        shape = (2, positions // LANES, w.shape[1] // 2, LANES)
        if own_apart:
            out_shape = (
                jax.ShapeDtypeStruct(shape, jnp.bfloat16),
                jax.ShapeDtypeStruct(shape, jnp.float32),
            )
        else:
            out_shape = (jax.ShapeDtypeStruct((w.shape[0],) + shape, jnp.bfloat16),)
        out_specs = tuple(
            pl.BlockSpec(o.shape, functools.partial(lambda n, i: (0,) * n, len(o.shape)))
            for o in out_shape
        )
        scratch = [pltpu.VMEM((tiles, positions, LANES), jnp.bfloat16)]
    else:
        out_shape = (carry_shape, carry_shape)
        out_specs = (carry, carry)
    keys = positions * len(pairs)
    return pl.pallas_call(
        functools.partial(attention_kernel, len(pairs), state is not None, final),
        grid=(tiles,),
        in_specs=specs,
        out_specs=out_specs,
        out_shape=out_shape,
        scratch_shapes=scratch,
        compiler_params=pltpu.CompilerParams(vmem_limit_bytes=VMEM_LIMIT),
        cost_estimate=cost(1000 + 3200 * len(pairs)),
        name="attend",
    )(*operands)


def per_device(
    latent,
    stale_kv,
    timestep,
    w_time,
    gn_gain,
    gn_bias,
    conv_w,
    conv_b,
    ln_gain,
    ln_bias,
    w_qkv,
    w_out,
):
    latent_rows = latent[0]
    rows_count = lax.axis_size("rows")
    tp_count = lax.axis_size("tp")
    span_rows, local_channels, grid_width = latent_rows.shape
    positions = span_rows * grid_width
    group_width = D // GROUPS
    local_groups = local_channels // group_width
    my_block = lax.axis_index("rows")
    cfg = lax.axis_index("cfg")
    tp = lax.axis_index("tp")

    latent32 = latent_rows.astype(jnp.float32)
    values32 = latent32.reshape(span_rows, local_groups, group_width, grid_width)
    sums = jnp.stack(
        [jnp.sum(values32, axis=(0, 2, 3)), jnp.sum(values32 * values32, axis=(0, 2, 3))]
    )
    table = jnp.pad(sums.reshape(-1), (0, LANES - 2 * local_groups))
    table = summed(table, "rows")

    up_pairs = [(i, i + 1) for i in range(rows_count - 1)]
    down_pairs = [(i + 1, i) for i in range(rows_count - 1)]
    before = lax.ppermute(latent_rows[span_rows - 1 :], "rows", up_pairs)
    after = lax.ppermute(latent_rows[:1], "rows", down_pairs)
    flags = jnp.stack([my_block > 0, my_block < rows_count - 1, tp == cfg]).astype(jnp.int32)
    affine = jnp.stack([gn_gain, gn_bias], axis=1).astype(jnp.float32)
    amount = span_rows * rows_count * grid_width * group_width
    activated = activate_call(flags, table, amount, before, latent_rows, after, affine)
    x_mine, x_other = halves_of_inputs(activated)

    forward, backward = ring_pairs(rows_count)
    last = rows_count // 2
    pair = stale_kv[0].reshape(2, positions, -1)
    hops = [(pair, pair)]

    def next_hop(*after):
        ahead, behind = hops[-1]
        if len(hops) == last:
            ahead, behind = ahead[:1], behind[1:]
        if after:
            ahead, behind, *_ = lax.optimization_barrier((ahead, behind) + after)
        hops.append(
            (lax.ppermute(ahead, "rows", forward), lax.ppermute(behind, "rows", backward))
        )

    def blocks_of(hop):
        ahead, behind = hops[hop]
        if hop == last:
            return [((ahead, 0), (behind, 0))]
        return [((ahead, 0), (ahead, 1)), ((behind, 0), (behind, 1))]

    next_hop(table)

    local_features = w_qkv.shape[2]
    w_project = w_qkv.transpose(1, 0, 2)
    flip = jnp.logical_and(tp_count == 2, tp == 0)
    w_back = arrange_call(flip, w_out, tp_count)
    order = jnp.stack([tp, 1 - tp]).astype(jnp.int32) if tp_count == 2 else jnp.zeros((1,), jnp.int32)
    flags_other, order, w_back, *_ = lax.optimization_barrier(
        (flags, order, w_back) + tuple(x_mine[1:]) + hops[1]
    )
    next_hop()

    conv_sent = conv_call(flags_other, x_other, conv_w, jnp.bfloat16)
    conv_received = swapped(conv_sent, "cfg")
    conv_own = conv_call(flags, x_mine, conv_w, jnp.float32)

    half_width = TEMB // 2
    frequencies = jnp.exp(
        -math.log(10000.0) * jnp.arange(half_width, dtype=jnp.float32) / half_width
    )
    angles = timestep.astype(jnp.float32)[0] * frequencies
    embedding = jnp.concatenate([jnp.cos(angles), jnp.sin(angles)])
    time_bias = jnp.dot(
        jax.nn.silu(embedding)[None, :], w_time.astype(jnp.float32), precision=lax.Precision.HIGHEST
    )[0]
    bias = conv_b.astype(jnp.float32) + time_bias
    wide = tp_count == 2
    rows = vector_rows(ln_gain, ln_bias) if wide else jnp.zeros((16, LANES), jnp.bfloat16)
    resid = small_call(
        resid_kernel,
        (span_rows, local_channels + rows.shape[0], grid_width),
        "residual",
        conv_own,
        conv_received,
        latent_rows,
        bias[:, None],
        rows,
    )
    if tp_count == 2:
        parts = [resid, need(swapped(resid, "tp"), hops[2])]
    else:
        full = lax.all_gather(resid[:, :local_channels], "tp", axis=1, tiled=True)
        vectors = lax.all_gather(jnp.stack([ln_gain, ln_bias]), "tp", axis=1, tiled=True)
        parts = [attached(full, vector_rows(vectors[0], vectors[1]))]
    next_hop(resid)
    queries, fresh = project_call(order, parts, w_project)
    resid_split = small_call(
        split_kernel, (2, span_rows, local_channels // 2, grid_width), "parity_split", resid
    )
    fresh_kv = fresh.reshape(1, 2, span_rows, grid_width, local_features)

    group = [((fresh, 0), (fresh, 1))] + blocks_of(1)
    state = None
    for hop in range(2, last + 1):
        state = attention_call(queries, group, state)
        while len(hops) <= last:
            next_hop(state[0])
        group = blocks_of(hop)
    if tp_count == 2:
        sent, kept_terms = attention_call(queries, group, state, w_back, True)
        terms = (kept_terms, swapped(sent, "tp"))
    else:
        (sent,) = attention_call(queries, group, state, w_back)
        terms = (lax.psum_scatter(sent, "tp", scatter_dimension=0),)

    other_branch = swapped(branch_call(1 - cfg, resid_split, terms), "cfg")
    kept = branch_call(cfg, resid_split, terms)
    is_cond = cfg == 0
    cond_out = jnp.where(is_cond, kept, other_branch).astype(jnp.float32)
    uncond_out = jnp.where(is_cond, other_branch, kept).astype(jnp.float32)
    guided = (uncond_out + guidance * (cond_out - uncond_out)).astype(jnp.bfloat16)
    return (guided[:, :, None, :], fresh_kv)


def solution(mesh):
    in_specs = (
        P("cfg", "rows", "tp", None),
        P("cfg", None, "rows", None, "tp"),
        P(),
        P(None, "tp"),
        P("tp"),
        P("tp"),
        P(None, None, "tp", "cfg"),
        P("tp"),
        P("tp"),
        P("tp"),
        P(None, None, "tp"),
        P("tp", None),
    )
    out_specs = (P("rows", "tp", "cfg", None), P("cfg", None, "rows", None, "tp"))
    return jax.shard_map(
        per_device, mesh=mesh, in_specs=in_specs, out_specs=out_specs, check_vma=False
    )
```

```python
import functools
import math

import jax
import jax.numpy as jnp
from jax import lax
from jax.experimental import pallas as pl
from jax.experimental.pallas import tpu as pltpu
from jax.sharding import PartitionSpec as P

D = 1280
HD = 64
GROUPS = 32
TEMB = 320
LANES = 128

epsilon = 1e-05
guidance = 5.0
SCORE_SCALE = 1.0 / math.sqrt(HD)
MIB = 1024 * 1024
VMEM_LIMIT = 32 * MIB
COST_SHARE = 0.02


def cost(work):
    return pl.CostEstimate(flops=int(work * 1e6 * COST_SHARE), bytes_accessed=1000, transcendentals=0)


def swapped(array, axis):
    return lax.ppermute(array, axis, [(i, i ^ 1) for i in range(lax.axis_size(axis))])


def ring_pairs(count):
    order = list(range(0, count, 2)) + list(range(count - 1, 0, -2))
    forward = [(order[i], order[(i + 1) % count]) for i in range(count)]
    backward = [(j, i) for i, j in forward]
    return forward, backward


def gather_tp(array, axis):
    if lax.axis_size("tp") != 2:
        return lax.all_gather(array, "tp", axis=axis, tiled=True)
    other = swapped(array, "tp")
    first = lax.axis_index("tp") == 0
    return jnp.concatenate(
        [jnp.where(first, array, other), jnp.where(first, other, array)], axis=axis
    )


def summed(array, axes):
    count = lax.axis_size(axes)
    spread = jnp.broadcast_to(array[None], (count,) + array.shape)
    return jnp.sum(lax.all_to_all(spread, axes, 0, 0, tiled=True), axis=0)


def need(array, others):
    return lax.optimization_barrier((array,) + tuple(others))[0]


def halves_of_inputs(own):
    cfg = lax.axis_index("cfg")
    if lax.axis_size("tp") != 2:
        full = lax.all_gather(own, "tp", axis=1, tiled=True)
        half = full.shape[1] // 2
        mine = lax.dynamic_slice_in_dim(full, cfg * half, half, 1)
        sent = lax.dynamic_slice_in_dim(full, (1 - cfg) * half, half, 1)
        return [mine], [swapped(sent, "cfg")]
    across = lax.ppermute(own, ("cfg", "tp"), [(1, 3), (2, 0)])
    pairs = [(0, 1), (3, 2)]
    own_side = lax.ppermute(own, ("cfg", "tp"), pairs)
    across_side = lax.ppermute(across, ("cfg", "tp"), pairs)
    return [own, own_side], [across, across_side]


def conv_kernel(choices, amount, flags_ref, sums_ref, *refs):
    x_refs = refs[:choices]
    affine_ref, w_hbm, out_ref, w_ref, act_ref, sems = refs[choices:]
    rows = out_ref.shape[0]
    ins = affine_ref.shape[0]
    copies = {}
    for b in (1, 0, 2):
        for a in range(3):
            copies[a, b] = pltpu.make_async_copy(
                w_hbm.at[a, b], w_ref.at[b, :, a * ins : (a + 1) * ins], sems.at[a, b]
            )
            copies[a, b].start()

    groups = ins // (D // GROUPS)
    base = flags_ref[3]

    def column(offset):
        return jnp.concatenate(
            [jnp.full((D // GROUPS, 1), sums_ref[base + offset + g], jnp.float32) for g in range(groups)],
            axis=0,
        )

    mean = column(0) / amount
    variance = column(GROUPS) / amount - mean * mean
    scale = lax.rsqrt(variance + epsilon) * affine_ref[:, 0:1]
    shift = affine_ref[:, 1:2]
    for r in range(rows + 2):
        x = x_refs[0][r]
        if choices == 2:
            x = jnp.where(flags_ref[2] == 1, x, x_refs[1][r])
        z = ((x.astype(jnp.float32) - mean) * scale + shift) * 0.5
        z = z + z * jnp.tanh(z)
        if r == 0:
            z = jnp.where(flags_ref[0] == 1, z, 0.0)
        if r == rows + 1:
            z = jnp.where(flags_ref[1] == 1, z, 0.0)
        z = z.astype(jnp.bfloat16)
        for a in range(3):
            if 0 <= r - a < rows:
                act_ref[a * ins : (a + 1) * ins, (r - a) * LANES : (r - a + 1) * LANES] = z

    width = min(2, rows)
    lane = lax.broadcasted_iota(jnp.int32, (out_ref.shape[1], LANES), 1)
    for start in range(0, rows, width):
        cols = slice(start * LANES, (start + width) * LANES)
        total = [0.0] * width
        for b in (1, 0, 2):
            if start == 0:
                for a in range(3):
                    copies[a, b].wait()
            y = jnp.dot(w_ref[b], act_ref[:, cols], preferred_element_type=jnp.float32)
            for r in range(width):
                part = y[:, r * LANES : (r + 1) * LANES]
                if b == 0:
                    part = jnp.where(lane == 0, 0.0, pltpu.roll(part, 1, axis=1))
                if b == 2:
                    part = jnp.where(lane == LANES - 1, 0.0, pltpu.roll(part, LANES - 1, axis=1))
                total[r] = total[r] + part
        for r in range(width):
            out_ref[start + r] = total[r].astype(out_ref.dtype)


def conv_call(flags, sums, amount, xs, affine, conv_w, out_dtype):
    x = xs[0]
    rows = x.shape[0] - 2
    outs, ins = conv_w.shape[2:]
    return pl.pallas_call(
        functools.partial(conv_kernel, len(xs), amount),
        in_specs=[
            pl.BlockSpec(memory_space=pltpu.SMEM),
            pl.BlockSpec(memory_space=pltpu.SMEM),
            *[pl.BlockSpec(memory_space=pltpu.VMEM)] * (len(xs) + 1),
            pl.BlockSpec(memory_space=pltpu.HBM),
        ],
        out_specs=pl.BlockSpec(memory_space=pltpu.VMEM),
        out_shape=jax.ShapeDtypeStruct((rows, outs, LANES), out_dtype),
        scratch_shapes=[
            pltpu.VMEM((3, outs, 3 * ins), jnp.bfloat16),
            pltpu.VMEM((3 * ins, rows * LANES), jnp.bfloat16),
            pltpu.SemaphoreType.DMA((3, 3)),
        ],
        compiler_params=pltpu.CompilerParams(vmem_limit_bytes=57 * MIB),
        cost_estimate=cost(9000),
        name="norm_conv",
    )(flags, sums, *xs, affine, conv_w)


def parity_matrix(channels):
    half = channels // 2
    to = lax.broadcasted_iota(jnp.int32, (channels, channels), 0)
    source = lax.broadcasted_iota(jnp.int32, (channels, channels), 1)
    wanted = jnp.where(to < half, 2 * to, 2 * (to - half) + 1)
    return (source == wanted).astype(jnp.bfloat16)


def split_kernel(own_ref, split_ref):
    rows, channels, _ = own_ref.shape
    half = channels // 2
    chosen = parity_matrix(channels)
    for r in range(rows):
        y = jnp.dot(chosen, own_ref[r], preferred_element_type=jnp.float32).astype(jnp.bfloat16)
        split_ref[0, r] = y[:half]
        split_ref[1, r] = y[half:]


def split_call(own):
    rows, channels, _ = own.shape
    return pl.pallas_call(
        split_kernel,
        in_specs=[pl.BlockSpec(memory_space=pltpu.VMEM)],
        out_specs=pl.BlockSpec(memory_space=pltpu.VMEM),
        out_shape=jax.ShapeDtypeStruct((2, rows, channels // 2, LANES), jnp.bfloat16),
        compiler_params=pltpu.CompilerParams(vmem_limit_bytes=VMEM_LIMIT),
        cost_estimate=cost(1000),
        name="parity_split",
    )(own)


def arrange_kernel(flip_ref, w_ref, out_ref):
    count, channels, _ = out_ref.shape
    chosen = parity_matrix(channels)
    for i in range(count):
        y = lax.dot_general(
            chosen,
            w_ref[:, i * channels : (i + 1) * channels],
            (((1,), (1,)), ((), ())),
            preferred_element_type=jnp.float32,
        )
        out_ref[jnp.where(flip_ref[0] == 1, count - 1 - i, i)] = y.astype(jnp.bfloat16)


def arrange_call(flip, w_out, count):
    features, channels = w_out.shape
    return pl.pallas_call(
        arrange_kernel,
        in_specs=[
            pl.BlockSpec(memory_space=pltpu.SMEM),
            pl.BlockSpec(memory_space=pltpu.VMEM),
        ],
        out_specs=pl.BlockSpec(memory_space=pltpu.VMEM),
        out_shape=jax.ShapeDtypeStruct((count, channels // count, features), jnp.bfloat16),
        compiler_params=pltpu.CompilerParams(vmem_limit_bytes=VMEM_LIMIT),
        cost_estimate=cost(2000),
        name="arrange",
    )(flip.astype(jnp.int32).reshape(1), w_out)


def project_kernel(parts, order_ref, *refs):
    part_refs = refs[:parts]
    affine_ref, w_hbm, q_ref, kv_ref, w_ref, normed_ref, sems = refs[parts:]
    rows, channels, _ = part_refs[0].shape
    total = parts * channels
    copies = [pltpu.make_async_copy(w_hbm.at[i], w_ref.at[i], sems.at[i]) for i in range(3)]
    for copy in copies:
        copy.start()
    for r in range(rows):
        x = [ref[r].astype(jnp.float32) for ref in part_refs]
        mean = sum(jnp.sum(a, axis=0, keepdims=True) for a in x) / total
        var = sum(jnp.sum(a * a, axis=0, keepdims=True) for a in x) / total - mean * mean
        inverse = lax.rsqrt(var + epsilon)
        for j in range(parts):
            at = pl.ds(pl.multiple_of(order_ref[j] * channels, LANES), channels)
            z = (x[j] - mean) * inverse * affine_ref[at, 0:1] + affine_ref[at, 1:2]
            normed_ref[r * LANES : (r + 1) * LANES, at] = z.astype(jnp.bfloat16).T
    for i in range(3):
        copies[i].wait()
        y = jnp.dot(normed_ref[...], w_ref[i], preferred_element_type=jnp.float32)
        y = y.astype(jnp.bfloat16)
        if i == 0:
            q_ref[...] = y * SCORE_SCALE
        else:
            kv_ref[i - 1] = y


def project_call(order, parts, affine, w):
    rows = parts[0].shape[0]
    positions = rows * LANES
    _, depth, features = w.shape
    vmem = pl.BlockSpec(memory_space=pltpu.VMEM)
    return pl.pallas_call(
        functools.partial(project_kernel, len(parts)),
        in_specs=[
            pl.BlockSpec(memory_space=pltpu.SMEM),
            *[vmem] * (len(parts) + 1),
            pl.BlockSpec(memory_space=pltpu.HBM),
        ],
        out_specs=(vmem, vmem),
        out_shape=(
            jax.ShapeDtypeStruct((positions, features), jnp.bfloat16),
            jax.ShapeDtypeStruct((2, positions, features), jnp.bfloat16),
        ),
        scratch_shapes=[
            pltpu.VMEM((3, depth, features), jnp.bfloat16),
            pltpu.VMEM((positions, depth), jnp.bfloat16),
            pltpu.SemaphoreType.DMA((3,)),
        ],
        compiler_params=pltpu.CompilerParams(vmem_limit_bytes=55 * MIB),
        cost_estimate=cost(6500),
        name="norm_project",
    )(order, *parts, affine, w)


def branch_kernel(parity_ref, resid_ref, *refs):
    total = resid_ref[0].astype(jnp.float32)
    for ref in refs[:-1]:
        total = total + ref[0].astype(jnp.float32)
    refs[-1][...] = total.astype(jnp.bfloat16)


def branch_call(parity, resid_split, terms):
    shape = resid_split.shape
    block = pl.BlockSpec((1,) + shape[1:], lambda i, parity: (parity[0], 0, 0, 0))
    return pl.pallas_call(
        branch_kernel,
        grid_spec=pltpu.PrefetchScalarGridSpec(
            num_scalar_prefetch=1,
            grid=(1,),
            in_specs=[block] * (1 + len(terms)),
            out_specs=pl.BlockSpec(shape[1:], lambda i, parity: (0, 0, 0)),
        ),
        out_shape=jax.ShapeDtypeStruct(shape[1:], jnp.bfloat16),
        compiler_params=pltpu.CompilerParams(vmem_limit_bytes=VMEM_LIMIT),
        cost_estimate=cost(1000),
        name="branch_out",
    )(parity.astype(jnp.int32).reshape(1), resid_split, *terms)


def attention_kernel(blocks, carried, final, *refs):
    q_ref = refs[0]
    kv_refs = refs[1 : 1 + 2 * blocks]
    at = 1 + 2 * blocks
    if carried:
        m_in, acc_in = refs[at : at + 2]
        at += 2
    if final:
        w_ref = refs[at]
        at += 1
        out_refs = refs[at:-1]
        joined_ref = refs[-1]
    else:
        m_out, acc_out = refs[at:]
    positions = q_ref.shape[0]
    tile = min(256, positions)
    starts = range(0, positions, tile)
    lanes = lambda array, low: (lax.broadcasted_iota(jnp.int32, array.shape, 1) < HD) == low

    def scores(item):
        start, head, block = item
        q = q_ref[start : start + tile, :]
        q = jnp.where(lanes(q, head == 0), q, jnp.zeros_like(q))
        return lax.dot_general(
            q,
            kv_refs[2 * block][0],
            (((1,), (1,)), ((), ())),
            preferred_element_type=jnp.float32,
        )

    items = [(start, head, block) for start in starts for block in range(blocks) for head in (0, 1)]
    state = {}
    upcoming = scores(items[0])
    for number, item in enumerate(items):
        s = upcoming
        if number + 1 < len(items):
            upcoming = scores(items[number + 1])
        start, head, block = item
        rows = slice(start, start + tile)
        if block == 0 and carried:
            peak, acc = m_in[0, head, rows, :], acc_in[0, head, rows, :]
        elif block == 0:
            peak = acc = None
        else:
            peak, acc = state[start, head]
        v = kv_refs[2 * block + 1][0]
        v = jnp.where(lanes(v, head == 0), v, jnp.ones_like(v))
        top = jnp.broadcast_to(jnp.max(s, axis=1, keepdims=True), (tile, LANES))
        new_peak = top if peak is None else jnp.maximum(peak, top)
        wide = jnp.concatenate([new_peak] * (s.shape[1] // LANES), axis=1)
        p = jnp.exp(s - wide).astype(jnp.bfloat16)
        term = jnp.dot(p, v, preferred_element_type=jnp.float32)
        acc = term if acc is None else acc * jnp.exp(peak - new_peak) + term
        state[start, head] = new_peak, acc
        if block < blocks - 1:
            continue
        if not final:
            m_out[0, head, rows, :] = new_peak
            acc_out[0, head, rows, :] = acc
        elif head == 1:
            parts = [state[start, h][1] for h in (0, 1)]
            parts = [a / pltpu.roll(a, HD, axis=1) for a in parts]
            pair = jnp.where(lanes(acc, True), parts[0], parts[1]).astype(jnp.bfloat16)
            joined_ref[pl.program_id(0), rows, :] = pair

    if final:
        tiles, _, _ = joined_ref.shape

        @pl.when(pl.program_id(0) == tiles - 1)
        def _():
            joined = jnp.concatenate([joined_ref[i] for i in range(tiles)], axis=1)
            for j in range(w_ref.shape[0]):
                y = lax.dot_general(
                    w_ref[j],
                    joined,
                    (((1,), (1,)), ((), ())),
                    preferred_element_type=jnp.float32,
                )
                out = out_refs[j] if len(out_refs) > 1 else out_refs[0].at[j]
                half = w_ref.shape[1] // 2
                for parity in range(2):
                    for r in range(positions // LANES):
                        out[parity, r] = y[
                            parity * half : (parity + 1) * half, r * LANES : (r + 1) * LANES
                        ].astype(out.dtype)


def attention_call(q, pairs, state, w=None, own_apart=False):
    positions, features = q.shape
    tiles = features // LANES
    final = w is not None
    carry = pl.BlockSpec((1, 2, positions, LANES), lambda i: (i, 0, 0, 0))
    carry_shape = jax.ShapeDtypeStruct((tiles, 2, positions, LANES), jnp.float32)
    operands = [q]
    specs = [pl.BlockSpec((positions, LANES), lambda i: (0, i))]
    for pair in pairs:
        for array, place in pair:
            operands.append(array)
            specs.append(
                pl.BlockSpec((1, positions, LANES), functools.partial(lambda p, i: (p, 0, i), place))
            )
    if state is not None:
        operands += list(state)
        specs += [carry, carry]
    scratch = []
    if final:
        operands.append(w)
        specs.append(pl.BlockSpec(w.shape, lambda i: (0, 0, 0)))
        shape = (2, positions // LANES, w.shape[1] // 2, LANES)
        if own_apart:
            out_shape = (
                jax.ShapeDtypeStruct(shape, jnp.bfloat16),
                jax.ShapeDtypeStruct(shape, jnp.float32),
            )
        else:
            out_shape = (jax.ShapeDtypeStruct((w.shape[0],) + shape, jnp.bfloat16),)
        out_specs = tuple(
            pl.BlockSpec(o.shape, functools.partial(lambda n, i: (0,) * n, len(o.shape)))
            for o in out_shape
        )
        scratch = [pltpu.VMEM((tiles, positions, LANES), jnp.bfloat16)]
    else:
        out_shape = (carry_shape, carry_shape)
        out_specs = (carry, carry)
    keys = positions * len(pairs)
    return pl.pallas_call(
        functools.partial(attention_kernel, len(pairs), state is not None, final),
        grid=(tiles,),
        in_specs=specs,
        out_specs=out_specs,
        out_shape=out_shape,
        scratch_shapes=scratch,
        compiler_params=pltpu.CompilerParams(vmem_limit_bytes=VMEM_LIMIT),
        cost_estimate=cost(1000 + 3200 * len(pairs)),
        name="attend",
    )(*operands)


def per_device(
    latent,
    stale_kv,
    timestep,
    w_time,
    gn_gain,
    gn_bias,
    conv_w,
    conv_b,
    ln_gain,
    ln_bias,
    w_qkv,
    w_out,
):
    latent_rows = latent[0]
    rows_count = lax.axis_size("rows")
    tp_count = lax.axis_size("tp")
    span_rows, local_channels, grid_width = latent_rows.shape
    positions = span_rows * grid_width
    group_width = D // GROUPS
    local_groups = local_channels // group_width
    my_block = lax.axis_index("rows")
    cfg = lax.axis_index("cfg")
    tp = lax.axis_index("tp")

    latent32 = latent_rows.astype(jnp.float32)
    values32 = latent32.reshape(span_rows, local_groups, group_width, grid_width)
    sums = jnp.stack(
        [jnp.sum(values32, axis=(0, 2, 3)), jnp.sum(values32 * values32, axis=(0, 2, 3))]
    )
    table = jnp.zeros((2, 2, GROUPS), jnp.float32)
    table = lax.dynamic_update_slice(table, sums[None], (cfg, 0, tp * local_groups))
    table = summed(table.reshape(-1), ("cfg", "rows", "tp"))

    up_pairs = [(i, i + 1) for i in range(rows_count - 1)]
    down_pairs = [(i + 1, i) for i in range(rows_count - 1)]
    before = lax.ppermute(latent_rows[span_rows - 1 :], "rows", up_pairs)
    after = lax.ppermute(latent_rows[:1], "rows", down_pairs)
    rimmed = jnp.concatenate([before, latent_rows, after], axis=0)

    x_mine, x_other = halves_of_inputs(rimmed)

    forward, backward = ring_pairs(rows_count)
    last = rows_count // 2
    pair = stale_kv[0].reshape(2, positions, -1)
    hops = [(pair, pair)]

    def next_hop(*after):
        ahead, behind = hops[-1]
        if len(hops) == last:
            ahead, behind = ahead[:1], behind[1:]
        if after:
            ahead, behind, *_ = lax.optimization_barrier((ahead, behind) + after)
        hops.append(
            (lax.ppermute(ahead, "rows", forward), lax.ppermute(behind, "rows", backward))
        )

    def blocks_of(hop):
        ahead, behind = hops[hop]
        if hop == last:
            return [((ahead, 0), (behind, 0))]
        return [((ahead, 0), (ahead, 1)), ((behind, 0), (behind, 1))]

    next_hop()

    vectors = gather_tp(jnp.stack([gn_gain, gn_bias, ln_gain, ln_bias]), 1).astype(jnp.float32)
    amount = span_rows * rows_count * grid_width * group_width
    half = D // 2
    gn_affine = lax.dynamic_slice_in_dim(vectors[:2], cfg * half, half, 1).T
    ln_affine = vectors[2:].T
    flags = jnp.stack([my_block > 0, my_block < rows_count - 1, tp == cfg]).astype(jnp.int32)
    place = cfg * (GROUPS // 2)
    flags_mine = jnp.append(flags, cfg * 2 * GROUPS + place)
    flags_other = jnp.append(flags, (1 - cfg) * 2 * GROUPS + place)

    local_features = w_qkv.shape[2]
    w_project = w_qkv.transpose(1, 0, 2)
    flip = jnp.logical_and(tp_count == 2, tp == 0)
    w_back = arrange_call(flip, w_out, tp_count)
    order = jnp.stack([tp, 1 - tp]).astype(jnp.int32) if tp_count == 2 else jnp.zeros((1,), jnp.int32)
    gn_affine, ln_affine, order, w_back = lax.optimization_barrier(
        (gn_affine, ln_affine, order, w_back)
    )

    flags_other = need(flags_other, hops[1])
    conv_sent = conv_call(flags_other, table, amount, x_other, gn_affine, conv_w, jnp.bfloat16)
    conv_received = swapped(conv_sent, "cfg")
    next_hop()
    conv_own = conv_call(flags_mine, table, amount, x_mine, gn_affine, conv_w, jnp.float32)

    half_width = TEMB // 2
    frequencies = jnp.exp(
        -math.log(10000.0) * jnp.arange(half_width, dtype=jnp.float32) / half_width
    )
    angles = timestep.astype(jnp.float32)[0] * frequencies
    embedding = jnp.concatenate([jnp.cos(angles), jnp.sin(angles)])
    time_bias = jnp.dot(
        jax.nn.silu(embedding)[None, :], w_time.astype(jnp.float32), precision=lax.Precision.HIGHEST
    )[0]
    bias = conv_b.astype(jnp.float32) + time_bias
    resid = (
        latent32 + (conv_own + conv_received.astype(jnp.float32) + bias[None, :, None])
    ).astype(jnp.bfloat16)

    if tp_count == 2:
        parts = [resid, need(swapped(resid, "tp"), hops[2])]
    else:
        parts = [lax.all_gather(resid, "tp", axis=1, tiled=True)]
    next_hop(resid)
    queries, fresh = project_call(order, parts, ln_affine, w_project)
    resid_split = split_call(resid)
    fresh_kv = fresh.reshape(1, 2, span_rows, grid_width, local_features)

    group = [((fresh, 0), (fresh, 1))] + blocks_of(1)
    state = None
    for hop in range(2, last + 1):
        state = attention_call(queries, group, state)
        while len(hops) <= last:
            next_hop(state[0])
        group = blocks_of(hop)
    if tp_count == 2:
        sent, kept_terms = attention_call(queries, group, state, w_back, True)
        terms = (kept_terms, swapped(sent, "tp"))
    else:
        (sent,) = attention_call(queries, group, state, w_back)
        terms = (lax.psum_scatter(sent, "tp", scatter_dimension=0),)

    other_branch = swapped(branch_call(1 - cfg, resid_split, terms), "cfg")
    kept = branch_call(cfg, resid_split, terms)
    is_cond = cfg == 0
    cond_out = jnp.where(is_cond, kept, other_branch).astype(jnp.float32)
    uncond_out = jnp.where(is_cond, other_branch, kept).astype(jnp.float32)
    guided = (uncond_out + guidance * (cond_out - uncond_out)).astype(jnp.bfloat16)
    return (guided[:, :, None, :], fresh_kv)


def solution(mesh):
    in_specs = (
        P("cfg", "rows", "tp", None),
        P("cfg", None, "rows", None, "tp"),
        P(),
        P(None, "tp"),
        P("tp"),
        P("tp"),
        P(None, None, "tp", "cfg"),
        P("tp"),
        P("tp"),
        P("tp"),
        P(None, None, "tp"),
        P("tp", None),
    )
    out_specs = (P("rows", "tp", "cfg", None), P("cfg", None, "rows", None, "tp"))
    return jax.shard_map(
        per_device, mesh=mesh, in_specs=in_specs, out_specs=out_specs, check_vma=False
    )
```

```python
import functools
import math

import jax
import jax.numpy as jnp
from jax import lax
from jax.experimental import pallas as pl
from jax.experimental.pallas import tpu as pltpu
from jax.sharding import PartitionSpec as P

D = 1280
HD = 64
GROUPS = 32
TEMB = 320
LANES = 128

epsilon = 1e-05
guidance = 5.0
SCORE_SCALE = 1.0 / math.sqrt(HD)
MIB = 1024 * 1024
VMEM_LIMIT = 32 * MIB
COST_SHARE = 0.02


def cost(work):
    return pl.CostEstimate(flops=int(work * 1e6 * COST_SHARE), bytes_accessed=1000, transcendentals=0)


def swapped(array, axis):
    return lax.ppermute(array, axis, [(i, i ^ 1) for i in range(lax.axis_size(axis))])


def ring_pairs(count):
    order = list(range(0, count, 2)) + list(range(count - 1, 0, -2))
    forward = [(order[i], order[(i + 1) % count]) for i in range(count)]
    backward = [(j, i) for i, j in forward]
    return forward, backward


def gather_tp(array, axis):
    if lax.axis_size("tp") != 2:
        return lax.all_gather(array, "tp", axis=axis, tiled=True)
    other = swapped(array, "tp")
    first = lax.axis_index("tp") == 0
    return jnp.concatenate(
        [jnp.where(first, array, other), jnp.where(first, other, array)], axis=axis
    )


def summed(array, axes):
    count = lax.axis_size(axes)
    spread = jnp.broadcast_to(array[None], (count,) + array.shape)
    return jnp.sum(lax.all_to_all(spread, axes, 0, 0, tiled=True), axis=0)


def need(array, others):
    return lax.optimization_barrier((array,) + tuple(others))[0]


def halves_of_inputs(own):
    cfg = lax.axis_index("cfg")
    if lax.axis_size("tp") != 2:
        full = lax.all_gather(own, "tp", axis=1, tiled=True)
        half = full.shape[1] // 2
        mine = lax.dynamic_slice_in_dim(full, cfg * half, half, 1)
        sent = lax.dynamic_slice_in_dim(full, (1 - cfg) * half, half, 1)
        return [mine], [swapped(sent, "cfg")]
    across = lax.ppermute(own, ("cfg", "tp"), [(1, 3), (2, 0)])
    pairs = [(0, 1), (3, 2)]
    own_side = lax.ppermute(own, ("cfg", "tp"), pairs)
    across_side = lax.ppermute(across, ("cfg", "tp"), pairs)
    return [own, own_side], [across, across_side]


def conv_kernel(choices, amount, flags_ref, sums_ref, *refs):
    x_refs = refs[:choices]
    affine_ref, w_hbm, out_ref, w_ref, act_ref, sems = refs[choices:]
    rows = out_ref.shape[0]
    ins = affine_ref.shape[0]
    copies = {}
    for b in (1, 0, 2):
        for a in range(3):
            copies[a, b] = pltpu.make_async_copy(
                w_hbm.at[a, b], w_ref.at[b, :, a * ins : (a + 1) * ins], sems.at[a, b]
            )
            copies[a, b].start()

    groups = ins // (D // GROUPS)
    base = flags_ref[3]

    def column(offset):
        return jnp.concatenate(
            [jnp.full((D // GROUPS, 1), sums_ref[base + offset + g], jnp.float32) for g in range(groups)],
            axis=0,
        )

    mean = column(0) / amount
    variance = column(GROUPS) / amount - mean * mean
    scale = lax.rsqrt(variance + epsilon) * affine_ref[:, 0:1]
    shift = affine_ref[:, 1:2]
    for r in range(rows + 2):
        x = x_refs[0][r]
        if choices == 2:
            x = jnp.where(flags_ref[2] == 1, x, x_refs[1][r])
        z = ((x.astype(jnp.float32) - mean) * scale + shift) * 0.5
        z = z + z * jnp.tanh(z)
        if r == 0:
            z = jnp.where(flags_ref[0] == 1, z, 0.0)
        if r == rows + 1:
            z = jnp.where(flags_ref[1] == 1, z, 0.0)
        z = z.astype(jnp.bfloat16)
        for a in range(3):
            if 0 <= r - a < rows:
                act_ref[a * ins : (a + 1) * ins, (r - a) * LANES : (r - a + 1) * LANES] = z

    width = min(2, rows)
    lane = lax.broadcasted_iota(jnp.int32, (out_ref.shape[1], LANES), 1)
    for start in range(0, rows, width):
        cols = slice(start * LANES, (start + width) * LANES)
        total = [0.0] * width
        for b in (1, 0, 2):
            if start == 0:
                for a in range(3):
                    copies[a, b].wait()
            y = jnp.dot(w_ref[b], act_ref[:, cols], preferred_element_type=jnp.float32)
            for r in range(width):
                part = y[:, r * LANES : (r + 1) * LANES]
                if b == 0:
                    part = jnp.where(lane == 0, 0.0, pltpu.roll(part, 1, axis=1))
                if b == 2:
                    part = jnp.where(lane == LANES - 1, 0.0, pltpu.roll(part, LANES - 1, axis=1))
                total[r] = total[r] + part
        for r in range(width):
            out_ref[start + r] = total[r].astype(out_ref.dtype)


def conv_call(flags, sums, amount, xs, affine, conv_w, out_dtype):
    x = xs[0]
    rows = x.shape[0] - 2
    outs, ins = conv_w.shape[2:]
    return pl.pallas_call(
        functools.partial(conv_kernel, len(xs), amount),
        in_specs=[
            pl.BlockSpec(memory_space=pltpu.SMEM),
            pl.BlockSpec(memory_space=pltpu.SMEM),
            *[pl.BlockSpec(memory_space=pltpu.VMEM)] * (len(xs) + 1),
            pl.BlockSpec(memory_space=pltpu.HBM),
        ],
        out_specs=pl.BlockSpec(memory_space=pltpu.VMEM),
        out_shape=jax.ShapeDtypeStruct((rows, outs, LANES), out_dtype),
        scratch_shapes=[
            pltpu.VMEM((3, outs, 3 * ins), jnp.bfloat16),
            pltpu.VMEM((3 * ins, rows * LANES), jnp.bfloat16),
            pltpu.SemaphoreType.DMA((3, 3)),
        ],
        compiler_params=pltpu.CompilerParams(vmem_limit_bytes=57 * MIB),
        cost_estimate=cost(9000),
        name="norm_conv",
    )(flags, sums, *xs, affine, conv_w)


def parity_matrix(channels):
    half = channels // 2
    to = lax.broadcasted_iota(jnp.int32, (channels, channels), 0)
    source = lax.broadcasted_iota(jnp.int32, (channels, channels), 1)
    wanted = jnp.where(to < half, 2 * to, 2 * (to - half) + 1)
    return (source == wanted).astype(jnp.bfloat16)


def split_kernel(own_ref, split_ref):
    rows, channels, _ = own_ref.shape
    half = channels // 2
    chosen = parity_matrix(channels)
    for r in range(rows):
        y = jnp.dot(chosen, own_ref[r], preferred_element_type=jnp.float32).astype(jnp.bfloat16)
        split_ref[0, r] = y[:half]
        split_ref[1, r] = y[half:]


def split_call(own):
    rows, channels, _ = own.shape
    return pl.pallas_call(
        split_kernel,
        in_specs=[pl.BlockSpec(memory_space=pltpu.VMEM)],
        out_specs=pl.BlockSpec(memory_space=pltpu.VMEM),
        out_shape=jax.ShapeDtypeStruct((2, rows, channels // 2, LANES), jnp.bfloat16),
        compiler_params=pltpu.CompilerParams(vmem_limit_bytes=VMEM_LIMIT),
        cost_estimate=cost(1000),
        name="parity_split",
    )(own)


def arrange_kernel(flip_ref, w_ref, out_ref):
    count, channels, _ = out_ref.shape
    chosen = parity_matrix(channels)
    for i in range(count):
        y = lax.dot_general(
            chosen,
            w_ref[:, i * channels : (i + 1) * channels],
            (((1,), (1,)), ((), ())),
            preferred_element_type=jnp.float32,
        )
        out_ref[jnp.where(flip_ref[0] == 1, count - 1 - i, i)] = y.astype(jnp.bfloat16)


def arrange_call(flip, w_out, count):
    features, channels = w_out.shape
    return pl.pallas_call(
        arrange_kernel,
        in_specs=[
            pl.BlockSpec(memory_space=pltpu.SMEM),
            pl.BlockSpec(memory_space=pltpu.VMEM),
        ],
        out_specs=pl.BlockSpec(memory_space=pltpu.VMEM),
        out_shape=jax.ShapeDtypeStruct((count, channels // count, features), jnp.bfloat16),
        compiler_params=pltpu.CompilerParams(vmem_limit_bytes=VMEM_LIMIT),
        cost_estimate=cost(2000),
        name="arrange",
    )(flip.astype(jnp.int32).reshape(1), w_out)


def project_kernel(parts, order_ref, *refs):
    part_refs = refs[:parts]
    affine_ref, w_hbm, q_ref, kv_ref, w_ref, normed_ref, sems = refs[parts:]
    rows, channels, _ = part_refs[0].shape
    total = parts * channels
    copies = [pltpu.make_async_copy(w_hbm.at[i], w_ref.at[i], sems.at[i]) for i in range(3)]
    for copy in copies:
        copy.start()
    for r in range(rows):
        x = [ref[r].astype(jnp.float32) for ref in part_refs]
        mean = sum(jnp.sum(a, axis=0, keepdims=True) for a in x) / total
        var = sum(jnp.sum(a * a, axis=0, keepdims=True) for a in x) / total - mean * mean
        inverse = lax.rsqrt(var + epsilon)
        for j in range(parts):
            at = pl.ds(pl.multiple_of(order_ref[j] * channels, LANES), channels)
            z = (x[j] - mean) * inverse * affine_ref[at, 0:1] + affine_ref[at, 1:2]
            normed_ref[r * LANES : (r + 1) * LANES, at] = z.astype(jnp.bfloat16).T
    for i in range(3):
        copies[i].wait()
        y = jnp.dot(normed_ref[...], w_ref[i], preferred_element_type=jnp.float32)
        y = y.astype(jnp.bfloat16)
        if i == 0:
            q_ref[...] = y * SCORE_SCALE
        else:
            kv_ref[i - 1] = y


def project_call(order, parts, affine, w):
    rows = parts[0].shape[0]
    positions = rows * LANES
    _, depth, features = w.shape
    vmem = pl.BlockSpec(memory_space=pltpu.VMEM)
    return pl.pallas_call(
        functools.partial(project_kernel, len(parts)),
        in_specs=[
            pl.BlockSpec(memory_space=pltpu.SMEM),
            *[vmem] * (len(parts) + 1),
            pl.BlockSpec(memory_space=pltpu.HBM),
        ],
        out_specs=(vmem, vmem),
        out_shape=(
            jax.ShapeDtypeStruct((positions, features), jnp.bfloat16),
            jax.ShapeDtypeStruct((2, positions, features), jnp.bfloat16),
        ),
        scratch_shapes=[
            pltpu.VMEM((3, depth, features), jnp.bfloat16),
            pltpu.VMEM((positions, depth), jnp.bfloat16),
            pltpu.SemaphoreType.DMA((3,)),
        ],
        compiler_params=pltpu.CompilerParams(vmem_limit_bytes=55 * MIB),
        cost_estimate=cost(6500),
        name="norm_project",
    )(order, *parts, affine, w)


def branch_kernel(parity_ref, resid_ref, *refs):
    total = resid_ref[0].astype(jnp.float32)
    for ref in refs[:-1]:
        total = total + ref[0].astype(jnp.float32)
    refs[-1][...] = total.astype(jnp.bfloat16)


def branch_call(parity, resid_split, terms):
    shape = resid_split.shape
    block = pl.BlockSpec((1,) + shape[1:], lambda i, parity: (parity[0], 0, 0, 0))
    return pl.pallas_call(
        branch_kernel,
        grid_spec=pltpu.PrefetchScalarGridSpec(
            num_scalar_prefetch=1,
            grid=(1,),
            in_specs=[block] * (1 + len(terms)),
            out_specs=pl.BlockSpec(shape[1:], lambda i, parity: (0, 0, 0)),
        ),
        out_shape=jax.ShapeDtypeStruct(shape[1:], jnp.bfloat16),
        compiler_params=pltpu.CompilerParams(vmem_limit_bytes=VMEM_LIMIT),
        cost_estimate=cost(1000),
        name="branch_out",
    )(parity.astype(jnp.int32).reshape(1), resid_split, *terms)


def attention_kernel(blocks, carried, final, *refs):
    q_ref = refs[0]
    kv_refs = refs[1 : 1 + 2 * blocks]
    at = 1 + 2 * blocks
    if carried:
        m_in, acc_in = refs[at : at + 2]
        at += 2
    if final:
        w_ref = refs[at]
        at += 1
        out_refs = refs[at:-1]
        joined_ref = refs[-1]
    else:
        m_out, acc_out = refs[at:]
    positions = q_ref.shape[0]
    tile = min(256, positions)
    starts = range(0, positions, tile)
    lanes = lambda array, low: (lax.broadcasted_iota(jnp.int32, array.shape, 1) < HD) == low

    def scores(item):
        start, head, block = item
        q = q_ref[start : start + tile, :]
        q = jnp.where(lanes(q, head == 0), q, jnp.zeros_like(q))
        return lax.dot_general(
            q,
            kv_refs[2 * block][0],
            (((1,), (1,)), ((), ())),
            preferred_element_type=jnp.float32,
        )

    items = [(start, head, block) for start in starts for block in range(blocks) for head in (0, 1)]
    state = {}
    upcoming = scores(items[0])
    for number, item in enumerate(items):
        s = upcoming
        if number + 1 < len(items):
            upcoming = scores(items[number + 1])
        start, head, block = item
        rows = slice(start, start + tile)
        if block == 0 and carried:
            peak, acc = m_in[0, head, rows, :], acc_in[0, head, rows, :]
        elif block == 0:
            peak = acc = None
        else:
            peak, acc = state[start, head]
        v = kv_refs[2 * block + 1][0]
        v = jnp.where(lanes(v, head == 0), v, jnp.ones_like(v))
        top = jnp.broadcast_to(jnp.max(s, axis=1, keepdims=True), (tile, LANES))
        new_peak = top if peak is None else jnp.maximum(peak, top)
        wide = jnp.concatenate([new_peak] * (s.shape[1] // LANES), axis=1)
        p = jnp.exp(s - wide).astype(jnp.bfloat16)
        term = jnp.dot(p, v, preferred_element_type=jnp.float32)
        acc = term if acc is None else acc * jnp.exp(peak - new_peak) + term
        state[start, head] = new_peak, acc
        if block < blocks - 1:
            continue
        if not final:
            m_out[0, head, rows, :] = new_peak
            acc_out[0, head, rows, :] = acc
        elif head == 1:
            parts = [state[start, h][1] for h in (0, 1)]
            parts = [a / pltpu.roll(a, HD, axis=1) for a in parts]
            pair = jnp.where(lanes(acc, True), parts[0], parts[1]).astype(jnp.bfloat16)
            joined_ref[pl.program_id(0), rows, :] = pair

    if final:
        tiles, _, _ = joined_ref.shape

        @pl.when(pl.program_id(0) == tiles - 1)
        def _():
            joined = jnp.concatenate([joined_ref[i] for i in range(tiles)], axis=1)
            for j in range(w_ref.shape[0]):
                y = lax.dot_general(
                    w_ref[j],
                    joined,
                    (((1,), (1,)), ((), ())),
                    preferred_element_type=jnp.float32,
                )
                out = out_refs[j] if len(out_refs) > 1 else out_refs[0].at[j]
                half = w_ref.shape[1] // 2
                for parity in range(2):
                    for r in range(positions // LANES):
                        out[parity, r] = y[
                            parity * half : (parity + 1) * half, r * LANES : (r + 1) * LANES
                        ].astype(out.dtype)


def attention_call(q, pairs, state, w=None, own_apart=False):
    positions, features = q.shape
    tiles = features // LANES
    final = w is not None
    carry = pl.BlockSpec((1, 2, positions, LANES), lambda i: (i, 0, 0, 0))
    carry_shape = jax.ShapeDtypeStruct((tiles, 2, positions, LANES), jnp.float32)
    operands = [q]
    specs = [pl.BlockSpec((positions, LANES), lambda i: (0, i))]
    for pair in pairs:
        for array, place in pair:
            operands.append(array)
            specs.append(
                pl.BlockSpec((1, positions, LANES), functools.partial(lambda p, i: (p, 0, i), place))
            )
    if state is not None:
        operands += list(state)
        specs += [carry, carry]
    scratch = []
    if final:
        operands.append(w)
        specs.append(pl.BlockSpec(w.shape, lambda i: (0, 0, 0)))
        shape = (2, positions // LANES, w.shape[1] // 2, LANES)
        if own_apart:
            out_shape = (
                jax.ShapeDtypeStruct(shape, jnp.bfloat16),
                jax.ShapeDtypeStruct(shape, jnp.float32),
            )
        else:
            out_shape = (jax.ShapeDtypeStruct((w.shape[0],) + shape, jnp.bfloat16),)
        out_specs = tuple(
            pl.BlockSpec(o.shape, functools.partial(lambda n, i: (0,) * n, len(o.shape)))
            for o in out_shape
        )
        scratch = [pltpu.VMEM((tiles, positions, LANES), jnp.bfloat16)]
    else:
        out_shape = (carry_shape, carry_shape)
        out_specs = (carry, carry)
    keys = positions * len(pairs)
    return pl.pallas_call(
        functools.partial(attention_kernel, len(pairs), state is not None, final),
        grid=(tiles,),
        in_specs=specs,
        out_specs=out_specs,
        out_shape=out_shape,
        scratch_shapes=scratch,
        compiler_params=pltpu.CompilerParams(vmem_limit_bytes=VMEM_LIMIT),
        cost_estimate=cost(1000 + 3200 * len(pairs)),
        name="attend",
    )(*operands)


def per_device(
    latent,
    stale_kv,
    timestep,
    w_time,
    gn_gain,
    gn_bias,
    conv_w,
    conv_b,
    ln_gain,
    ln_bias,
    w_qkv,
    w_out,
):
    latent_rows = latent[0]
    rows_count = lax.axis_size("rows")
    tp_count = lax.axis_size("tp")
    span_rows, local_channels, grid_width = latent_rows.shape
    positions = span_rows * grid_width
    group_width = D // GROUPS
    local_groups = local_channels // group_width
    my_block = lax.axis_index("rows")
    cfg = lax.axis_index("cfg")
    tp = lax.axis_index("tp")

    latent32 = latent_rows.astype(jnp.float32)
    values32 = latent32.reshape(span_rows, local_groups, group_width, grid_width)
    sums = jnp.stack(
        [jnp.sum(values32, axis=(0, 2, 3)), jnp.sum(values32 * values32, axis=(0, 2, 3))]
    )
    table = jnp.zeros((2, 2, GROUPS), jnp.float32)
    table = lax.dynamic_update_slice(table, sums[None], (cfg, 0, tp * local_groups))
    table = summed(table.reshape(-1), ("cfg", "rows", "tp"))

    up_pairs = [(i, i + 1) for i in range(rows_count - 1)]
    down_pairs = [(i + 1, i) for i in range(rows_count - 1)]
    before = lax.ppermute(latent_rows[span_rows - 1 :], "rows", up_pairs)
    after = lax.ppermute(latent_rows[:1], "rows", down_pairs)
    rimmed = jnp.concatenate([before, latent_rows, after], axis=0)

    x_mine, x_other = halves_of_inputs(rimmed)

    forward, backward = ring_pairs(rows_count)
    last = rows_count // 2
    pair = stale_kv[0].reshape(2, positions, -1)
    hops = [(pair, pair)]

    def next_hop(*after):
        ahead, behind = hops[-1]
        if len(hops) == last:
            ahead, behind = ahead[:1], behind[1:]
        if after:
            ahead, behind, *_ = lax.optimization_barrier((ahead, behind) + after)
        hops.append(
            (lax.ppermute(ahead, "rows", forward), lax.ppermute(behind, "rows", backward))
        )

    def blocks_of(hop):
        ahead, behind = hops[hop]
        if hop == last:
            return [((ahead, 0), (behind, 0))]
        return [((ahead, 0), (ahead, 1)), ((behind, 0), (behind, 1))]

    next_hop()

    vectors = gather_tp(jnp.stack([gn_gain, gn_bias, ln_gain, ln_bias]), 1).astype(jnp.float32)
    amount = span_rows * rows_count * grid_width * group_width
    half = D // 2
    gn_affine = lax.dynamic_slice_in_dim(vectors[:2], cfg * half, half, 1).T
    ln_affine = vectors[2:].T
    flags = jnp.stack([my_block > 0, my_block < rows_count - 1, tp == cfg]).astype(jnp.int32)
    place = cfg * (GROUPS // 2)
    flags_mine = jnp.append(flags, cfg * 2 * GROUPS + place)
    flags_other = jnp.append(flags, (1 - cfg) * 2 * GROUPS + place)

    local_features = w_qkv.shape[2]
    w_project = w_qkv.transpose(1, 0, 2)
    flip = jnp.logical_and(tp_count == 2, tp == 0)
    w_back = arrange_call(flip, w_out, tp_count)
    order = jnp.stack([tp, 1 - tp]).astype(jnp.int32) if tp_count == 2 else jnp.zeros((1,), jnp.int32)
    gn_affine, ln_affine, order, w_back = lax.optimization_barrier(
        (gn_affine, ln_affine, order, w_back)
    )

    flags_other = need(flags_other, hops[1])
    conv_sent = conv_call(flags_other, table, amount, x_other, gn_affine, conv_w, jnp.bfloat16)
    conv_received = swapped(conv_sent, "cfg")
    next_hop()
    conv_own = conv_call(flags_mine, table, amount, x_mine, gn_affine, conv_w, jnp.float32)

    half_width = TEMB // 2
    frequencies = jnp.exp(
        -math.log(10000.0) * jnp.arange(half_width, dtype=jnp.float32) / half_width
    )
    angles = timestep.astype(jnp.float32)[0] * frequencies
    embedding = jnp.concatenate([jnp.cos(angles), jnp.sin(angles)])
    time_bias = jnp.dot(
        jax.nn.silu(embedding)[None, :], w_time.astype(jnp.float32), precision=lax.Precision.HIGHEST
    )[0]
    bias = conv_b.astype(jnp.float32) + time_bias
    resid = (
        latent32 + (conv_own + conv_received.astype(jnp.float32) + bias[None, :, None])
    ).astype(jnp.bfloat16)

    if tp_count == 2:
        parts = [resid, need(swapped(resid, "tp"), hops[2])]
    else:
        parts = [lax.all_gather(resid, "tp", axis=1, tiled=True)]
    next_hop(resid)
    queries, fresh = project_call(order, parts, ln_affine, w_project)
    resid_split = split_call(resid)
    fresh_kv = fresh.reshape(1, 2, span_rows, grid_width, local_features)

    group = [((fresh, 0), (fresh, 1))] + blocks_of(1)
    state = None
    for hop in range(2, last + 1):
        if hop == 3:
            group = group + blocks_of(3)
            continue
        state = attention_call(queries, group, state)
        while len(hops) <= last:
            next_hop(state[0])
        group = blocks_of(hop)
    if tp_count == 2:
        sent, kept_terms = attention_call(queries, group, state, w_back, True)
        terms = (kept_terms, swapped(sent, "tp"))
    else:
        (sent,) = attention_call(queries, group, state, w_back)
        terms = (lax.psum_scatter(sent, "tp", scatter_dimension=0),)

    other_branch = swapped(branch_call(1 - cfg, resid_split, terms), "cfg")
    kept = branch_call(cfg, resid_split, terms)
    is_cond = cfg == 0
    cond_out = jnp.where(is_cond, kept, other_branch).astype(jnp.float32)
    uncond_out = jnp.where(is_cond, other_branch, kept).astype(jnp.float32)
    guided = (uncond_out + guidance * (cond_out - uncond_out)).astype(jnp.bfloat16)
    return (guided[:, :, None, :], fresh_kv)


def solution(mesh):
    in_specs = (
        P("cfg", "rows", "tp", None),
        P("cfg", None, "rows", None, "tp"),
        P(),
        P(None, "tp"),
        P("tp"),
        P("tp"),
        P(None, None, "tp", "cfg"),
        P("tp"),
        P("tp"),
        P("tp"),
        P(None, None, "tp"),
        P("tp", None),
    )
    out_specs = (P("rows", "tp", "cfg", None), P("cfg", None, "rows", None, "tp"))
    return jax.shard_map(
        per_device, mesh=mesh, in_specs=in_specs, out_specs=out_specs, check_vma=False
    )
```

```python
import functools
import math

import jax
import jax.numpy as jnp
from jax import lax
from jax.experimental import pallas as pl
from jax.experimental.pallas import tpu as pltpu
from jax.sharding import PartitionSpec as P

D = 1280
HD = 64
GROUPS = 32
TEMB = 320
LANES = 128

epsilon = 1e-05
guidance = 5.0
SCORE_SCALE = 1.0 / math.sqrt(HD)
MIB = 1024 * 1024
VMEM_LIMIT = 32 * MIB
COST_SHARE = 0.02


def cost(work):
    return pl.CostEstimate(flops=int(work * 1e6 * COST_SHARE), bytes_accessed=1000, transcendentals=0)


def swapped(array, axis):
    return lax.ppermute(array, axis, [(i, i ^ 1) for i in range(lax.axis_size(axis))])


def ring_pairs(count):
    order = list(range(0, count, 2)) + list(range(count - 1, 0, -2))
    forward = [(order[i], order[(i + 1) % count]) for i in range(count)]
    backward = [(j, i) for i, j in forward]
    return forward, backward


def gather_tp(array, axis):
    if lax.axis_size("tp") != 2:
        return lax.all_gather(array, "tp", axis=axis, tiled=True)
    other = swapped(array, "tp")
    first = lax.axis_index("tp") == 0
    return jnp.concatenate(
        [jnp.where(first, array, other), jnp.where(first, other, array)], axis=axis
    )


def summed(array, axes):
    count = lax.axis_size(axes)
    spread = jnp.broadcast_to(array[None], (count,) + array.shape)
    return jnp.sum(lax.all_to_all(spread, axes, 0, 0, tiled=True), axis=0)


def need(array, others):
    return lax.optimization_barrier((array,) + tuple(others))[0]


def halves_of_inputs(own):
    cfg = lax.axis_index("cfg")
    if lax.axis_size("tp") != 2:
        full = lax.all_gather(own, "tp", axis=1, tiled=True)
        half = full.shape[1] // 2
        mine = lax.dynamic_slice_in_dim(full, cfg * half, half, 1)
        sent = lax.dynamic_slice_in_dim(full, (1 - cfg) * half, half, 1)
        return [mine], [swapped(sent, "cfg")]
    across = lax.ppermute(own, ("cfg", "tp"), [(1, 3), (2, 0)])
    pairs = [(0, 1), (3, 2)]
    own_side = lax.ppermute(own, ("cfg", "tp"), pairs)
    across_side = lax.ppermute(across, ("cfg", "tp"), pairs)
    return [own, own_side], [across, across_side]


def conv_kernel(choices, amount, flags_ref, sums_ref, *refs):
    x_refs = refs[:choices]
    affine_ref, w_hbm, out_ref, w_ref, act_ref, sems = refs[choices:]
    rows = out_ref.shape[0]
    ins = affine_ref.shape[0]
    copies = {}
    for b in (1, 0, 2):
        for a in range(3):
            copies[a, b] = pltpu.make_async_copy(
                w_hbm.at[a, b], w_ref.at[b, :, a * ins : (a + 1) * ins], sems.at[a, b]
            )
            copies[a, b].start()

    groups = ins // (D // GROUPS)
    base = flags_ref[3]

    def column(offset):
        return jnp.concatenate(
            [jnp.full((D // GROUPS, 1), sums_ref[base + offset + g], jnp.float32) for g in range(groups)],
            axis=0,
        )

    mean = column(0) / amount
    variance = column(GROUPS) / amount - mean * mean
    scale = lax.rsqrt(variance + epsilon) * affine_ref[:, 0:1]
    shift = affine_ref[:, 1:2]
    for r in range(rows + 2):
        x = x_refs[0][r]
        if choices == 2:
            x = jnp.where(flags_ref[2] == 1, x, x_refs[1][r])
        z = ((x.astype(jnp.float32) - mean) * scale + shift) * 0.5
        z = z + z * jnp.tanh(z)
        if r == 0:
            z = jnp.where(flags_ref[0] == 1, z, 0.0)
        if r == rows + 1:
            z = jnp.where(flags_ref[1] == 1, z, 0.0)
        z = z.astype(jnp.bfloat16)
        for a in range(3):
            if 0 <= r - a < rows:
                act_ref[a * ins : (a + 1) * ins, (r - a) * LANES : (r - a + 1) * LANES] = z

    width = min(2, rows)
    lane = lax.broadcasted_iota(jnp.int32, (out_ref.shape[1], LANES), 1)
    for start in range(0, rows, width):
        cols = slice(start * LANES, (start + width) * LANES)
        total = [0.0] * width
        for b in (1, 0, 2):
            if start == 0:
                for a in range(3):
                    copies[a, b].wait()
            y = jnp.dot(w_ref[b], act_ref[:, cols], preferred_element_type=jnp.float32)
            for r in range(width):
                part = y[:, r * LANES : (r + 1) * LANES]
                if b == 0:
                    part = jnp.where(lane == 0, 0.0, pltpu.roll(part, 1, axis=1))
                if b == 2:
                    part = jnp.where(lane == LANES - 1, 0.0, pltpu.roll(part, LANES - 1, axis=1))
                total[r] = total[r] + part
        for r in range(width):
            out_ref[start + r] = total[r].astype(out_ref.dtype)


def conv_call(flags, sums, amount, xs, affine, conv_w, out_dtype):
    x = xs[0]
    rows = x.shape[0] - 2
    outs, ins = conv_w.shape[2:]
    return pl.pallas_call(
        functools.partial(conv_kernel, len(xs), amount),
        in_specs=[
            pl.BlockSpec(memory_space=pltpu.SMEM),
            pl.BlockSpec(memory_space=pltpu.SMEM),
            *[pl.BlockSpec(memory_space=pltpu.VMEM)] * (len(xs) + 1),
            pl.BlockSpec(memory_space=pltpu.HBM),
        ],
        out_specs=pl.BlockSpec(memory_space=pltpu.VMEM),
        out_shape=jax.ShapeDtypeStruct((rows, outs, LANES), out_dtype),
        scratch_shapes=[
            pltpu.VMEM((3, outs, 3 * ins), jnp.bfloat16),
            pltpu.VMEM((3 * ins, rows * LANES), jnp.bfloat16),
            pltpu.SemaphoreType.DMA((3, 3)),
        ],
        compiler_params=pltpu.CompilerParams(vmem_limit_bytes=57 * MIB),
        cost_estimate=cost(9000),
        name="norm_conv",
    )(flags, sums, *xs, affine, conv_w)


def parity_matrix(channels):
    half = channels // 2
    to = lax.broadcasted_iota(jnp.int32, (channels, channels), 0)
    source = lax.broadcasted_iota(jnp.int32, (channels, channels), 1)
    wanted = jnp.where(to < half, 2 * to, 2 * (to - half) + 1)
    return (source == wanted).astype(jnp.bfloat16)


def split_kernel(own_ref, split_ref):
    rows, channels, _ = own_ref.shape
    half = channels // 2
    chosen = parity_matrix(channels)
    for r in range(rows):
        y = jnp.dot(chosen, own_ref[r], preferred_element_type=jnp.float32).astype(jnp.bfloat16)
        split_ref[0, r] = y[:half]
        split_ref[1, r] = y[half:]


def split_call(own):
    rows, channels, _ = own.shape
    return pl.pallas_call(
        split_kernel,
        in_specs=[pl.BlockSpec(memory_space=pltpu.VMEM)],
        out_specs=pl.BlockSpec(memory_space=pltpu.VMEM),
        out_shape=jax.ShapeDtypeStruct((2, rows, channels // 2, LANES), jnp.bfloat16),
        compiler_params=pltpu.CompilerParams(vmem_limit_bytes=VMEM_LIMIT),
        cost_estimate=cost(1000),
        name="parity_split",
    )(own)


def arrange_kernel(flip_ref, w_ref, out_ref):
    count, channels, _ = out_ref.shape
    chosen = parity_matrix(channels)
    for i in range(count):
        y = lax.dot_general(
            chosen,
            w_ref[:, i * channels : (i + 1) * channels],
            (((1,), (1,)), ((), ())),
            preferred_element_type=jnp.float32,
        )
        out_ref[jnp.where(flip_ref[0] == 1, count - 1 - i, i)] = y.astype(jnp.bfloat16)


def arrange_call(flip, w_out, count):
    features, channels = w_out.shape
    return pl.pallas_call(
        arrange_kernel,
        in_specs=[
            pl.BlockSpec(memory_space=pltpu.SMEM),
            pl.BlockSpec(memory_space=pltpu.VMEM),
        ],
        out_specs=pl.BlockSpec(memory_space=pltpu.VMEM),
        out_shape=jax.ShapeDtypeStruct((count, channels // count, features), jnp.bfloat16),
        compiler_params=pltpu.CompilerParams(vmem_limit_bytes=VMEM_LIMIT),
        cost_estimate=cost(2000),
        name="arrange",
    )(flip.astype(jnp.int32).reshape(1), w_out)


def project_kernel(parts, order_ref, *refs):
    part_refs = refs[:parts]
    affine_ref, w_hbm, q_ref, kv_ref, w_ref, normed_ref, sems = refs[parts:]
    rows, channels, _ = part_refs[0].shape
    total = parts * channels
    copies = [pltpu.make_async_copy(w_hbm.at[i], w_ref.at[i], sems.at[i]) for i in range(3)]
    for copy in copies:
        copy.start()
    for r in range(rows):
        x = [ref[r].astype(jnp.float32) for ref in part_refs]
        mean = sum(jnp.sum(a, axis=0, keepdims=True) for a in x) / total
        var = sum(jnp.sum(a * a, axis=0, keepdims=True) for a in x) / total - mean * mean
        inverse = lax.rsqrt(var + epsilon)
        for j in range(parts):
            at = pl.ds(pl.multiple_of(order_ref[j] * channels, LANES), channels)
            z = (x[j] - mean) * inverse * affine_ref[at, 0:1] + affine_ref[at, 1:2]
            normed_ref[r * LANES : (r + 1) * LANES, at] = z.astype(jnp.bfloat16).T
    for i in range(3):
        copies[i].wait()
        y = jnp.dot(normed_ref[...], w_ref[i], preferred_element_type=jnp.float32)
        y = y.astype(jnp.bfloat16)
        if i == 0:
            q_ref[...] = y * SCORE_SCALE
        else:
            kv_ref[i - 1] = y


def project_call(order, parts, affine, w):
    rows = parts[0].shape[0]
    positions = rows * LANES
    _, depth, features = w.shape
    vmem = pl.BlockSpec(memory_space=pltpu.VMEM)
    return pl.pallas_call(
        functools.partial(project_kernel, len(parts)),
        in_specs=[
            pl.BlockSpec(memory_space=pltpu.SMEM),
            *[vmem] * (len(parts) + 1),
            pl.BlockSpec(memory_space=pltpu.HBM),
        ],
        out_specs=(vmem, vmem),
        out_shape=(
            jax.ShapeDtypeStruct((positions, features), jnp.bfloat16),
            jax.ShapeDtypeStruct((2, positions, features), jnp.bfloat16),
        ),
        scratch_shapes=[
            pltpu.VMEM((3, depth, features), jnp.bfloat16),
            pltpu.VMEM((positions, depth), jnp.bfloat16),
            pltpu.SemaphoreType.DMA((3,)),
        ],
        compiler_params=pltpu.CompilerParams(vmem_limit_bytes=55 * MIB),
        cost_estimate=cost(6500),
        name="norm_project",
    )(order, *parts, affine, w)


def branch_kernel(parity_ref, resid_ref, *refs):
    total = resid_ref[0].astype(jnp.float32)
    for ref in refs[:-1]:
        total = total + ref[0].astype(jnp.float32)
    refs[-1][...] = total.astype(jnp.bfloat16)


def branch_call(parity, resid_split, terms):
    shape = resid_split.shape
    block = pl.BlockSpec((1,) + shape[1:], lambda i, parity: (parity[0], 0, 0, 0))
    return pl.pallas_call(
        branch_kernel,
        grid_spec=pltpu.PrefetchScalarGridSpec(
            num_scalar_prefetch=1,
            grid=(1,),
            in_specs=[block] * (1 + len(terms)),
            out_specs=pl.BlockSpec(shape[1:], lambda i, parity: (0, 0, 0)),
        ),
        out_shape=jax.ShapeDtypeStruct(shape[1:], jnp.bfloat16),
        compiler_params=pltpu.CompilerParams(vmem_limit_bytes=VMEM_LIMIT),
        cost_estimate=cost(1000),
        name="branch_out",
    )(parity.astype(jnp.int32).reshape(1), resid_split, *terms)


def attention_kernel(blocks, carried, final, *refs):
    q_ref = refs[0]
    kv_refs = refs[1 : 1 + 2 * blocks]
    at = 1 + 2 * blocks
    if carried:
        m_in, acc_in = refs[at : at + 2]
        at += 2
    if final:
        w_ref = refs[at]
        at += 1
        out_refs = refs[at:-1]
        joined_ref = refs[-1]
    else:
        m_out, acc_out = refs[at:]
    positions = q_ref.shape[0]
    tile = min(512, positions)
    starts = range(0, positions, tile)
    lanes = lambda array, low: (lax.broadcasted_iota(jnp.int32, array.shape, 1) < HD) == low

    def scores(item):
        start, head, block = item
        q = q_ref[start : start + tile, :]
        q = jnp.where(lanes(q, head == 0), q, jnp.zeros_like(q))
        return lax.dot_general(
            q,
            kv_refs[2 * block][0],
            (((1,), (1,)), ((), ())),
            preferred_element_type=jnp.float32,
        )

    items = [(start, head, block) for start in starts for block in range(blocks) for head in (0, 1)]
    state = {}
    upcoming = scores(items[0])
    for number, item in enumerate(items):
        s = upcoming
        if number + 1 < len(items):
            upcoming = scores(items[number + 1])
        start, head, block = item
        rows = slice(start, start + tile)
        if block == 0 and carried:
            peak, acc = m_in[0, head, rows, :], acc_in[0, head, rows, :]
        elif block == 0:
            peak = acc = None
        else:
            peak, acc = state[start, head]
        v = kv_refs[2 * block + 1][0]
        v = jnp.where(lanes(v, head == 0), v, jnp.ones_like(v))
        top = jnp.broadcast_to(jnp.max(s, axis=1, keepdims=True), (tile, LANES))
        new_peak = top if peak is None else jnp.maximum(peak, top)
        wide = jnp.concatenate([new_peak] * (s.shape[1] // LANES), axis=1)
        p = jnp.exp(s - wide).astype(jnp.bfloat16)
        term = jnp.dot(p, v, preferred_element_type=jnp.float32)
        acc = term if acc is None else acc * jnp.exp(peak - new_peak) + term
        state[start, head] = new_peak, acc
        if block < blocks - 1:
            continue
        if not final:
            m_out[0, head, rows, :] = new_peak
            acc_out[0, head, rows, :] = acc
        elif head == 1:
            parts = [state[start, h][1] for h in (0, 1)]
            parts = [a / pltpu.roll(a, HD, axis=1) for a in parts]
            pair = jnp.where(lanes(acc, True), parts[0], parts[1]).astype(jnp.bfloat16)
            joined_ref[pl.program_id(0), rows, :] = pair

    if final:
        tiles, _, _ = joined_ref.shape

        @pl.when(pl.program_id(0) == tiles - 1)
        def _():
            joined = jnp.concatenate([joined_ref[i] for i in range(tiles)], axis=1)
            for j in range(w_ref.shape[0]):
                y = lax.dot_general(
                    w_ref[j],
                    joined,
                    (((1,), (1,)), ((), ())),
                    preferred_element_type=jnp.float32,
                )
                out = out_refs[j] if len(out_refs) > 1 else out_refs[0].at[j]
                half = w_ref.shape[1] // 2
                for parity in range(2):
                    for r in range(positions // LANES):
                        out[parity, r] = y[
                            parity * half : (parity + 1) * half, r * LANES : (r + 1) * LANES
                        ].astype(out.dtype)


def attention_call(q, pairs, state, w=None, own_apart=False):
    positions, features = q.shape
    tiles = features // LANES
    final = w is not None
    carry = pl.BlockSpec((1, 2, positions, LANES), lambda i: (i, 0, 0, 0))
    carry_shape = jax.ShapeDtypeStruct((tiles, 2, positions, LANES), jnp.float32)
    operands = [q]
    specs = [pl.BlockSpec((positions, LANES), lambda i: (0, i))]
    for pair in pairs:
        for array, place in pair:
            operands.append(array)
            specs.append(
                pl.BlockSpec((1, positions, LANES), functools.partial(lambda p, i: (p, 0, i), place))
            )
    if state is not None:
        operands += list(state)
        specs += [carry, carry]
    scratch = []
    if final:
        operands.append(w)
        specs.append(pl.BlockSpec(w.shape, lambda i: (0, 0, 0)))
        shape = (2, positions // LANES, w.shape[1] // 2, LANES)
        if own_apart:
            out_shape = (
                jax.ShapeDtypeStruct(shape, jnp.bfloat16),
                jax.ShapeDtypeStruct(shape, jnp.float32),
            )
        else:
            out_shape = (jax.ShapeDtypeStruct((w.shape[0],) + shape, jnp.bfloat16),)
        out_specs = tuple(
            pl.BlockSpec(o.shape, functools.partial(lambda n, i: (0,) * n, len(o.shape)))
            for o in out_shape
        )
        scratch = [pltpu.VMEM((tiles, positions, LANES), jnp.bfloat16)]
    else:
        out_shape = (carry_shape, carry_shape)
        out_specs = (carry, carry)
    keys = positions * len(pairs)
    return pl.pallas_call(
        functools.partial(attention_kernel, len(pairs), state is not None, final),
        grid=(tiles,),
        in_specs=specs,
        out_specs=out_specs,
        out_shape=out_shape,
        scratch_shapes=scratch,
        compiler_params=pltpu.CompilerParams(vmem_limit_bytes=VMEM_LIMIT),
        cost_estimate=cost(1000 + 3200 * len(pairs)),
        name="attend",
    )(*operands)


def per_device(
    latent,
    stale_kv,
    timestep,
    w_time,
    gn_gain,
    gn_bias,
    conv_w,
    conv_b,
    ln_gain,
    ln_bias,
    w_qkv,
    w_out,
):
    latent_rows = latent[0]
    rows_count = lax.axis_size("rows")
    tp_count = lax.axis_size("tp")
    span_rows, local_channels, grid_width = latent_rows.shape
    positions = span_rows * grid_width
    group_width = D // GROUPS
    local_groups = local_channels // group_width
    my_block = lax.axis_index("rows")
    cfg = lax.axis_index("cfg")
    tp = lax.axis_index("tp")

    latent32 = latent_rows.astype(jnp.float32)
    values32 = latent32.reshape(span_rows, local_groups, group_width, grid_width)
    sums = jnp.stack(
        [jnp.sum(values32, axis=(0, 2, 3)), jnp.sum(values32 * values32, axis=(0, 2, 3))]
    )
    table = jnp.zeros((2, 2, GROUPS), jnp.float32)
    table = lax.dynamic_update_slice(table, sums[None], (cfg, 0, tp * local_groups))
    table = summed(table.reshape(-1), ("cfg", "rows", "tp"))

    up_pairs = [(i, i + 1) for i in range(rows_count - 1)]
    down_pairs = [(i + 1, i) for i in range(rows_count - 1)]
    before = lax.ppermute(latent_rows[span_rows - 1 :], "rows", up_pairs)
    after = lax.ppermute(latent_rows[:1], "rows", down_pairs)
    rimmed = jnp.concatenate([before, latent_rows, after], axis=0)

    x_mine, x_other = halves_of_inputs(rimmed)

    forward, backward = ring_pairs(rows_count)
    last = rows_count // 2
    pair = stale_kv[0].reshape(2, positions, -1)
    hops = [(pair, pair)]

    def next_hop(*after):
        ahead, behind = hops[-1]
        if len(hops) == last:
            ahead, behind = ahead[:1], behind[1:]
        if after:
            ahead, behind, *_ = lax.optimization_barrier((ahead, behind) + after)
        hops.append(
            (lax.ppermute(ahead, "rows", forward), lax.ppermute(behind, "rows", backward))
        )

    def blocks_of(hop):
        ahead, behind = hops[hop]
        if hop == last:
            return [((ahead, 0), (behind, 0))]
        return [((ahead, 0), (ahead, 1)), ((behind, 0), (behind, 1))]

    next_hop()

    vectors = gather_tp(jnp.stack([gn_gain, gn_bias, ln_gain, ln_bias]), 1).astype(jnp.float32)
    amount = span_rows * rows_count * grid_width * group_width
    half = D // 2
    gn_affine = lax.dynamic_slice_in_dim(vectors[:2], cfg * half, half, 1).T
    ln_affine = vectors[2:].T
    flags = jnp.stack([my_block > 0, my_block < rows_count - 1, tp == cfg]).astype(jnp.int32)
    place = cfg * (GROUPS // 2)
    flags_mine = jnp.append(flags, cfg * 2 * GROUPS + place)
    flags_other = jnp.append(flags, (1 - cfg) * 2 * GROUPS + place)

    local_features = w_qkv.shape[2]
    w_project = w_qkv.transpose(1, 0, 2)
    flip = jnp.logical_and(tp_count == 2, tp == 0)
    w_back = arrange_call(flip, w_out, tp_count)
    order = jnp.stack([tp, 1 - tp]).astype(jnp.int32) if tp_count == 2 else jnp.zeros((1,), jnp.int32)
    gn_affine, ln_affine, order, w_back = lax.optimization_barrier(
        (gn_affine, ln_affine, order, w_back)
    )

    flags_other = need(flags_other, hops[1])
    conv_sent = conv_call(flags_other, table, amount, x_other, gn_affine, conv_w, jnp.bfloat16)
    conv_received = swapped(conv_sent, "cfg")
    next_hop()
    conv_own = conv_call(flags_mine, table, amount, x_mine, gn_affine, conv_w, jnp.float32)

    half_width = TEMB // 2
    frequencies = jnp.exp(
        -math.log(10000.0) * jnp.arange(half_width, dtype=jnp.float32) / half_width
    )
    angles = timestep.astype(jnp.float32)[0] * frequencies
    embedding = jnp.concatenate([jnp.cos(angles), jnp.sin(angles)])
    time_bias = jnp.dot(
        jax.nn.silu(embedding)[None, :], w_time.astype(jnp.float32), precision=lax.Precision.HIGHEST
    )[0]
    bias = conv_b.astype(jnp.float32) + time_bias
    resid = (
        latent32 + (conv_own + conv_received.astype(jnp.float32) + bias[None, :, None])
    ).astype(jnp.bfloat16)

    if tp_count == 2:
        parts = [resid, need(swapped(resid, "tp"), hops[2])]
    else:
        parts = [lax.all_gather(resid, "tp", axis=1, tiled=True)]
    next_hop(resid)
    queries, fresh = project_call(order, parts, ln_affine, w_project)
    resid_split = split_call(resid)
    fresh_kv = fresh.reshape(1, 2, span_rows, grid_width, local_features)

    group = [((fresh, 0), (fresh, 1))] + blocks_of(1)
    state = None
    for hop in range(2, last + 1):
        if hop == 3:
            group = group + blocks_of(3)
            continue
        state = attention_call(queries, group, state)
        while len(hops) <= last:
            next_hop(state[0])
        group = blocks_of(hop)
    if tp_count == 2:
        sent, kept_terms = attention_call(queries, group, state, w_back, True)
        terms = (kept_terms, swapped(sent, "tp"))
    else:
        (sent,) = attention_call(queries, group, state, w_back)
        terms = (lax.psum_scatter(sent, "tp", scatter_dimension=0),)

    other_branch = swapped(branch_call(1 - cfg, resid_split, terms), "cfg")
    kept = branch_call(cfg, resid_split, terms)
    is_cond = cfg == 0
    cond_out = jnp.where(is_cond, kept, other_branch).astype(jnp.float32)
    uncond_out = jnp.where(is_cond, other_branch, kept).astype(jnp.float32)
    guided = (uncond_out + guidance * (cond_out - uncond_out)).astype(jnp.bfloat16)
    return (guided[:, :, None, :], fresh_kv)


def solution(mesh):
    in_specs = (
        P("cfg", "rows", "tp", None),
        P("cfg", None, "rows", None, "tp"),
        P(),
        P(None, "tp"),
        P("tp"),
        P("tp"),
        P(None, None, "tp", "cfg"),
        P("tp"),
        P("tp"),
        P("tp"),
        P(None, None, "tp"),
        P("tp", None),
    )
    out_specs = (P("rows", "tp", "cfg", None), P("cfg", None, "rows", None, "tp"))
    return jax.shard_map(
        per_device, mesh=mesh, in_specs=in_specs, out_specs=out_specs, check_vma=False
    )
```
